32 devices in a mesh: dp: 16 (over z, y, x), seq: 2 (over core).
Axes of the slice: x: 2, y: 2, z: 4, core: 2. Of those that a mesh axis runs over, the one named last changes fastest.
Arguments:
- phonemes: bfloat16 [2, 32, 128, 512], P(None, None, 'dp'), may hold values from -60 to 60, as said below
- style_vector: bfloat16 [2, 32, 128], P(None, 'dp'), may hold values from -6 to 6
- frame_phone: int32 [2, 32, 1024], P(None, 'dp', 'seq'), may hold values from 0 to 127, as said below
- frame_count: int32 [2, 32], P(None, 'dp'), may hold values from 640 to 1024, as said below
- cotangent: bfloat16 [2, 32, 1024, 512], P(None, 'dp', 'seq'), may hold values from -6 to 6
- conv_master: float32 [3145728], P('dp'), may hold values from -0.15625 to 0.15625
- conv_moment: float32 [3145728], P('dp'), may hold values from -48 to 48
- conv_square: float32 [3145728], P('dp'), may hold values from 5.89824 to 23.59296
- bias_master: float32 [1024], P('dp'), may hold values from -2 to 2
- bias_moment: float32 [1024], P('dp'), may hold values from -80 to 80
- bias_square: float32 [1024], P('dp'), may hold values from 16.384 to 65.536
- style_master: float32 [524288], P('dp'), may hold values from -0.25 to 0.25
- style_moment: float32 [524288], P('dp'), may hold values from -80 to 80
- style_square: float32 [524288], P('dp'), may hold values from 16.384 to 65.536
- offset_master: float32 [4096], P('dp'), may hold values from -2 to 2
- offset_moment: float32 [4096], P('dp'), may hold values from -80 to 80
- offset_square: float32 [4096], P('dp'), may hold values from 16.384 to 65.536
Outputs:
- frames_out: float32 [2, 32, 1024, 512], P(None, 'dp', 'seq')
- phoneme_grad: float32 [2, 32, 128, 512], P(None, None, 'dp', 'seq')
- style_grad: float32 [2, 32, 128], P(None, 'dp')
- updated_conv: float32 [3145728], P('dp')
- moment_conv: float32 [3145728], P('dp')
- square_conv: float32 [3145728], P('dp')
- bfloat_conv: bfloat16 [3145728], P('dp')
- updated_bias: float32 [1024], P('dp')
- moment_bias: float32 [1024], P('dp')
- square_bias: float32 [1024], P('dp')
- bfloat_bias: bfloat16 [1024], P('dp')
- updated_style: float32 [524288], P('dp')
- moment_style: float32 [524288], P('dp')
- square_style: float32 [524288], P('dp')
- bfloat_style: bfloat16 [524288], P('dp')
- updated_offset: float32 [4096], P('dp')
- moment_offset: float32 [4096], P('dp')
- square_offset: float32 [4096], P('dp')
- bfloat_offset: bfloat16 [4096], P('dp')
The draws below stay inside these ranges and needn't reach their ends.
Inputs may be any that keep to these rules, and one draw needn't show every extreme that they name: `phonemes`: phoneme features of order one, with varying scales. Frames from frame_count to 1023 of an item are padding. `frame_phone`: never falls along an item's frames.
All inputs are finite; a program needn't handle non-finite values.
Results may differ from the reference program's by a relative error of at most 0.014.
Values may be sent and summed in bfloat16 or wider, within the bound.
A program may use at most 192 MiB of HBM per device.

```python
import math
import jax
import jax.numpy as jnp
from jax import lax

D = 512
S = 128
KERN = 3
LAYERS = 2
PH = 128
FRAME_SLOT_LIMIT = 1024
MICRO = 2
STEP = 10
ITEMS_MB = 32


def draw_phonemes(key, part):
    base_key, row_key, column_key = jax.random.split(jax.random.fold_in(key, 11), 3)
    shape = (MICRO, ITEMS_MB, PH, D)
    base = jnp.clip(jax.random.normal(base_key, shape, jnp.float32), -6.0, 6.0)
    rows = jnp.exp(jax.random.uniform(row_key, (MICRO, ITEMS_MB, PH, 1), jnp.float32, math.log(0.32), math.log(3.2)))
    columns = jnp.exp(jax.random.uniform(column_key, (D,), jnp.float32, math.log(0.32), math.log(3.2)))
    return (base * rows * columns).astype(jnp.bfloat16)


def draw_frame_count(key, part):
    counts = jax.random.randint(jax.random.fold_in(key, 23), (MICRO, ITEMS_MB), FRAME_SLOT_LIMIT * 5 // 8, FRAME_SLOT_LIMIT + 1)
    counts = counts.at[0, 0].set(FRAME_SLOT_LIMIT)
    counts = counts.at[0, 1].set(FRAME_SLOT_LIMIT * 5 // 8)
    return counts.astype(jnp.int32)


def draw_frame_phone(key, part):
    lengths = jax.random.randint(jax.random.fold_in(key, 37), (MICRO, ITEMS_MB, PH), 1, 2 * FRAME_SLOT_LIMIT // PH)
    bounds = jnp.cumsum(lengths, axis=-1).astype(jnp.int32)
    frames = jnp.arange(FRAME_SLOT_LIMIT, dtype=jnp.int32)

    def locate(limits):
        return jnp.searchsorted(limits, frames, side='right').astype(jnp.int32)
    index = jax.vmap(jax.vmap(locate))(bounds)
    index = jnp.minimum(index, PH - 1)
    index = index.at[:, :, FRAME_SLOT_LIMIT - 1].set(PH - 1)
    return index.astype(jnp.int32)


def block_levels(stream_key, dims, cuts, low, largest):
    factor_of = 1.0
    for dim, shards_of in cuts:
        draws = jax.random.uniform(jax.random.fold_in(jax.random.fold_in(stream_key, 6), dim), (shards_of,), jnp.float32, low / len(cuts), largest / len(cuts))
        factor_of = factor_of * jnp.repeat(jnp.exp(draws), dims[dim] // shards_of).reshape((-1,) + (1,) * (len(dims) - 1 - dim))
    return factor_of


def gaussian(key, dims, deviation, reach, cuts=(), kind=jnp.bfloat16):
    array = jax.random.normal(key, dims, jnp.float32) * deviation
    if len(cuts) > 0:
        array = block_levels(key, dims, cuts, -0.22, 0.18) * array
    return jnp.clip(array, min=-reach, max=reach).astype(kind)


def setup_inputs(seed: int = 0) -> dict:
    key_list = jax.random.split(jax.random.key(seed), 18)
    phonemes = draw_phonemes(jax.random.fold_in(key_list[17], 71), 0)
    style_vector = gaussian(key_list[1], (MICRO, ITEMS_MB, S), 1.0, 6.0, ((1, 16),))
    frame_phone = draw_frame_phone(jax.random.fold_in(key_list[17], 71), 0)
    frame_count = draw_frame_count(jax.random.fold_in(key_list[17], 71), 0)
    cotangent = gaussian(key_list[4], (MICRO, ITEMS_MB, FRAME_SLOT_LIMIT, D), 1.0, 6.0, ((1, 16), (2, 2)))
    conv_master = gaussian(key_list[5], (2 * LAYERS * KERN * D * D,), (KERN * D) ** -0.5, 0.15625, ((0, 16),), jnp.float32)
    conv_moment = gaussian(key_list[6], (2 * LAYERS * KERN * D * D,), (0.111 * 0.3 * (MICRO * ITEMS_MB * FRAME_SLOT_LIMIT) ** 0.5), 48.0, ((0, 16),), jnp.float32)
    conv_square = jnp.clip(jnp.exp(math.log(23.59296) - 1.3862944 * jax.random.uniform(key_list[7], (2 * LAYERS * KERN * D * D,), jnp.float32) ** block_levels(key_list[7], (2 * LAYERS * KERN * D * D,), ((0, 16),), -0.2, 0.2)), 5.89824, 23.59296)
    bias_master = gaussian(key_list[8], (LAYERS * D,), 0.15, 2.0, ((0, 16),), jnp.float32)
    bias_moment = gaussian(key_list[9], (LAYERS * D,), (0.111 * 0.5 * (MICRO * ITEMS_MB * FRAME_SLOT_LIMIT) ** 0.5), 80.0, ((0, 16),), jnp.float32)
    bias_square = jnp.clip(jnp.exp(math.log(65.536) - 1.3862944 * jax.random.uniform(key_list[10], (LAYERS * D,), jnp.float32) ** block_levels(key_list[10], (LAYERS * D,), ((0, 16),), -0.2, 0.2)), 16.384, 65.536)
    style_master = gaussian(key_list[11], (4 * LAYERS * S * D,), (4 * S) ** -0.5, 0.25, ((0, 16),), jnp.float32)
    style_moment = gaussian(key_list[12], (4 * LAYERS * S * D,), (0.111 * 0.5 * (MICRO * ITEMS_MB * FRAME_SLOT_LIMIT) ** 0.5), 80.0, ((0, 16),), jnp.float32)
    style_square = jnp.clip(jnp.exp(math.log(65.536) - 1.3862944 * jax.random.uniform(key_list[13], (4 * LAYERS * S * D,), jnp.float32) ** block_levels(key_list[13], (4 * LAYERS * S * D,), ((0, 16),), -0.2, 0.2)), 16.384, 65.536)
    offset_master = gaussian(key_list[14], (4 * LAYERS * D,), 0.15, 2.0, ((0, 16),), jnp.float32)
    offset_moment = gaussian(key_list[15], (4 * LAYERS * D,), (0.111 * 0.5 * (MICRO * ITEMS_MB * FRAME_SLOT_LIMIT) ** 0.5), 80.0, ((0, 16),), jnp.float32)
    offset_square = jnp.clip(jnp.exp(math.log(65.536) - 1.3862944 * jax.random.uniform(key_list[16], (4 * LAYERS * D,), jnp.float32) ** block_levels(key_list[16], (4 * LAYERS * D,), ((0, 16),), -0.2, 0.2)), 16.384, 65.536)
    return {"phonemes": phonemes, "style_vector": style_vector, "frame_phone": frame_phone, "frame_count": frame_count, "cotangent": cotangent, "conv_master": conv_master, "conv_moment": conv_moment, "conv_square": conv_square, "bias_master": bias_master, "bias_moment": bias_moment, "bias_square": bias_square, "style_master": style_master, "style_moment": style_moment, "style_square": style_square, "offset_master": offset_master, "offset_moment": offset_moment, "offset_square": offset_square}


NORM_EPS = 1e-05
HALF_ROOT = 0.7071067811865476
MOMENT_DECAY = 0.9
SQUARE_DECAY = 0.999
LEARN_RATE = 0.05
WEIGHT_DECAY = 0.01
ADAM_EPS = 1e-08

@jax.custom_vjp
def low(v):
    return lax.optimization_barrier(v.astype(jnp.bfloat16)).astype(jnp.float32)

@jax.custom_vjp
def low_back(v):
    return v

def low_keep(v):
    return (low(v), None)

def low_pass(kept, grad):
    return (grad,)

def back_keep(v):
    return (v, None)

def back_low(kept, grad):
    return (low(grad),)
low.defvjp(low_keep, low_pass)
low_back.defvjp(back_keep, back_low)

def adain(values, valid, counted, style_rows, weight, offset_amount):
    mean_value = lax.optimization_barrier(jnp.sum(valid * values, axis=1, keepdims=True)) / counted
    centered = values - mean_value
    variance = lax.optimization_barrier(jnp.sum(valid * centered * centered, axis=1, keepdims=True)) / counted
    normed = centered * lax.rsqrt(variance + NORM_EPS)
    params = jnp.dot(style_rows, weight, precision=lax.Precision.HIGHEST) + offset_amount
    return (1.0 + params[:, None, :D]) * normed + params[:, None, D:]

def convolve(values, weight_tensors):
    padded_frames = jnp.pad(values, ((0, 0), (1, 1), (0, 0)))
    block_result = jnp.einsum('wpl,lo->wpo', padded_frames[:, 0:FRAME_SLOT_LIMIT], weight_tensors[0], precision=lax.Precision.HIGHEST)
    for kernel_tap_index in range(1, KERN):
        block_result = block_result + jnp.einsum('wpl,lo->wpo', padded_frames[:, kernel_tap_index:kernel_tap_index + FRAME_SLOT_LIMIT], weight_tensors[kernel_tap_index], precision=lax.Precision.HIGHEST)
    return block_result

def pick_rows(table_rows, slot_index):
    return table_rows[slot_index]

def forward(phon, style_rows, conv_flat, bias_flat, style_flat, offset_flat, phone, counts):
    conv_all = low(conv_flat).reshape(2 * LAYERS, KERN, D, D)
    bias_all = low(bias_flat).reshape(LAYERS, D)
    style_all = low(style_flat).reshape(2 * LAYERS, S, 2 * D)
    offset_all = low(offset_flat).reshape(2 * LAYERS, 2 * D)
    frame_positions = jnp.arange(FRAME_SLOT_LIMIT, dtype=jnp.int32)
    valid = (frame_positions[None, :] < counts[:, None]).astype(jnp.float32)[:, :, None]
    counted = lax.optimization_barrier(jnp.sum(valid, axis=1, keepdims=True))
    upsampled = jax.vmap(pick_rows)(phon, phone)
    hidden = low_back(upsampled * valid)
    for layer in range(LAYERS):
        first = low(valid * jax.nn.silu(adain(hidden, valid, counted, style_rows, style_all[2 * layer], offset_all[2 * layer])))
        middle = low_back(convolve(first, conv_all[2 * layer]))
        second = low(valid * jax.nn.silu(adain(middle, valid, counted, style_rows, style_all[2 * layer + 1], offset_all[2 * layer + 1])))
        branch = low_back(convolve(second, conv_all[2 * layer + 1]) + bias_all[layer])
        hidden = valid * (hidden + branch) * HALF_ROOT
    return hidden

def adamw_update(master, moment, square, gradient, step_value):
    new_moment = MOMENT_DECAY * moment + (1.0 - MOMENT_DECAY) * gradient
    new_square = SQUARE_DECAY * square + (1.0 - SQUARE_DECAY) * gradient * gradient
    first_fix = 1.0 - jnp.power(jnp.float32(MOMENT_DECAY), step_value)
    second_fix = 1.0 - jnp.power(jnp.float32(SQUARE_DECAY), step_value)
    updated = master - LEARN_RATE * (new_moment / first_fix / (jnp.sqrt(new_square / second_fix) + ADAM_EPS) + WEIGHT_DECAY * master)
    return (updated, new_moment, new_square, updated.astype(jnp.bfloat16))

def reference(phonemes, style_vector, frame_phone, frame_count, cotangent, conv_master, conv_moment, conv_square, bias_master, bias_moment, bias_square, style_master, style_moment, style_square, offset_master, offset_moment, offset_square):
    total_rows = MICRO * ITEMS_MB
    group = 4 if total_rows % 4 == 0 else 1
    blocks = total_rows // group
    phon = phonemes.reshape(blocks, group, PH, D)
    styles = style_vector.reshape(blocks, group, S)
    phones = frame_phone.reshape(blocks, group, FRAME_SLOT_LIMIT)
    counts = frame_count.reshape(blocks, group)
    cotans = cotangent.reshape(blocks, group, FRAME_SLOT_LIMIT, D)
    masters = (conv_master, bias_master, style_master, offset_master)

    def visit(summed, inputs):
        part_phon, part_style, part_phone, part_count, part_cot = inputs

        def run_block(phon32, style32, conv_flat, bias_flat, style_flat, offset_flat):
            return forward(phon32, style32, conv_flat, bias_flat, style_flat, offset_flat, part_phone, part_count)
        frames, pull = jax.vjp(run_block, part_phon.astype(jnp.float32), part_style.astype(jnp.float32), conv_master, bias_master, style_master, offset_master)
        gradients = pull(part_cot.astype(jnp.float32))
        summed = tuple((earlier + latest for earlier, latest in zip(summed, gradients[2:])))
        return (summed, (frames, gradients[0], gradients[1]))
    zeros = tuple((jnp.zeros_like(master) for master in masters))
    summed, (frames, phon_grad, style_grad) = lax.scan(visit, zeros, (phon, styles, phones, counts, cotans))
    step_value = jnp.float32(STEP)
    conv_out = adamw_update(conv_master, conv_moment, conv_square, summed[0], step_value)
    bias_out = adamw_update(bias_master, bias_moment, bias_square, summed[1], step_value)
    style_out = adamw_update(style_master, style_moment, style_square, summed[2], step_value)
    offset_out = adamw_update(offset_master, offset_moment, offset_square, summed[3], step_value)
    return (frames.reshape(MICRO, ITEMS_MB, FRAME_SLOT_LIMIT, D), phon_grad.reshape(MICRO, ITEMS_MB, PH, D), style_grad.reshape(MICRO, ITEMS_MB, S), conv_out[0], conv_out[1], conv_out[2], conv_out[3], bias_out[0], bias_out[1], bias_out[2], bias_out[3], style_out[0], style_out[1], style_out[2], style_out[3], offset_out[0], offset_out[1], offset_out[2], offset_out[3])
```

```python
import functools

import jax
import jax.numpy as jnp
from jax import lax
from jax.experimental import pallas as pl
from jax.experimental.pallas import tpu as pltpu
from jax.sharding import PartitionSpec as P

D = 512
S = 128
KERN = 3
LAYERS = 2
CONVS = 2 * LAYERS
PH = 128
STEP = 10
FRAMES = 1024
SEG = 16
RUN = FRAMES // SEG
HALF = D // 2
ITEMS = 2
PADDED = FRAMES + 2 * SEG
TABLE_ROWS = ITEMS * PH

NORM_EPS = 1e-05
HALF_ROOT = 0.7071067811865476
MOMENT_DECAY = 0.9
SQUARE_DECAY = 0.999
LEARN_RATE = 0.05
WEIGHT_DECAY = 0.01
ADAM_EPS = 1e-08

BF = jnp.bfloat16
F32 = jnp.float32
MESH = pl.DeviceIdType.MESH
HIGH = lax.Precision.HIGHEST

C_SCALE, C_SHIFT, C_INV, C_MI, C_ONE, C_2, C_3 = range(7)


def factor(ndp):
    return {16: (4, 2, 2), 128: (4, 8, 4)}.get(ndp, (4, ndp // 4, 1))


def dot(a, b):
    return jnp.dot(a, b, preferred_element_type=F32)


def dot_nt(a, b, precision=None):
    return lax.dot_general(a, b, (((1,), (1,)), ((), ())), preferred_element_type=F32, precision=precision)


def dot_tn(a, b, precision=None):
    return lax.dot_general(a, b, (((0,), (0,)), ((), ())), preferred_element_type=F32, precision=precision)


def fold(tile):
    rows, cols = tile.shape
    return jnp.sum(tile.reshape(rows // 8, 8, cols), axis=0)


def valid_rows(start, rows, count, value):
    i = lax.broadcasted_iota(jnp.int32, (rows, 128), 0)
    frame = (i & (SEG - 1)) * RUN + (i >> 4) + start // SEG
    return jnp.where(frame < count, jnp.float32(value), jnp.float32(0.0))


def train_kernel(cfg, *refs):
    ndp, (n0, n1, n2), slots = cfg["ndp"], cfg["dims"], cfg["slots"]
    shard, srows, remote_phon = cfg["shard"], cfg["srows"], cfg["remote_phon"]
    comm = cfg.get("comm", True)
    skip = cfg.get("skip", ())
    nq = ndp // CONVS
    nb = ndp // 8
    nz = cfg["chunks"]
    (
        phon, sv, fphone, cnt, cot, wmas, smas, brow, orow,
        o_frames, o_phone, o_small, o_gconv, o_gstyle,
        W, PAD, AT, ST, G, GY, COT, PM, OHP, TABLE, FPH, WM, SM, AE,
        SVR, PARS, PARR, COEF, STAT, BIAS, BGRAD, GSTS, GSTR, SX,
        DW, SIBR, RB, RA, ZR, GF, PGX,
        loc, ss, rs, s_z, r_z, s_f, r_f, s_s, r_s, s_b, r_b,
        rss, rsr, rbs, rbr, ras, rar, zs, zr,
    ) = refs
    SGS, SGR = PARS, PARR
    me = lax.axis_index("dp")
    c = lax.axis_index("seq")
    c0, c1, c2 = me // (n1 * n2), (me // n2) % n1, me % n2
    sib = (me, 1 - c)

    def remote(src, dst, send, recv, target):
        return pltpu.make_async_remote_copy(
            src_ref=src, dst_ref=dst, send_sem=send, recv_sem=recv, device_id=target, device_id_type=MESH
        )

    def wait_bytes(ref, sem):
        pltpu.make_async_copy(ref, ref, sem).wait()

    def sent(copy):
        copy.wait_send()

    def peers(fn):
        def one(d, carry):
            fn(lax.rem(me + d, ndp))
            return carry
        lax.fori_loop(1, ndp, one, 0)

    barrier = pltpu.get_barrier_semaphore()
    peers(lambda d: pl.semaphore_signal(barrier, inc=1, device_id=(d, c), device_id_type=MESH))
    pl.semaphore_signal(barrier, inc=1, device_id=sib, device_id_type=MESH)

    own_in = [
        pltpu.make_async_copy(wmas, WM, loc.at[0]),
        pltpu.make_async_copy(smas, SM, loc.at[1]),
        pltpu.make_async_copy(cot.at[c], COT.at[:, pl.ds(pl.multiple_of(c * HALF * 2, 512), 512)], loc.at[2]),
        pltpu.make_async_copy(fphone.at[c], FPH.at[:, pl.ds(pl.multiple_of(c * HALF * 2, 512), 512)], loc.at[3]),
    ]
    if remote_phon:
        own_in.append(
            pltpu.make_async_copy(
                phon.at[c, pl.ds(pl.multiple_of(me * 16, 16), 16)],
                TABLE.at[pl.ds(pl.multiple_of(me * 16, 16), 16)], loc.at[4],
            )
        )
    else:
        own_in.append(pltpu.make_async_copy(phon, TABLE, loc.at[4]))
    for copy in own_in:
        copy.start()

    own_in[0].wait()
    for cb in range(4):
        W[cb // 2, c0, c1, c2, :, (cb % 2) * 128:(cb % 2) * 128 + 128] = WM[
            pl.ds(cb, shard, stride=4), :
        ].astype(BF)
    own_in[1].wait()
    quarter = lax.rem(me, S // srows)
    for cb in range(8):
        block = SM[pl.ds(cb, srows, stride=8), :].astype(BF).astype(F32)
        for qq in range(S // srows):
            AE[qq * srows:(qq + 1) * srows, cb * 128:cb * 128 + 128] = jnp.where(quarter == qq, block, 0.0)
    vec = sv[c].astype(F32)
    vec = jnp.concatenate([jnp.broadcast_to(vec[i:i + 1], (4, S)) for i in range(ITEMS)], axis=0)
    SVR[me] = vec

    pl.semaphore_wait(barrier, ndp)

    def send_sv(d):
        return remote(SVR.at[me], SVR.at[me], ss.at[0], rs.at[0], (d, c))

    def send_phon(d):
        return remote(
            phon.at[c, pl.ds(pl.multiple_of(d * 16, 16), 16)],
            TABLE.at[pl.ds(pl.multiple_of(me * 16, 16), 16)], ss.at[1], rs.at[1], (d, c),
        )

    send_fph = remote(
        fphone.at[1 - c], FPH.at[:, pl.ds(pl.multiple_of(c * 512, 512), 512)], ss.at[2], rs.at[2], sib
    )
    send_cot = remote(
        cot.at[1 - c], COT.at[:, pl.ds(pl.multiple_of(c * 512, 512), 512)], ss.at[3], rs.at[3], sib
    )
    peers(lambda d: send_sv(d).start())
    if remote_phon:
        peers(lambda d: send_phon(d).start())
    send_fph.start()
    send_cot.start()

    rows = shard // nz

    def order(t):
        if t == 0:
            return c0
        return jnp.where(t - 1 < c0, t - 1, t)

    def z_hop(zz, q, up):
        to = c0 + (1 if up else -1)
        target = ((to * n1 + c1) * n2 + c2, c)
        piece = W.at[c, zz, c1, c2, pl.ds(q * rows, rows)]
        return remote(piece, piece, s_z.at[zz, q, 0 if up else 1], r_z.at[zz, q], target)

    def z_sends(zz, q, fn):
        @pl.when(jnp.logical_and(zz <= c0, c0 < n0 - 1))
        def _():
            fn(z_hop(zz, q, True))

        @pl.when(jnp.logical_and(zz >= c0, c0 > 0))
        def _():
            fn(z_hop(zz, q, False))

    def own_z(up, fn):
        for q in range(nz):
            @pl.when(c0 < n0 - 1 if up else c0 > 0)
            def _():
                fn(z_hop(c0, q, up))

    def first_sends(zz, fn):
        piece = W.at[c, zz, c1, c2]

        @pl.when(c == 0)
        def _():
            for k in range(1, n2):
                to = lax.rem(c2 + k, n2)
                fn(remote(piece, piece, s_f.at[zz, k], r_f.at[zz, k], ((c0 * n1 + c1) * n2 + to, c)))

        @pl.when(c == 1)
        def _():
            for k in range(1, n1):
                to = lax.rem(c1 + k, n1)
                fn(remote(piece, piece, s_f.at[zz, k], r_f.at[zz, k], ((c0 * n1 + to) * n2 + c2, c)))

    def second_sends(zz, fn):
        @pl.when(c == 0)
        def _():
            line = W.at[0, zz, c1]
            for k in range(1, n1):
                to = lax.rem(c1 + k, n1)
                fn(remote(line, line, s_s.at[zz, k], r_s.at[zz, k], ((c0 * n1 + to) * n2 + c2, c)))

        @pl.when(c == 1)
        def _():
            line = W.at[1, zz, :, c2]
            for k in range(1, n2):
                to = lax.rem(c2 + k, n2)
                fn(remote(line, line, s_s.at[zz, k], r_s.at[zz, k], ((c0 * n1 + c1) * n2 + to, c)))

    def first_wait(zz):
        @pl.when(c == 0)
        def _():
            for k in range(1, n2):
                wait_bytes(W.at[c, zz, c1, c2], r_f.at[zz, k])

        @pl.when(c == 1)
        def _():
            for k in range(1, n1):
                wait_bytes(W.at[c, zz, c1, c2], r_f.at[zz, k])

    def second_wait(zz):
        @pl.when(c == 0)
        def _():
            for k in range(1, n1):
                wait_bytes(W.at[0, zz, c1], r_s.at[zz, k])

        @pl.when(c == 1)
        def _():
            for k in range(1, n2):
                wait_bytes(W.at[1, zz, :, c2], r_s.at[zz, k])

    def sib_send(zz):
        return remote(W.at[c, zz], W.at[c, zz], s_b.at[zz], r_b.at[zz], sib)

    def ev0(t):
        zz = order(t)
        if t > 0:
            for q in range(nz):
                wait_bytes(W.at[c, zz, c1, c2, pl.ds(q * rows, rows)], r_z.at[zz, q])
                z_sends(zz, q, lambda copy: copy.start())

            @pl.when(zz == c0 - 1)
            def _():
                own_z(True, lambda copy: copy.start())
        first_sends(zz, lambda copy: copy.start())

    def ev1(t):
        zz = order(t)
        first_wait(zz)
        second_sends(zz, lambda copy: copy.start())

    def ev2(t):
        zz = order(t)
        second_wait(zz)
        sib_send(zz).start()

    def ev3(t):
        zz = order(t)
        wait_bytes(W.at[c, zz], r_b.at[zz])

    own_z(False, lambda copy: copy.start())

    @pl.when(c0 == 0)
    def _():
        own_z(True, lambda copy: copy.start())
    ev0(0)

    def make_perm(t, carry):
        r0 = pl.multiple_of(t * 128, 128)
        row = lax.broadcasted_iota(jnp.int32, (128, FRAMES), 0)
        col = lax.broadcasted_iota(jnp.int32, (128, FRAMES), 1)
        frame = (row & (SEG - 1)) * RUN + (row >> 4) + r0 // SEG
        PM[pl.ds(r0, 128), :] = jnp.where(col == frame, 1.0, 0.0).astype(BF)
        return carry

    lax.fori_loop(0, FRAMES // 128, make_perm, 0)

    row_kind = lax.broadcasted_iota(jnp.int32, (ndp * 8, 1), 0) & 3
    wait_bytes(SVR.at[pl.ds(0, ndp - 1)], rs.at[0])
    svall = SVR[...].reshape(ndp * 8, S)
    acc = jnp.zeros((ndp * 8, 256), F32)
    for b in range(4):
        acc = acc + dot(
            jnp.where(row_kind == b, svall, 0.0).astype(BF), AE[:, b * 256:b * 256 + 256].astype(BF)
        )
    offset_kind = lax.rem(me, nq) * 4 // nq
    acc = acc + jnp.where(row_kind == offset_kind, orow[0:1, :].astype(BF).astype(F32), 0.0)
    PARS[:, :, 0:256] = acc.reshape(ndp, 8, 256)
    PARS[:, :, 256:384] = jnp.broadcast_to(brow[0:1, :].astype(BF).astype(F32).reshape(1, 1, 128), (ndp, 8, 128))

    def send_par(d):
        return remote(PARS.at[d], PARR.at[me], ss.at[4], rs.at[4], (d, c))

    peers(lambda d: send_par(d).start())
    PARR[me] = PARS[me]

    own_in[3].wait()
    wait_bytes(FPH.at[:, pl.ds(0, 512)], rs.at[2])
    for i in range(ITEMS):
        phone = FPH[i:i + 1, :]
        if slots & (slots - 1) == 0:
            shift = slots.bit_length() - 1
            place = ((phone >> shift) << (shift + 1)) + i * slots + (phone & (slots - 1))
        else:
            place = (phone // slots) * (2 * slots) + i * slots + phone % slots
        slot = lax.broadcasted_iota(jnp.int32, (TABLE_ROWS, FRAMES), 0)
        onehot = jnp.where(slot == place, 1.0, 0.0).astype(BF)
        for t in range(4):
            OHP[i, :, t * 256:t * 256 + 256] = dot_nt(onehot, PM[t * 256:t * 256 + 256, :]).astype(BF)

    STAT[...] = jnp.zeros(STAT.shape, F32)
    own_in[4].wait()
    if remote_phon:
        wait_bytes(TABLE.at[pl.ds(0, 16 * (ndp - 1))], rs.at[1])
    for i in range(ITEMS):
        count = cnt[c, i]
        for t in range(4):
            x = dot(OHP[i, :, t * 256:t * 256 + 256].T, TABLE[...])
            mask = valid_rows(t * 256, 256, count, 1.0)
            x = x * jnp.concatenate([mask] * 4, axis=1)
            ST[0, i, t * 256:t * 256 + 256, :] = x.astype(BF)
            STAT[i, 0] += fold(x)
            STAT[i, 1] += fold(x * x)

    ev1(0)
    own_in[2].wait()
    wait_bytes(COT.at[:, pl.ds(0, 512)], rs.at[3])
    for i in range(ITEMS):
        count = cnt[c, i]

        def permute(t, carry):
            r0 = pl.multiple_of(t * 256, 256)
            y = dot(PM[pl.ds(r0, 256), :], COT[i])
            mask = valid_rows(r0, 256, count, 1.0)
            G[i, pl.ds(r0, 256), :] = (y * jnp.concatenate([mask] * 4, axis=1)).astype(BF)
            return carry

        lax.fori_loop(0, 4, permute, 0)

    wait_bytes(PARR.at[pl.ds(0, ndp - 1)], rs.at[4])
    for j in range(CONVS):
        total = jnp.sum(PARR[j * nq:(j + 1) * nq, :, 0:256], axis=0)
        for i in range(ITEMS):
            for b in range(4):
                COEF[j, i, 8 + b // 2:9 + b // 2, (b % 2) * 256:(b % 2) * 256 + 256] = total[
                    4 * i + b:4 * i + b + 1, :
                ]
    for l in range(LAYERS):
        for qb in range(4):
            first = l * (ndp // 2) + qb * nb
            BIAS[l, :, qb * 128:qb * 128 + 128] = jnp.sum(PARR[first:first + nb, :, 256:384], axis=0)

    def stats_to_coef(j):
        for i in range(ITEMS):
            n = cnt[c, i].astype(F32)
            sums = jnp.sum(STAT[i, 0], axis=0, keepdims=True)
            squares = jnp.sum(STAT[i, 1], axis=0, keepdims=True)
            mean = sums / n
            var = jnp.maximum(squares / n - mean * mean, 0.0)
            inv = lax.rsqrt(var + NORM_EPS)
            one = (1.0 + COEF[j, i, 8:9]) * inv
            shift = COEF[j, i, 9:10] - mean * one

            def put(k, v):
                COEF[j, i, k:k + 1] = v
            put(C_SCALE, 0.5 * one)
            put(C_SHIFT, 0.5 * shift)
            put(C_INV, inv)
            put(C_MI, mean * inv)
            put(C_ONE, one)

    def coef(j, i, k, cols):
        return COEF[j, i, k:k + 1, cols]

    def edges():
        row = lax.broadcasted_iota(jnp.int32, (SEG, D), 0)
        for i in range(ITEMS):
            last = PAD[i, FRAMES:FRAMES + SEG, :].astype(F32)
            head = jnp.where(row == 0, 0.0, pltpu.roll(last, 1, 0))
            PAD[i, 0:SEG, :] = head.astype(BF)
            first = PAD[i, SEG:2 * SEG, :].astype(F32)
            tail = jnp.where(row == SEG - 1, 0.0, pltpu.roll(first, SEG - 1, 0))
            PAD[i, FRAMES + SEG:PADDED, :] = tail.astype(BF)

    TR = 128

    def adain_forward(j):
        stats_to_coef(j)
        for i in range(ITEMS):
            count = cnt[c, i]

            def tile(t, carry):
                r0 = pl.multiple_of(t * TR, TR)
                mask = valid_rows(r0, TR, count, 1.0)
                for cb in range(4):
                    cols = slice(cb * 128, cb * 128 + 128)
                    x = ST[j, i, pl.ds(r0, TR), cols].astype(F32)
                    v = x * coef(j, i, C_SCALE, cols) + coef(j, i, C_SHIFT, cols)
                    a = ((v + v * jnp.tanh(v)) * mask).astype(BF)
                    PAD[i, pl.ds(r0 + SEG, TR), cols] = a
                    AT[j, cols, pl.ds(i * FRAMES + r0, TR)] = a.T
                return carry

            lax.fori_loop(0, FRAMES // TR, tile, 0)
        edges()

    M = 512

    def taps(j):
        return [W[h, j].reshape(KERN * D, HALF) for h in range(2)]

    def conv_forward(j, epilogue):
        def tile(t, carry):
            i = t // (FRAMES // M)
            r0 = pl.multiple_of(lax.rem(t, FRAMES // M) * M, M)
            for h in range(2):
                acc = None
                weights = W[h, j].reshape(KERN * D, HALF)
                for k in range(KERN):
                    part = dot(PAD[i, pl.ds(r0 + SEG * k, M), :], weights[k * D:(k + 1) * D])
                    acc = part if acc is None else acc + part
                epilogue(i, r0, h, acc)
            return carry
        lax.fori_loop(0, ITEMS * FRAMES // M, tile, 0)

    def middle_out(j):
        def epilogue(i, r0, h, acc):
            count = cnt[c, i]
            for rb in range(0, M, 128):
                mask = valid_rows(r0 + rb, 128, count, 1.0)
                for cb in range(2):
                    cols = slice(h * HALF + cb * 128, h * HALF + cb * 128 + 128)
                    p = acc[rb:rb + 128, cb * 128:cb * 128 + 128]
                    ST[j + 1, i, pl.ds(r0 + rb, 128), cols] = p.astype(BF)
                    kept = p * mask
                    STAT[i, 0, :, cols] += fold(kept)
                    STAT[i, 1, :, cols] += fold(kept * p)
        return epilogue

    def block_out(l):
        def epilogue(i, r0, h, acc):
            count = cnt[c, i]
            for rb in range(0, M, 128):
                mask = valid_rows(r0 + rb, 128, count, HALF_ROOT)
                for cb in range(2):
                    cols = slice(h * HALF + cb * 128, h * HALF + cb * 128 + 128)
                    q = acc[rb:rb + 128, cb * 128:cb * 128 + 128] + BIAS[l, 0:1, cols]
                    x = (ST[2 * l, i, pl.ds(r0 + rb, 128), cols].astype(F32) + q) * mask
                    if l < LAYERS - 1:
                        ST[2 * l + 2, i, pl.ds(r0 + rb, 128), cols] = x.astype(BF)
                        STAT[i, 0, :, cols] += fold(x)
                        STAT[i, 1, :, cols] += fold(x * x)
                    else:
                        COT[i, pl.ds(r0 + rb, 128), cols] = x.astype(BF)
        return epilogue

    adain_forward(0)
    STAT[...] = jnp.zeros(STAT.shape, F32)
    ev0(1)
    ev2(0)
    ev1(1)
    ev0(2)
    ev2(1)
    ev1(2)
    ev3(0)
    ev3(1)
    conv_forward(0, middle_out(0))
    ev0(3)
    adain_forward(1)
    STAT[...] = jnp.zeros(STAT.shape, F32)
    ev2(2)
    ev1(3)
    ev3(2)
    conv_forward(1, block_out(0))
    adain_forward(2)
    STAT[...] = jnp.zeros(STAT.shape, F32)
    ev2(3)
    ev3(3)
    conv_forward(2, middle_out(2))
    adain_forward(3)
    conv_forward(3, block_out(1))

    def weight_grad(j):
        MW = 256

        def tile(t, carry):
            r0 = pl.multiple_of(t * MW, MW)
            for k in range(KERN):
                for h in range(2):
                    acc = None
                    for i in range(ITEMS):
                        part = dot(
                            AT[j, pl.ds(r0, MW), i * FRAMES:(i + 1) * FRAMES],
                            PAD[i, (2 - k) * SEG:(2 - k) * SEG + FRAMES, h * HALF:(h + 1) * HALF],
                        )
                        acc = part if acc is None else acc + part
                    DWF.at[j, h][pl.ds(k * D + r0, MW), :] = acc.astype(BF)
            return carry

        lax.fori_loop(0, D // MW, tile, 0)

    DWF = DW.reshape(CONVS, 2, KERN * D, HALF)

    def input_grad(j):
        STAT[...] = jnp.zeros(STAT.shape, F32)

        def tile(t, carry):
            i = t // (FRAMES // M)
            r0 = pl.multiple_of(lax.rem(t, FRAMES // M) * M, M)
            count = cnt[c, i]
            for n in range(2):
                acc = None
                for k in range(KERN):
                    for h in range(2):
                        weights = W[h, j].reshape(KERN * D, HALF)
                        part = dot_nt(
                            PAD[i, pl.ds(r0 + SEG * (2 - k), M), h * HALF:(h + 1) * HALF],
                            weights[k * D + n * HALF:k * D + (n + 1) * HALF],
                        )
                        acc = part if acc is None else acc + part
                for rb in range(0, M, 128):
                    mask = valid_rows(r0 + rb, 128, count, 0.5)
                    for cb in range(2):
                        cols = slice(n * HALF + cb * 128, n * HALF + cb * 128 + 128)
                        x = ST[j, i, pl.ds(r0 + rb, 128), cols].astype(F32)

                        def cf(k):
                            return COEF[j, i, k:k + 1, cols]
                        v = x * cf(C_SCALE) + cf(C_SHIFT)
                        th = jnp.tanh(v)
                        u = acc[rb:rb + 128, cb * 128:cb * 128 + 128] * mask
                        gy = (u + u * th) * (1.0 + v * (1.0 - th))
                        xhat = x * cf(C_INV) - cf(C_MI)
                        STAT[i, 0, :, cols] += fold(gy)
                        STAT[i, 1, :, cols] += fold(gy * xhat)
                        GY[i, pl.ds(r0 + rb, 128), cols] = gy.astype(BF)
            return carry

        lax.fori_loop(0, ITEMS * FRAMES // M, tile, 0)

    def send_gst(j, fn):
        def one(q, carry):
            d = j * nq + q
            variant = lax.rem(lax.rem(d, ndp // 2) // nb, 2)

            @pl.when(d != me)
            def _():
                fn(remote(GSTS.at[j, variant], GSTR.at[me], ss.at[5], rs.at[5], (d, c)))
            return carry
        lax.fori_loop(0, nq, one, 0)

    def adain_sums(j):
        for i in range(ITEMS):
            n = cnt[c, i].astype(F32)
            gt = jnp.sum(STAT[i, 0], axis=0, keepdims=True)
            gs = jnp.sum(STAT[i, 1], axis=0, keepdims=True)
            one, inv, mi = (COEF[j, i, k:k + 1] for k in (C_ONE, C_INV, C_MI))
            each = one / n
            COEF[j, i, C_2:C_2 + 1] = each * (gt - mi * gs)
            COEF[j, i, C_3:C_3 + 1] = each * inv * gs
            for b in range(4):
                part = (gs if b < 2 else gt)[:, (b % 2) * 256:(b % 2) * 256 + 256]
                for v in range(2):
                    GSTS[j, v, 4 * i + b:4 * i + b + 1, 0:256] = part
        for v in range(2):
            qb = (j % 2) * 2 + v
            GSTS[j, v, :, 256:384] = jnp.broadcast_to(
                BGRAD[j // 2, 0:1, qb * 128:qb * 128 + 128], (8, 128)
            )
        variant_me = lax.rem(lax.rem(me, ndp // 2) // nb, 2)

        @pl.when(me // nq == j)
        def _():
            GSTR[me] = GSTS[j, variant_me]
        send_gst(j, lambda copy: copy.start())

    def adain_backward(j):
        adain_sums(j)
        for i in range(ITEMS):
            count = cnt[c, i]

            def tile(t, carry):
                r0 = pl.multiple_of(t * TR, TR)
                mask = valid_rows(r0, TR, count, 1.0)
                for cb in range(4):
                    cols = slice(cb * 128, cb * 128 + 128)
                    gy = GY[i, pl.ds(r0, TR), cols].astype(F32)
                    x = ST[j, i, pl.ds(r0, TR), cols].astype(F32)
                    gh = gy * coef(j, i, C_ONE, cols) - x * coef(j, i, C_3, cols) - coef(j, i, C_2, cols)
                    gh = gh * mask
                    if j % 2 == 1:
                        PAD[i, pl.ds(r0 + SEG, TR), cols] = gh.astype(BF)
                    else:
                        g = G[i, pl.ds(r0, TR), cols].astype(F32) * HALF_ROOT + gh
                        if j > 0:
                            G[i, pl.ds(r0, TR), cols] = g.astype(BF)
                            g = g * HALF_ROOT
                            BGRAD[j // 2 - 1, :, cols] += fold(g.astype(BF).astype(F32))
                        PAD[i, pl.ds(r0 + SEG, TR), cols] = g.astype(BF)
                return carry

            lax.fori_loop(0, FRAMES // TR, tile, 0)
        if j > 0:
            edges()
        if j > 0 and j % 2 == 0:
            close_bias(j // 2 - 1)

    def close_bias(l):
        BGRAD[l] = jnp.broadcast_to(jnp.sum(BGRAD[l], axis=0, keepdims=True), (8, D))

    def rs_sib(j):
        return remote(DW.at[j, 1 - c], SIBR.at[j], rss.at[j], rsr.at[j], sib)

    def rs_second(j, fn):
        @pl.when(c == 0)
        def _():
            for k in range(1, n1):
                to = lax.rem(c1 + k, n1)
                fn(remote(DW.at[j, 0, to], RB.at[j, pl.ds((k - 1) * n2, n2)], rbs.at[j, k], rbr.at[j, k],
                          ((c0 * n1 + to) * n2 + c2, c)))

        @pl.when(c == 1)
        def _():
            for k in range(1, n2):
                to = lax.rem(c2 + k, n2)
                fn(remote(DW.at[j, 1, :, to], RB.at[j, pl.ds((k - 1) * n1, n1)], rbs.at[j, k], rbr.at[j, k],
                          ((c0 * n1 + c1) * n2 + to, c)))

    def rs_first(j, fn):
        @pl.when(c == 0)
        def _():
            for k in range(1, n2):
                to = lax.rem(c2 + k, n2)
                fn(remote(DW.at[j, 0, c1, to], RA.at[j, k - 1], ras.at[j, k], rar.at[j, k],
                          ((c0 * n1 + c1) * n2 + to, c)))

        @pl.when(c == 1)
        def _():
            for k in range(1, n1):
                to = lax.rem(c1 + k, n1)
                fn(remote(DW.at[j, 1, to, c2], RA.at[j, k - 1], ras.at[j, k], rar.at[j, k],
                          ((c0 * n1 + to) * n2 + c2, c)))

    def rs_plane(j, fn):
        @pl.when(c0 != j)
        def _():
            k = lax.rem(c0 - j + n0, n0)
            fn(remote(DW.at[j, c, c1, c2], ZR.at[k - 1], zs.at[j], zr.at[k], ((j * n1 + c1) * n2 + c2, c)))

    def rv0(j):
        rs_sib(j).start()

    def rv1(j):
        wait_bytes(SIBR.at[j], rsr.at[j])

        def one(y, carry):
            for x in range(n2):
                DW[j, c, y, x] = (DW[j, c, y, x].astype(F32) + SIBR[j, y, x].astype(F32)).astype(BF)
            return carry
        lax.fori_loop(0, n1, one, 0)
        rs_second(j, lambda copy: copy.start())

    def rv2(j):
        @pl.when(c == 0)
        def _():
            for k in range(1, n1):
                wait_bytes(RB.at[j, pl.ds((k - 1) * n2, n2)], rbr.at[j, k])
            for x in range(n2):
                total = DW[j, 0, c1, x].astype(F32)
                for k in range(1, n1):
                    total = total + RB[j, (k - 1) * n2 + x].astype(F32)
                DW[j, 0, c1, x] = total.astype(BF)

        @pl.when(c == 1)
        def _():
            for k in range(1, n2):
                wait_bytes(RB.at[j, pl.ds((k - 1) * n1, n1)], rbr.at[j, k])
            for y in range(n1):
                total = DW[j, 1, y, c2].astype(F32)
                for k in range(1, n2):
                    total = total + RB[j, (k - 1) * n1 + y].astype(F32)
                DW[j, 1, y, c2] = total.astype(BF)
        rs_first(j, lambda copy: copy.start())

    def rv3(j):
        def add(n):
            for k in range(1, n):
                wait_bytes(RA.at[j, k - 1], rar.at[j, k])
            total = DW[j, c, c1, c2].astype(F32)
            for k in range(1, n):
                total = total + RA[j, k - 1].astype(F32)
            DW[j, c, c1, c2] = total.astype(BF)

        @pl.when(c == 0)
        def _():
            add(n2)

        @pl.when(c == 1)
        def _():
            add(n1)
        rs_plane(j, lambda copy: copy.start())

    BGRAD[...] = jnp.zeros(BGRAD.shape, F32)
    for i in range(ITEMS):
        def enter(t, carry):
            r0 = pl.multiple_of(t * TR, TR)
            g = (G[i, pl.ds(r0, TR), :].astype(F32) * HALF_ROOT).astype(BF)
            PAD[i, pl.ds(r0 + SEG, TR), :] = g
            BGRAD[LAYERS - 1] += fold(g.astype(F32))
            return carry
        lax.fori_loop(0, FRAMES // TR, enter, 0)
    edges()
    close_bias(LAYERS - 1)

    weight_grad(3)
    rv0(3)
    input_grad(3)
    rv1(3)
    adain_backward(3)
    weight_grad(2)
    rv0(2)
    rv2(3)
    input_grad(2)
    rv3(3)
    rv1(2)
    adain_backward(2)
    weight_grad(1)
    rv0(1)
    rv2(2)
    input_grad(1)
    rv3(2)
    rv1(1)
    adain_backward(1)
    weight_grad(0)
    rv0(0)
    rv2(1)
    input_grad(0)
    rv3(1)
    rv1(0)
    adain_backward(0)

    for n in range(2):
        cols = slice(n * HALF, (n + 1) * HALF)
        pg = dot(OHP[0], PAD[0, SEG:SEG + FRAMES, cols]) + dot(OHP[1], PAD[1, SEG:SEG + FRAMES, cols])

        @pl.when(c == n)
        def _():
            PGX[c] = pg.astype(BF)

        @pl.when(c != n)
        def _():
            TABLE[:, 0:HALF] = pg.astype(BF)
    send_pgx = remote(TABLE.at[:, pl.ds(0, HALF)], PGX.at[c], ss.at[6], rs.at[6], sib)
    send_pgx.start()
    rv2(0)

    def unpermute(t, carry):
        f0 = pl.multiple_of(t * 256, 256)
        back = PM[:, pl.ds(f0, 256)].T
        for i in range(ITEMS):
            GY[i, pl.ds(f0, 256), :] = dot(back, COT[i]).astype(BF)
        return carry

    lax.fori_loop(0, FRAMES // 256, unpermute, 0)
    send_frames = remote(
        GY.at[:, pl.ds(pl.multiple_of((1 - c) * 512, 512), 512)], o_frames.at[c], ss.at[7], rs.at[7], sib
    )
    send_frames.start()
    keep_frames = pltpu.make_async_copy(
        GY.at[:, pl.ds(pl.multiple_of(c * 512, 512), 512)], o_frames.at[c], loc.at[5]
    )
    keep_frames.start()

    wait_bytes(PGX.at[0], rs.at[6])

    def send_pg(d):
        return remote(
            PGX.at[:, pl.ds(pl.multiple_of(d * 16, 16), 16)],
            o_phone.at[:, pl.ds(pl.multiple_of(me * 16, 16), 16)], ss.at[8], rs.at[8], (d, c),
        )

    if remote_phon:
        peers(lambda d: send_pg(d).start())
        mine = pl.ds(pl.multiple_of(me * 16, 16), 16)
        o_phone[:, mine] = PGX[:, mine]
    else:
        o_phone[...] = PGX[...]

    wait_bytes(GSTR.at[pl.ds(0, ndp - 1)], rs.at[5])
    gall = GSTR[:, :, 0:256].reshape(ndp * 8, 256)
    back_rows = jnp.zeros((ndp * 8, S), F32)
    for b in range(4):
        picked = jnp.where(row_kind == b, svall_of(SVR, ndp), 0.0)
        da = dot_tn(picked, gall, HIGH)
        part = None
        for qq in range(S // srows):
            piece = jnp.where(quarter == qq, da[qq * srows:(qq + 1) * srows], 0.0)
            part = piece if part is None else part + piece
        SX[0, 0:srows, b * 256:b * 256 + 256] = part
        back_rows = back_rows + dot_nt(
            jnp.where(row_kind == b, gall, 0.0), AE[:, b * 256:b * 256 + 256], HIGH
        )
    peers(lambda d: sent(send_par(d)))
    SGS[:, :, 0:S] = back_rows.reshape(ndp, 8, S)

    def send_sg(d):
        return remote(SGS.at[d, :, pl.ds(0, S)], SGR.at[me, :, pl.ds(0, S)], ss.at[9], rs.at[9], (d, c))

    peers(lambda d: send_sg(d).start())
    SGR[me, :, 0:S] = SGS[me, :, 0:S]
    SX[0, srows:srows + 8, :] = jnp.zeros((8, 1024), F32)
    SX[0, srows:srows + 1, 0:256] = jnp.sum(jnp.where(row_kind == offset_kind, gall, 0.0), axis=0, keepdims=True)
    SX[0, srows:srows + 1, 256:384] = jnp.sum(GSTR[:, 0:1, 256:384], axis=0)
    rv3(0)
    wait_bytes(SGR.at[pl.ds(0, ndp - 1), :, pl.ds(0, S)], rs.at[9])
    sg = jnp.sum(SGR[:, :, 0:S], axis=0)
    for i in range(ITEMS):
        SX[0, srows + 1 + i:srows + 2 + i, 0:S] = jnp.sum(sg[4 * i:4 * i + 4], axis=0, keepdims=True)
    send_sx = remote(SX.at[0], SX.at[1], ss.at[10], rs.at[10], sib)
    send_sx.start()

    total = DW[c0, c, c1, c2].astype(F32)
    for k in range(1, n0):
        wait_bytes(ZR.at[k - 1], zr.at[k])
        total = total + ZR[k - 1].astype(F32)
    GF[c] = total
    send_gf = remote(GF.at[c], GF.at[c], ss.at[11], rs.at[11], sib)
    send_gf.start()

    wait_bytes(SX.at[1], rs.at[10])
    o_small[0] = SX[0, srows:srows + 8, 0:384] + SX[1, srows:srows + 8, 0:384]
    o_small[1 + c] = SX[0, srows:srows + 8, 0:384]
    o_small[2 - c] = SX[1, srows:srows + 8, 0:384]
    for cb in range(8):
        cols = slice(cb * 128, cb * 128 + 128)
        o_gstyle[pl.ds(cb, srows, stride=8), :] = SX[0, 0:srows, cols] + SX[1, 0:srows, cols]
    wait_bytes(GF.at[c], rs.at[11])
    for cb in range(4):
        o_gconv[pl.ds(cb, shard, stride=4), :] = GF[cb // 2, :, (cb % 2) * 128:(cb % 2) * 128 + 128]

    if remote_phon:
        wait_bytes(o_phone.at[:, pl.ds(0, 16 * (ndp - 1))], rs.at[8])
    wait_bytes(GY.at[:, pl.ds(0, 512)], rs.at[7])
    keep_frames.wait()

    peers(lambda d: sent(send_sv(d)))
    if remote_phon:
        peers(lambda d: sent(send_phon(d)))
        peers(lambda d: sent(send_pg(d)))
    peers(lambda d: sent(send_sg(d)))
    for copy in (send_fph, send_cot, send_pgx, send_frames, send_sx, send_gf):
        sent(copy)
    for j in range(CONVS):
        send_gst(j, sent)
        sent(rs_sib(j))
        rs_second(j, sent)
        rs_first(j, sent)
        rs_plane(j, sent)
    own_z(False, sent)
    own_z(True, sent)
    for t in range(n0):
        zz = order(t)
        if t > 0:
            for q in range(nz):
                z_sends(zz, q, sent)
        first_sends(zz, sent)
        second_sends(zz, sent)
        sent(sib_send(zz))


def svall_of(SVR, ndp):
    return SVR[...].reshape(ndp * 8, S)


def run_train(cfg, phon, sv, fphone, cnt, cot, wmas, smas, brow, orow):
    ndp, (n0, n1, n2) = cfg["ndp"], cfg["dims"]
    shard, srows = cfg["shard"], cfg["srows"]
    nz = cfg["chunks"]
    nmax = max(n1, n2)
    vm = pltpu.VMEM
    dma = pltpu.SemaphoreType.DMA
    any_ = pl.BlockSpec(memory_space=pl.ANY)
    vmem = pl.BlockSpec(memory_space=pltpu.VMEM)
    smem = pl.BlockSpec(memory_space=pltpu.SMEM)
    scratch = [
        vm((2, n0, n1, n2, shard, HALF), BF),
        vm((ITEMS, PADDED, D), BF),
        vm((CONVS, D, ITEMS * FRAMES), BF),
        vm((CONVS, ITEMS, FRAMES, D), BF),
        vm((ITEMS, FRAMES, D), BF),
        vm((ITEMS, FRAMES, D), BF),
        vm((ITEMS, FRAMES, D), BF),
        vm((FRAMES, FRAMES), BF),
        vm((ITEMS, TABLE_ROWS, FRAMES), BF),
        vm((TABLE_ROWS, D), BF),
        vm((ITEMS, FRAMES), jnp.int32),
        vm((shard * 4, 128), F32),
        vm((srows * 8, 128), F32),
        vm((S, 1024), F32),
        vm((ndp, 8, S), F32),
        vm((ndp, 8, 384), F32),
        vm((ndp, 8, 384), F32),
        vm((CONVS, ITEMS, 16, D), F32),
        vm((ITEMS, 2, 8, D), F32),
        vm((LAYERS, 8, D), F32),
        vm((LAYERS, 8, D), F32),
        vm((CONVS, 2, 8, 384), F32),
        vm((ndp, 8, 384), F32),
        vm((2, srows + 8, 1024), F32),
        vm((CONVS, 2, n1, n2, shard, HALF), BF),
        vm((CONVS, n1, n2, shard, HALF), BF),
        vm((CONVS, max((n1 - 1) * n2, (n2 - 1) * n1), shard, HALF), BF),
        vm((CONVS, nmax - 1, shard, HALF), BF),
        vm((n0 - 1, shard, HALF), BF),
        vm((2, shard, HALF), F32),
        vm((2, TABLE_ROWS, HALF), BF),
        dma((6,)), dma((12,)), dma((12,)),
        dma((n0, nz, 2)), dma((n0, nz)),
        dma((n0, nmax)), dma((n0, nmax)),
        dma((n0, nmax)), dma((n0, nmax)),
        dma((n0,)), dma((n0,)),
        dma((CONVS,)), dma((CONVS,)),
        dma((CONVS, nmax)), dma((CONVS, nmax)),
        dma((CONVS, nmax)), dma((CONVS, nmax)),
        dma((CONVS,)), dma((n0,)),
    ]
    return pl.pallas_call(
        functools.partial(train_kernel, cfg),
        out_shape=(
            jax.ShapeDtypeStruct((2, ITEMS, FRAMES // 2, D), BF),
            jax.ShapeDtypeStruct((2, TABLE_ROWS, HALF), BF),
            jax.ShapeDtypeStruct((3, 8, 384), F32),
            jax.ShapeDtypeStruct((shard * 4, 128), F32),
            jax.ShapeDtypeStruct((srows * 8, 128), F32),
        ),
        in_specs=[any_, vmem, any_, smem, any_, any_, any_, vmem, vmem],
        out_specs=(any_, vmem, vmem, vmem, vmem),
        scratch_shapes=scratch,
        compiler_params=pltpu.CompilerParams(
            collective_id=0, has_side_effects=True, vmem_limit_bytes=63 * 2**20
        ),
    )(phon, sv, fphone, cnt, cot, wmas, smas, brow, orow)


def adamw_update(master, moment, square, gradient, step_value):
    new_moment = MOMENT_DECAY * moment + (1.0 - MOMENT_DECAY) * gradient
    new_square = SQUARE_DECAY * square + (1.0 - SQUARE_DECAY) * gradient * gradient
    first_fix = 1.0 - jnp.power(jnp.float32(MOMENT_DECAY), step_value)
    second_fix = 1.0 - jnp.power(jnp.float32(SQUARE_DECAY), step_value)
    updated = master - LEARN_RATE * (
        new_moment / first_fix / (jnp.sqrt(new_square / second_fix) + ADAM_EPS)
        + WEIGHT_DECAY * master
    )
    return (updated, new_moment, new_square, updated.astype(BF))


def on_device(
    phonemes, style_vector, frame_phone, frame_count, cotangent,
    conv_master, conv_moment, conv_square, bias_master, bias_moment, bias_square,
    style_master, style_moment, style_square, offset_master, offset_moment, offset_square,
):
    ndp = lax.axis_size("dp")
    micros, items, slots, _ = phonemes.shape
    shard = conv_master.shape[0] // D
    srows = style_master.shape[0] // (2 * D)
    bsize, osize = bias_master.shape[0], offset_master.shape[0]
    remote_phon = (ITEMS * slots) % 16 == 0
    cfg = dict(
        ndp=ndp, dims=factor(ndp), slots=slots, shard=shard, srows=srows, remote_phon=remote_phon,
        chunks=2 if shard % 32 == 0 else 1,
    )
    me = lax.axis_index("dp")
    c = lax.axis_index("seq")
    if remote_phon:
        phon = phonemes.reshape(micros, items * slots, D)
    else:
        mine = lax.dynamic_index_in_dim(phonemes, c, 0, keepdims=False)
        mine = mine.reshape(ndp, ITEMS * slots, D)
        phon = lax.all_to_all(mine, "dp", split_axis=0, concat_axis=0, tiled=True).reshape(TABLE_ROWS, D)
    spread = 128 // bsize
    brow = jnp.where(
        jnp.arange(128) // bsize == me % spread, jnp.tile(bias_master, spread), 0.0
    ).reshape(1, 128)
    if osize == 256:
        orow = offset_master.reshape(1, 256)
    else:
        wide = 256 // osize
        orow = jnp.where(
            jnp.arange(256) // osize == me % wide, jnp.tile(offset_master, wide), 0.0
        ).reshape(1, 256)
    frames, phone, small, gconv, gstyle = run_train(
        cfg, phon, style_vector, frame_phone, frame_count, cotangent,
        conv_master.reshape(shard * 4, 128), style_master.reshape(srows * 8, 128), brow, orow,
    )
    if remote_phon:
        phone_grads = phone.reshape(micros, items, slots, HALF).astype(F32)
    else:
        moved = lax.all_to_all(
            phone.reshape(micros, ndp, ITEMS * slots, HALF), "dp", split_axis=1, concat_axis=1, tiled=True
        )
        phone_grads = moved.reshape(micros, items, slots, HALF).astype(F32)
    style_grads = small[1:3, 1:3, 0:S]
    gbias = lax.dynamic_slice(small[0, 0, 256:384], ((me % spread) * bsize,), (bsize,))
    goff = small[0, 0, 0:256]
    if osize != 256:
        goff = lax.dynamic_slice(goff, ((me % (256 // osize)) * osize,), (osize,))
    step_value = jnp.float32(STEP)
    conv_out = adamw_update(conv_master, conv_moment, conv_square, gconv.reshape(-1), step_value)
    bias_out = adamw_update(bias_master, bias_moment, bias_square, gbias, step_value)
    style_out = adamw_update(style_master, style_moment, style_square, gstyle.reshape(-1), step_value)
    offset_out = adamw_update(offset_master, offset_moment, offset_square, goff, step_value)
    return (
        frames.astype(F32), phone_grads, style_grads, *conv_out, *bias_out, *style_out, *offset_out,
    )


def solution(mesh):
    return jax.shard_map(
        on_device,
        mesh=mesh,
        in_specs=(
            P(None, None, "dp", None), P(None, "dp", None), P(None, "dp", "seq"), P(None, "dp"),
            P(None, "dp", "seq", None), *[P("dp")] * 12,
        ),
        out_specs=(
            P(None, "dp", "seq", None), P(None, None, "dp", "seq"), P(None, "dp", None), *[P("dp")] * 16,
        ),
        check_vma=False,
    )
```

```python
import functools

import jax
import jax.numpy as jnp
from jax import lax
from jax.experimental import pallas as pl
from jax.experimental.pallas import tpu as pltpu
from jax.sharding import PartitionSpec as P

D = 512
S = 128
KERN = 3
LAYERS = 2
CONVS = 2 * LAYERS
PH = 128
STEP = 10
FRAMES = 1024
SEG = 16
RUN = FRAMES // SEG
HALF = D // 2
ITEMS = 2
PADDED = FRAMES + 2 * SEG
TABLE_ROWS = ITEMS * PH

NORM_EPS = 1e-05
HALF_ROOT = 0.7071067811865476
MOMENT_DECAY = 0.9
SQUARE_DECAY = 0.999
LEARN_RATE = 0.05
WEIGHT_DECAY = 0.01
ADAM_EPS = 1e-08

BF = jnp.bfloat16
F32 = jnp.float32
MESH = pl.DeviceIdType.MESH

C_SCALE, C_SHIFT, C_INV, C_MI, C_ONE, C_2, C_3 = range(7)


PLAN = (
    (
        (4.5, "v", 0), (7.0, "z", 1), (7.0, "f", 1), (11.0, "b", 0), (14.0, "z", 2), (14.0, "f", 2), (19.0, "b", 1),
        (21.0, "z", 3), (21.0, "f", 3), (27.5, "b", 2), (36.0, "b", 3),
    ),
    (
        (10.7, "v", 1), (11.0, "z", 0), (11.0, "f", 0), (11.1, "z", 2), (11.1, "f", 2), (11.2, "b", 1), (20.5, "b", 0),
        (21.0, "z", 3), (21.0, "f", 3), (29.0, "b", 2), (37.5, "b", 3),
    ),
    (
        (6.0, "w", 0), (6.0, "f", 0), (10.7, "v", 2), (11.0, "b", 2), (17.0, "z", 1), (17.0, "f", 1), (18.5, "b", 0),
        (19.0, "z", 3), (19.0, "f", 3), (27.0, "b", 1), (35.5, "b", 3),
    ),
    (
        (10.7, "v", 3), (11.0, "z", 0), (11.0, "f", 0), (12.0, "b", 3), (21.5, "b", 0), (21.6, "z", 1), (21.6, "f", 1),
        (24.0, "z", 2), (24.0, "f", 2), (30.0, "b", 1), (38.5, "b", 2),
    ),
)
EARLY = ((2,), (0,), (1,), (2,))
LATE = ((1,), (2, 3), (3, 0), (1, 0))
RELAY = (2, 3)


def factor(ndp):
    return {16: (4, 2, 2), 128: (4, 8, 4)}.get(ndp, (4, ndp // 4, 1))


def dot(a, b):
    return jnp.dot(a, b, preferred_element_type=F32)


def dot_nt(a, b):
    return lax.dot_general(a, b, (((1,), (1,)), ((), ())), preferred_element_type=F32)


def dot_tn(a, b):
    return lax.dot_general(a, b, (((0,), (0,)), ((), ())), preferred_element_type=F32)


def fold(tile):
    rows, cols = tile.shape
    return jnp.sum(tile.reshape(rows // 8, 8, cols), axis=0)


def valid_rows(start, rows, count, value):
    i = lax.broadcasted_iota(jnp.int32, (rows, 128), 0)
    frame = (i & (SEG - 1)) * RUN + (i >> 4) + start // SEG
    return jnp.where(frame < count, jnp.float32(value), jnp.float32(0.0))


def train_kernel(cfg, *refs):
    ndp, (n0, n1, n2), slots = cfg["ndp"], cfg["dims"], cfg["slots"]
    shard, srows, remote_phon = cfg["shard"], cfg["srows"], cfg["remote_phon"]
    comm = cfg.get("comm", True)
    skip = cfg.get("skip", ())
    nq = ndp // CONVS
    nb = ndp // 8
    (
        phon, sv, fphone, cnt, cot, wmas, smas, rowin,
        o_frames, o_phone, o_sg, o_gbias, o_goff, o_gconv, o_gstyle,
        W, PAD, AT, ST, G, GY, COT, PM, OHP, TABLE, FPH, WM, SM, AE,
        SVR, PARS, PARR, COEF, STAT, BIAS, BGRAD, GSTS, GSTR, BGR, SGR, SX,
        DW, SIBR, RB, RA, ZR, GF, PGX,
        loc, ss, rs, s_o, r_o, s_z, r_z, s_f, r_f, s_b, r_b,
        rss, rsr, rbs, rbr, ras, rar, zs, zr,
    ) = refs
    SGS = SVR
    me = lax.axis_index("dp")
    c = lax.axis_index("seq")
    c0, c1, c2 = me // (n1 * n2), (me // n2) % n1, me % n2
    sib = (me, 1 - c)

    def remote(src, dst, send, recv, target):
        return pltpu.make_async_remote_copy(
            src_ref=src, dst_ref=dst, send_sem=send, recv_sem=recv, device_id=target, device_id_type=MESH
        )

    def wait_bytes(ref, sem):
        pltpu.make_async_copy(ref, ref, sem).wait()

    def sent(copy):
        copy.wait_send()

    def peers(fn):
        def one(d, carry):
            fn(lax.rem(me + d, ndp))
            return carry
        lax.fori_loop(1, ndp, one, 0)

    barrier = pltpu.get_barrier_semaphore()
    peers(lambda d: pl.semaphore_signal(barrier, inc=1, device_id=(d, c), device_id_type=MESH))
    pl.semaphore_signal(barrier, inc=1, device_id=sib, device_id_type=MESH)

    own_in = [
        pltpu.make_async_copy(wmas, WM, loc.at[0]),
        pltpu.make_async_copy(smas, SM, loc.at[1]),
        pltpu.make_async_copy(cot.at[c], COT.at[:, pl.ds(pl.multiple_of(c * HALF * 2, 512), 512)], loc.at[2]),
        pltpu.make_async_copy(fphone.at[c], FPH.at[:, pl.ds(pl.multiple_of(c * HALF * 2, 512), 512)], loc.at[3]),
    ]
    if remote_phon:
        own_in.append(
            pltpu.make_async_copy(
                phon.at[c, pl.ds(pl.multiple_of(me * 16, 16), 16)],
                TABLE.at[pl.ds(pl.multiple_of(me * 16, 16), 16)], loc.at[4],
            )
        )
    else:
        own_in.append(pltpu.make_async_copy(phon, TABLE, loc.at[4]))
    for copy in own_in:
        copy.start()

    own_in[0].wait()
    for cb in range(4):
        W[cb // 2, c0, c1, c2, :, (cb % 2) * 128:(cb % 2) * 128 + 128] = WM[
            pl.ds(cb, shard, stride=4), :
        ].astype(BF)
    own_in[1].wait()
    quarter = lax.rem(me, S // srows)
    for cb in range(8):
        block = SM[pl.ds(cb, srows, stride=8), :].astype(BF).astype(F32)
        for qq in range(S // srows):
            AE[qq * srows:(qq + 1) * srows, cb * 128:cb * 128 + 128] = jnp.where(quarter == qq, block, 0.0)
    bias_row = rowin[8:16, :].astype(BF).astype(F32)
    vec = sv[c].astype(F32)
    kind8 = lax.broadcasted_iota(jnp.int32, (8, S), 0)
    SVR[me] = jnp.where(kind8 == 0, vec[0:1], jnp.where(kind8 == 1, vec[1:2], bias_row))

    def make_perm(t, carry):
        r0 = pl.multiple_of(t * 128, 128)
        row = lax.broadcasted_iota(jnp.int32, (128, FRAMES), 0)
        col = lax.broadcasted_iota(jnp.int32, (128, FRAMES), 1)
        frame = (row & (SEG - 1)) * RUN + (row >> 4) + r0 // SEG
        PM[pl.ds(r0, 128), :] = jnp.where(col == frame, 1.0, 0.0).astype(BF)
        return carry

    lax.fori_loop(0, FRAMES // 128, make_perm, 0)

    pl.semaphore_wait(barrier, ndp)

    def send_sv(d):
        return remote(SVR.at[me], SVR.at[me], ss.at[0], rs.at[0], (d, c))

    def send_phon(d):
        return remote(
            phon.at[c, pl.ds(pl.multiple_of(d * 16, 16), 16)],
            TABLE.at[pl.ds(pl.multiple_of(me * 16, 16), 16)], ss.at[1], rs.at[1], (d, c),
        )

    send_fph = remote(
        fphone.at[1 - c], FPH.at[:, pl.ds(pl.multiple_of(c * 512, 512), 512)], ss.at[2], rs.at[2], sib
    )
    send_cot = remote(
        cot.at[1 - c], COT.at[:, pl.ds(pl.multiple_of(c * 512, 512), 512)], ss.at[3], rs.at[3], sib
    )
    def z_send(zz, to, k, fn):
        piece = W.at[c, zz, c1, c2]
        fn(remote(piece, piece, s_z.at[k], r_z.at[zz], ((to * n1 + c1) * n2 + c2, c)))

    def z_sends(sends, p, fn):
        for to in sends[p]:
            z_send(p, to, to, fn)

    def z_wait(zz):
        wait_bytes(W.at[c, zz, c1, c2], r_z.at[zz])

    def ev_w(fn=None):
        if fn is None:
            z_wait(0)
        z_send(0, RELAY[1], RELAY[0], fn or start)

    def plane_sends(zz, fn):
        piece = W.at[c, zz, c1, c2]
        for k in range(1, n1 * n2):
            y, x = lax.rem(c1 + k // n2, n1), lax.rem(c2 + k % n2, n2)
            fn(remote(piece, piece, s_f.at[zz, k], r_f.at[zz, k], ((c0 * n1 + y) * n2 + x, c)))

    def plane_wait(zz):
        for k in range(1, n1 * n2):
            wait_bytes(W.at[c, zz, c1, c2], r_f.at[zz, k])

    def sib_send(zz):
        return remote(W.at[c, zz], W.at[c, zz], s_b.at[zz], r_b.at[zz], sib)

    def start(copy):
        copy.start()

    def ev_b(zz):
        plane_wait(zz)
        sib_send(zz).start()

    def plane_events(p):
        events = []
        for at, kind, zz in PLAN[p]:
            fn = {
                "v": lambda: z_sends(LATE, p, start),
                "z": lambda zz=zz: z_wait(zz),
                "w": ev_w,
                "f": lambda zz=zz: plane_sends(zz, start),
                "b": lambda zz=zz: ev_b(zz),
            }[kind]
            events.append((at, fn))
            if kind == "b":
                ready[p][zz] = at + 0.1
        return events

    ready = {p: {} for p in range(n0)}
    plan = {p: plane_events(p) for p in range(n0)}
    clock = {p: 0.0 for p in range(n0)}

    def take(passed, until=None):
        dues = {}
        for p in range(n0):
            clock[p] += passed
            if until is not None:
                clock[p] = max(clock[p], ready[p][until])
            dues[p] = [e for e in plan[p] if e[0] <= clock[p]]
            plan[p] = plan[p][len(dues[p]):]
            if until is not None:
                clock[p] += 2.4
        return dues

    def run_due(dues, when=True):
        for p, due in dues.items():
            if due:
                @pl.when(jnp.logical_and(c0 == p, when))
                def _(due=due):
                    for _, fn in due:
                        fn()

    def slot(passed, until=None):
        run_due(take(passed, until))
        if until is not None:
            wait_bytes(W.at[c, until], r_b.at[until])

    peers(lambda d: send_sv(d).start())

    for p in range(n0):
        @pl.when(c0 == p)
        def _():
            z_sends(EARLY, p, start)
    plane_sends(c0, start)
    send_fph.start()
    send_cot.start()

    slot(3.0)
    own_in[3].wait()
    wait_bytes(FPH.at[:, pl.ds(0, 512)], rs.at[2])
    for i in range(ITEMS):
        phone = FPH[i:i + 1, :]
        if slots & (slots - 1) == 0:
            shift = slots.bit_length() - 1
            place = ((phone >> shift) << (shift + 1)) + i * slots + (phone & (slots - 1))
        else:
            place = (phone // slots) * (2 * slots) + i * slots + phone % slots
        spot = lax.broadcasted_iota(jnp.int32, (TABLE_ROWS, FRAMES), 0)
        onehot = jnp.where(spot == place, 1.0, 0.0).astype(BF)
        for t in range(4):
            OHP[i, :, t * 256:t * 256 + 256] = dot_nt(onehot, PM[t * 256:t * 256 + 256, :]).astype(BF)
        if i == 0 and remote_phon:
            peers(lambda d: send_phon(d).start())
        slot(1.5)

    own_in[2].wait()
    wait_bytes(COT.at[:, pl.ds(0, 512)], rs.at[3])
    for i in range(ITEMS):
        count = cnt[c, i]

        def permute(t, carry):
            r0 = pl.multiple_of(t * 256, 256)
            y = dot(PM[pl.ds(r0, 256), :], COT[i])
            mask = valid_rows(r0, 256, count, 1.0)
            G[i][pl.ds(r0, 256), :] = (y * jnp.concatenate([mask] * 4, axis=1)).astype(BF)
            return carry

        lax.fori_loop(0, 4, permute, 0)
        slot(1.3)

    row_kind = lax.broadcasted_iota(jnp.int32, (ndp * 16, 1), 0) & 7

    def style_rows():
        got = SVR[...]
        pair = [jnp.broadcast_to(got[:, i:i + 1, :], (ndp, 8, S)) for i in range(ITEMS)]
        return jnp.concatenate(pair, axis=1).reshape(ndp * 16, S)

    wait_bytes(SVR.at[pl.ds(0, ndp - 1)], rs.at[0])
    svall = style_rows()
    acc = jnp.zeros((ndp * 16, 128), F32)
    for b in range(8):
        acc = acc + dot(
            jnp.where(row_kind == b, svall, 0.0).astype(BF), AE[:, b * 128:b * 128 + 128].astype(BF)
        )
    offs = rowin[0:8, :].astype(BF).astype(F32)
    acc = acc.reshape(ndp, 16, 128) + jnp.concatenate([offs, offs], axis=0).reshape(1, 16, 128)
    PARS[...] = acc.astype(BF)

    def send_par(d):
        return remote(PARS.at[d], PARR.at[me], ss.at[4], rs.at[4], (d, c))

    peers(lambda d: send_par(d).start())
    PARR[me] = PARS[me]
    slot(2.0)
    for i in range(ITEMS):
        STAT[i][...] = jnp.zeros(STAT[i].shape, F32)
    own_in[4].wait()
    if remote_phon:
        wait_bytes(TABLE.at[pl.ds(0, 16 * (ndp - 1))], rs.at[1])
    for i in range(ITEMS):
        count = cnt[c, i]
        for t in range(4):
            x = dot(OHP[i, :, t * 256:t * 256 + 256].T, TABLE[...])
            mask = valid_rows(t * 256, 256, count, 1.0)
            x = x * jnp.concatenate([mask] * 4, axis=1)
            ST[0][i][t * 256:t * 256 + 256, :] = x.astype(BF)
            STAT[i][0] += fold(x)
            STAT[i][1] += fold(x * x)
        slot(3.4 if i == 0 else 1.0)

    wait_bytes(PARR.at[pl.ds(0, ndp - 1)], rs.at[4])
    for j in range(CONVS):
        total = jnp.sum(PARR[j * nq:(j + 1) * nq].astype(F32), axis=0)
        for i in range(ITEMS):
            for b in range(8):
                COEF[j][i][8 + b // 4:9 + b // 4, (b % 4) * 128:(b % 4) * 128 + 128] = total[
                    8 * i + b:8 * i + b + 1, :
                ]
    for l in range(LAYERS):
        for qb in range(4):
            first = l * (ndp // 2) + qb * nb
            BIAS[l, :, qb * 128:qb * 128 + 128] = jnp.broadcast_to(
                jnp.sum(SVR[first:first + nb], axis=0)[2:3, :], (8, 128)
            )
    slot(0.5)

    def stats_to_coef(j, i):
        n = cnt[c, i].astype(F32)
        sums = jnp.sum(STAT[i][0], axis=0, keepdims=True)
        squares = jnp.sum(STAT[i][1], axis=0, keepdims=True)
        STAT[i][...] = jnp.zeros(STAT[i].shape, F32)
        mean = sums / n
        var = jnp.maximum(squares / n - mean * mean, 0.0)
        inv = lax.rsqrt(var + NORM_EPS)
        one = (1.0 + COEF[j][i][8:9]) * inv
        shift = COEF[j][i][9:10] - mean * one

        def put(k, v):
            COEF[j][i][k:k + 1] = v
        put(C_SCALE, 0.5 * one)
        put(C_SHIFT, 0.5 * shift)
        put(C_INV, inv)
        put(C_MI, mean * inv)
        put(C_ONE, one)

    def coef(j, i, k, cols):
        return COEF[j][i][k:k + 1, cols]

    def edges(pad, i):
        row = lax.broadcasted_iota(jnp.int32, (SEG, D), 0)
        last = PAD[pad][i][FRAMES:FRAMES + SEG, :].astype(F32)
        head = jnp.where(row == 0, 0.0, pltpu.roll(last, 1, 0))
        PAD[pad][i][0:SEG, :] = head.astype(BF)
        first = PAD[pad][i][SEG:2 * SEG, :].astype(F32)
        tail = jnp.where(row == SEG - 1, 0.0, pltpu.roll(first, SEG - 1, 0))
        PAD[pad][i][FRAMES + SEG:PADDED, :] = tail.astype(BF)

    TR = 128
    M = 512

    def adain_tile(j, i):
        count = cnt[c, i]

        def run(r1):
            for rb in range(0, M, TR):
                r0 = pl.multiple_of(r1 + rb, TR)
                mask = valid_rows(r0, TR, count, 1.0)
                for cb in range(4):
                    cols = slice(cb * 128, cb * 128 + 128)
                    x = ST[j][i][pl.ds(r0, TR), cols].astype(F32)
                    v = x * coef(j, i, C_SCALE, cols) + coef(j, i, C_SHIFT, cols)
                    a = ((v + v * jnp.tanh(v)) * mask).astype(BF)
                    PAD[j % 2][i][pl.ds(r0 + SEG, TR), cols] = a
                    AT[j][i][cols, pl.ds(r0, TR)] = a.T
        return run

    def conv_tile(j, i, epilogue):
        def run(r0):
            for h in range(2):
                acc = None
                weights = W[h, j].reshape(KERN * D, HALF)
                for k in range(KERN):
                    part = dot(PAD[j % 2][i][pl.ds(r0 + SEG * k, M), :], weights[k * D:(k + 1) * D])
                    acc = part if acc is None else acc + part
                epilogue(i, r0, h, acc)
        return run

    def together(passed, *parts, then=None):
        steps = FRAMES // M
        dues = [take(passed) for _ in range(steps - 1)]

        def step(t, carry):
            for part in parts:
                part(pl.multiple_of(t * M, M))
            for k, due in enumerate(dues):
                run_due(due, t == k)
            if then is not None:
                pl.when(t == 0)(then)
            return carry

        lax.fori_loop(0, steps, step, 0)
        slot(passed)

    def middle_out(j):
        def epilogue(i, r0, h, acc):
            count = cnt[c, i]
            masks = [valid_rows(r0 + rb, 128, count, 1.0) for rb in range(0, M, 128)]
            for cb in range(2):
                cols = slice(h * HALF + cb * 128, h * HALF + cb * 128 + 128)
                sums = [0.0, 0.0]
                for rb in range(0, M, 128):
                    p = acc[rb:rb + 128, cb * 128:cb * 128 + 128]
                    ST[j + 1][i][pl.ds(r0 + rb, 128), cols] = p.astype(BF)
                    kept = p * masks[rb // 128]
                    sums = [sums[0] + fold(kept), sums[1] + fold(kept * p)]
                for n in range(2):
                    STAT[i][n, :, cols] += sums[n]
        return epilogue

    def block_out(l):
        def epilogue(i, r0, h, acc):
            count = cnt[c, i]
            masks = [valid_rows(r0 + rb, 128, count, HALF_ROOT) for rb in range(0, M, 128)]
            for cb in range(2):
                cols = slice(h * HALF + cb * 128, h * HALF + cb * 128 + 128)
                sums = [0.0, 0.0]
                for rb in range(0, M, 128):
                    q = acc[rb:rb + 128, cb * 128:cb * 128 + 128] + BIAS[l, 0:1, cols]
                    x = (ST[2 * l][i][pl.ds(r0 + rb, 128), cols].astype(F32) + q) * masks[rb // 128]
                    if l < LAYERS - 1:
                        ST[2 * l + 2][i][pl.ds(r0 + rb, 128), cols] = x.astype(BF)
                        sums = [sums[0] + fold(x), sums[1] + fold(x * x)]
                    else:
                        COT[i, pl.ds(r0 + rb, 128), cols] = x.astype(BF)
                if l < LAYERS - 1:
                    for n in range(2):
                        STAT[i][n, :, cols] += sums[n]
        return epilogue

    def enter_tile(i):
        def run(r1):
            for rb in range(0, M, TR):
                r0 = pl.multiple_of(r1 + rb, TR)
                g = (G[i][pl.ds(r0, TR), :].astype(F32) * HALF_ROOT).astype(BF)
                PAD[1][i][pl.ds(r0 + SEG, TR), :] = g
                BGRAD[LAYERS - 1] += fold(g.astype(F32))
        return run

    def grad_weight_tile(j):
        def run(r1):
            h = jnp.where(r1 == 0, 1 - c, c)
            cols = pl.ds(pl.multiple_of(h * HALF, HALF), HALF)
            for r0 in range(0, D, 256):
                for k in range(KERN):
                    acc = None
                    for i in range(ITEMS):
                        part = dot(
                            AT[j][i][r0:r0 + 256, :], PAD[j % 2][i][(2 - k) * SEG:(2 - k) * SEG + FRAMES, cols]
                        )
                        acc = part if acc is None else acc + part
                    DWF[j].at[h][k * D + r0:k * D + r0 + 256, :] = acc.astype(BF)
        return run

    DWF = [DW[j].reshape(2, KERN * D, HALF) for j in range(CONVS)]

    def grad_input_tile(j, i):
        count = cnt[c, i]

        def run(r0):
            for n in range(2):
                acc = None
                for k in range(KERN):
                    for h in range(2):
                        weights = W[h, j].reshape(KERN * D, HALF)
                        part = dot_nt(
                            PAD[j % 2][i][pl.ds(r0 + SEG * (2 - k), M), h * HALF:(h + 1) * HALF],
                            weights[k * D + n * HALF:k * D + (n + 1) * HALF],
                        )
                        acc = part if acc is None else acc + part
                masks = [valid_rows(r0 + rb, 128, count, 0.5) for rb in range(0, M, 128)]
                for cb in range(2):
                    cols = slice(n * HALF + cb * 128, n * HALF + cb * 128 + 128)
                    sums = [0.0, 0.0]
                    for rb in range(0, M, 128):
                        mask = masks[rb // 128]
                        x = ST[j][i][pl.ds(r0 + rb, 128), cols].astype(F32)
                        v = x * coef(j, i, C_SCALE, cols) + coef(j, i, C_SHIFT, cols)
                        th = jnp.tanh(v)
                        u = acc[rb:rb + 128, cb * 128:cb * 128 + 128] * mask
                        gy = (u + u * th) * (1.0 + v * (1.0 - th))
                        xhat = x * coef(j, i, C_INV, cols) - coef(j, i, C_MI, cols)
                        sums = [sums[0] + fold(gy), sums[1] + fold(gy * xhat)]
                        GY[i][pl.ds(r0 + rb, 128), cols] = gy.astype(BF)
                    for k in range(2):
                        STAT[i][k, :, cols] += sums[k]
        return run

    def send_gst(j, fn):
        def one(q, carry):
            d = j * nq + q

            @pl.when(d != me)
            def _():
                fn(remote(GSTS.at[j], GSTR.at[me], ss.at[5], rs.at[5], (d, c)))
            return carry
        lax.fori_loop(0, nq, one, 0)

    def send_bias(l, fn):
        def one(q, carry):
            d = l * (ndp // 2) + q
            part = BGRAD.at[l, :, pl.ds(pl.multiple_of(q // nb * 128, 128), 128)]

            @pl.when(d != me)
            def _():
                fn(remote(part, BGR.at[me], ss.at[7], rs.at[7], (d, c)))
            return carry
        lax.fori_loop(0, ndp // 2, one, 0)

    def adain_sums(j, i):
        n = cnt[c, i].astype(F32)
        gt = jnp.sum(STAT[i][0], axis=0, keepdims=True)
        gs = jnp.sum(STAT[i][1], axis=0, keepdims=True)
        STAT[i][...] = jnp.zeros(STAT[i].shape, F32)
        one, inv, mi = (COEF[j][i][k:k + 1] for k in (C_ONE, C_INV, C_MI))
        each = one / n
        COEF[j][i][C_2:C_2 + 1] = each * (gt - mi * gs)
        COEF[j][i][C_3:C_3 + 1] = each * inv * gs
        rows = [x[:, b * 128:b * 128 + 128] for x in (gs, gt) for b in range(4)]
        GSTS[j, 8 * i:8 * i + 8, :] = jnp.concatenate(rows, axis=0).astype(BF)
        if i == ITEMS - 1:
            @pl.when(me // nq == j)
            def _():
                GSTR[me] = GSTS[j]
            send_gst(j, start)

    def adain_back_tile(j, i):
        count = cnt[c, i]

        def run(r1):
            for rb in range(0, M, TR):
                r0 = pl.multiple_of(r1 + rb, TR)
                mask = valid_rows(r0, TR, count, 1.0)
                for cb in range(4):
                    cols = slice(cb * 128, cb * 128 + 128)
                    gy = GY[i][pl.ds(r0, TR), cols].astype(F32)
                    x = ST[j][i][pl.ds(r0, TR), cols].astype(F32)
                    g = gy * coef(j, i, C_ONE, cols) - x * coef(j, i, C_3, cols) - coef(j, i, C_2, cols)
                    g = g * mask
                    if j % 2 == 0:
                        g = G[i][pl.ds(r0, TR), cols].astype(F32) * HALF_ROOT + g
                        if j > 0:
                            G[i][pl.ds(r0, TR), cols] = g.astype(BF)
                            g = g * HALF_ROOT
                            BGRAD[j // 2 - 1, :, cols] += fold(g.astype(BF).astype(F32))
                    PAD[1 - j % 2][i][pl.ds(r0 + SEG, TR), cols] = g.astype(BF)
        return run

    def rs_sib(j):
        return remote(DW[j].at[1 - c], SIBR.at[j], rss.at[j], rsr.at[j], sib)

    def rs_second(j, fn):
        @pl.when(c == 0)
        def _():
            for k in range(1, n1):
                to = lax.rem(c1 + k, n1)
                fn(remote(DW[j].at[0, to], RB.at[j, pl.ds((k - 1) * n2, n2)], rbs.at[j, k], rbr.at[j, k],
                          ((c0 * n1 + to) * n2 + c2, c)))

        @pl.when(c == 1)
        def _():
            for k in range(1, n2):
                to = lax.rem(c2 + k, n2)
                fn(remote(DW[j].at[1, :, to], RB.at[j, pl.ds((k - 1) * n1, n1)], rbs.at[j, k], rbr.at[j, k],
                          ((c0 * n1 + c1) * n2 + to, c)))

    def rs_first(j, fn):
        @pl.when(c == 0)
        def _():
            for k in range(1, n2):
                to = lax.rem(c2 + k, n2)
                fn(remote(DW[j].at[0, c1, to], RA.at[j, k - 1], ras.at[j, k], rar.at[j, k],
                          ((c0 * n1 + c1) * n2 + to, c)))

        @pl.when(c == 1)
        def _():
            for k in range(1, n1):
                to = lax.rem(c1 + k, n1)
                fn(remote(DW[j].at[1, to, c2], RA.at[j, k - 1], ras.at[j, k], rar.at[j, k],
                          ((c0 * n1 + to) * n2 + c2, c)))

    def rs_plane(j, fn):
        outer, inner = ((3, 2) if j < 2 else (0, 1))
        for p, to, k in ((j ^ 1, j, 0), (outer, inner, 2 + j % 2)):
            @pl.when(c0 == p)
            def _(to=to, k=k):
                fn(remote(DW[j].at[c, c1, c2], ZR.at[k], zs.at[j], zr.at[k], ((to * n1 + c1) * n2 + c2, c)))

    def rs_inner(j, fn):
        @pl.when(c0 == (2 if j < 2 else 1))
        def _():
            fn(remote(DW[j].at[c, c1, c2], ZR.at[1], zs.at[j], zr.at[1], ((j * n1 + c1) * n2 + c2, c)))

    def rv4(j):
        @pl.when(c0 == (2 if j < 2 else 1))
        def _():
            k = 2 + j % 2
            wait_bytes(ZR.at[k], zr.at[k])
            DW[j][c, c1, c2] = (DW[j][c, c1, c2].astype(F32) + ZR[k].astype(F32)).astype(BF)
        rs_inner(j, start)

    def rv0(j):
        rs_sib(j).start()

    def rv1(j):
        wait_bytes(SIBR.at[j], rsr.at[j])

        def one(y, carry):
            for x in range(n2):
                DW[j][c, y, x] = (DW[j][c, y, x].astype(F32) + SIBR[j, y, x].astype(F32)).astype(BF)
            return carry
        lax.fori_loop(0, n1, one, 0)
        rs_second(j, lambda copy: copy.start())

    def rv2(j):
        @pl.when(c == 0)
        def _():
            for k in range(1, n1):
                wait_bytes(RB.at[j, pl.ds((k - 1) * n2, n2)], rbr.at[j, k])
            for x in range(n2):
                total = DW[j][0, c1, x].astype(F32)
                for k in range(1, n1):
                    total = total + RB[j, (k - 1) * n2 + x].astype(F32)
                DW[j][0, c1, x] = total.astype(BF)

        @pl.when(c == 1)
        def _():
            for k in range(1, n2):
                wait_bytes(RB.at[j, pl.ds((k - 1) * n1, n1)], rbr.at[j, k])
            for y in range(n1):
                total = DW[j][1, y, c2].astype(F32)
                for k in range(1, n2):
                    total = total + RB[j, (k - 1) * n1 + y].astype(F32)
                DW[j][1, y, c2] = total.astype(BF)
        rs_first(j, lambda copy: copy.start())

    def rv3(j):
        def add(n):
            for k in range(1, n):
                wait_bytes(RA.at[j, k - 1], rar.at[j, k])
            total = DW[j][c, c1, c2].astype(F32)
            for k in range(1, n):
                total = total + RA[j, k - 1].astype(F32)
            DW[j][c, c1, c2] = total.astype(BF)

        @pl.when(c == 0)
        def _():
            add(n2)

        @pl.when(c == 1)
        def _():
            add(n1)
        rs_plane(j, lambda copy: copy.start())

    BGRAD[...] = jnp.zeros(BGRAD.shape, F32)
    stats_to_coef(0, 0)
    together(0.6, adain_tile(0, 0))
    edges(0, 0)
    for j in range(CONVS):
        epilogue = block_out(j // 2) if j % 2 else middle_out(j)
        stats_to_coef(j, 1)
        slot(0.0, j)
        together(1.3, conv_tile(j, 0, epilogue), adain_tile(j, 1))
        edges(j % 2, 1)
        if j < CONVS - 1:
            stats_to_coef(j + 1, 0)
            together(1.3, conv_tile(j, 1, epilogue), adain_tile(j + 1, 0))
            edges((j + 1) % 2, 0)
        else:
            together(1.3, conv_tile(j, 1, epilogue), enter_tile(0))
            edges(1, 0)

    together(1.3, grad_input_tile(3, 0), enter_tile(1))
    edges(1, 1)
    send_bias(1, start)
    for j in reversed(range(1, CONVS)):
        if j < CONVS - 1:
            together(1.3, grad_input_tile(j, 0))
        adain_sums(j, 0)
        together(1.3, grad_input_tile(j, 1), adain_back_tile(j, 0))
        edges(1 - j % 2, 0)
        adain_sums(j, 1)
        if j < CONVS - 1:
            rv2(j + 1)
        together(1.8, grad_weight_tile(j), adain_back_tile(j, 1), then=lambda: rv0(j))
        edges(1 - j % 2, 1)
        rv1(j)
        if j < CONVS - 1:
            rv3(j + 1)
        if j < CONVS - 2:
            rv4(j + 2)
        if j == 2:
            send_bias(0, start)
    together(1.8, grad_weight_tile(0), then=lambda: rv0(0))
    rv1(0)
    together(1.3, grad_input_tile(0, 0))
    rv2(1)
    adain_sums(0, 0)
    together(1.3, grad_input_tile(0, 1), adain_back_tile(0, 0))
    adain_sums(0, 1)
    together(0.3, adain_back_tile(0, 1))
    rv3(1)
    rv2(0)
    rv4(2)

    for n in range(2):
        cols = slice(n * HALF, (n + 1) * HALF)
        pg = dot(OHP[0], PAD[1][0][SEG:SEG + FRAMES, cols]) + dot(OHP[1], PAD[1][1][SEG:SEG + FRAMES, cols])

        @pl.when(c == n)
        def _():
            PGX[c] = pg.astype(BF)

        @pl.when(c != n)
        def _():
            TABLE[:, 0:HALF] = pg.astype(BF)
    send_pgx = remote(TABLE.at[:, pl.ds(0, HALF)], PGX.at[c], ss.at[6], rs.at[6], sib)
    send_pgx.start()

    def unpermute(t, carry):
        f0 = pl.multiple_of(t * 256, 256)
        back = PM[:, pl.ds(f0, 256)].T
        for i in range(ITEMS):
            GY[i][pl.ds(f0, 256), :] = dot(back, COT[i]).astype(BF)
        return carry

    wait_bytes(PGX.at[0], rs.at[6])

    def send_pg(d):
        return remote(
            PGX.at[:, pl.ds(pl.multiple_of(d * 16, 16), 16)],
            o_phone.at[:, pl.ds(pl.multiple_of(me * 16, 16), 16)], ss.at[8], rs.at[8], (d, c),
        )
    if remote_phon:
        peers(lambda d: send_pg(d).start())
        mine = pl.ds(pl.multiple_of(me * 16, 16), 16)
        o_phone[:, mine] = PGX[:, mine]
    else:
        o_phone[...] = PGX[...]

    lax.fori_loop(0, FRAMES // 512, unpermute, 0)
    rv3(0)

    peers(lambda d: sent(send_sv(d)))
    style_columns = style_rows().astype(BF).T
    column_kind = lax.broadcasted_iota(jnp.int32, (S, ndp * 16), 1) & 7
    weights = AE[...].astype(BF)
    wait_bytes(GSTR.at[pl.ds(0, ndp - 1)], rs.at[5])
    gall = GSTR[...].reshape(ndp * 16, 128)
    spread = jnp.concatenate(
        [jnp.where(row_kind == b, gall, jnp.zeros_like(gall)) for b in range(8)], axis=1
    )
    back_rows = dot_nt(spread, weights).reshape(ndp, 2, 8, S)
    item_sums = [jnp.sum(back_rows[:, i], axis=1, keepdims=True) for i in range(ITEMS)]
    half8 = lax.broadcasted_iota(jnp.int32, (1, 8, S), 1) < 4
    SGS[...] = jnp.where(half8, item_sums[0], item_sums[1])

    def send_sg(d):
        return remote(SGS.at[d], SGR.at[me], ss.at[9], rs.at[9], (d, c))

    peers(lambda d: send_sg(d).start())
    SGR[me] = SGS[me]
    rv4(1)
    for b in range(8):
        picked = jnp.where(column_kind == b, style_columns, jnp.zeros_like(style_columns))
        da = dot(picked, gall)
        part = None
        for qq in range(S // srows):
            piece = jnp.where(quarter == qq, da[qq * srows:(qq + 1) * srows], 0.0)
            part = piece if part is None else part + piece
        SX[0, 0:srows, b * 128:b * 128 + 128] = part
    summed = jnp.sum(GSTR[...].astype(F32), axis=0)
    SX[0, srows:srows + 8, 0:128] = summed[0:8] + summed[8:16]
    BGR[me] = BGRAD[
        me // (ndp // 2), :, pl.ds(pl.multiple_of(lax.rem(me, ndp // 2) // nb * 128, 128), 128)
    ]
    wait_bytes(BGR.at[pl.ds(0, ndp - 1)], rs.at[7])
    SX[0, srows:srows + 8, 128:256] = jnp.broadcast_to(
        jnp.sum(jnp.sum(BGR[...], axis=0), axis=0, keepdims=True), (8, 128)
    )
    lax.fori_loop(FRAMES // 512, FRAMES // 256, unpermute, 0)
    there, here = (pl.ds(pl.multiple_of(k * 512, 512), 512) for k in (1 - c, c))
    send_frames = [
        remote(GY[i].at[there], o_frames.at[c, i], s_o.at[i], r_o.at[i], sib) for i in range(ITEMS)
    ]
    keep_frames = [
        pltpu.make_async_copy(GY[i].at[here], o_frames.at[c, i], loc.at[5 + i]) for i in range(ITEMS)
    ]
    for copy in send_frames + keep_frames:
        copy.start()
    rv4(0)
    wait_bytes(SGR.at[pl.ds(0, ndp - 1)], rs.at[9])
    SX[0, srows:srows + 8, 256:384] = jnp.sum(SGR[...], axis=0)
    send_sx = remote(SX.at[0], SX.at[1], ss.at[10], rs.at[10], sib)
    send_sx.start()

    for j in range(CONVS):
        @pl.when(c0 == j)
        def _():
            total = DW[j][c, c1, c2].astype(F32)
            for k in range(2):
                wait_bytes(ZR.at[k], zr.at[k])
                total = total + ZR[k].astype(F32)
            GF[c] = total
    send_gf = remote(GF.at[c], GF.at[c], ss.at[11], rs.at[11], sib)
    send_gf.start()

    wait_bytes(SX.at[1], rs.at[10])
    both = SX[0, srows:srows + 8, 0:256] + SX[1, srows:srows + 8, 0:256]
    own_rows = [SX[n, srows:srows + 8, 256:384] for n in range(2)]
    for i in range(ITEMS):
        o_sg[c, i:i + 1, :] = own_rows[0][4 * i:4 * i + 1]
        o_sg[1 - c, i:i + 1, :] = own_rows[1][4 * i:4 * i + 1]

    def pick(block, size, at):
        tall, wide = max(1, size // 128), min(128, size)
        total = None
        for q in range(block.shape[0] * 128 // size):
            r, l = q * size // 128, q * size % 128
            part = jnp.where(at == q, block[r:r + tall, l:l + wide], 0.0)
            total = part if total is None else total + part
        return total

    o_goff[...] = pick(both[:, 0:128], cfg["osize"], lax.rem(me, nq))
    o_gbias[...] = pick(both[0:1, 128:256], cfg["bsize"], lax.rem(me, nb))
    for cb in range(8):
        cols = slice(cb * 128, cb * 128 + 128)
        o_gstyle[pl.ds(cb, srows, stride=8), :] = SX[0, 0:srows, cols] + SX[1, 0:srows, cols]
    wait_bytes(GF.at[c], rs.at[11])
    for cb in range(4):
        o_gconv[pl.ds(cb, shard, stride=4), :] = GF[cb // 2, :, (cb % 2) * 128:(cb % 2) * 128 + 128]

    if remote_phon:
        wait_bytes(o_phone.at[:, pl.ds(0, 16 * (ndp - 1))], rs.at[8])
    for i in range(ITEMS):
        wait_bytes(GY[i].at[pl.ds(0, 512)], r_o.at[i])
        keep_frames[i].wait()

    peers(lambda d: sent(send_par(d)))
    if remote_phon:
        peers(lambda d: sent(send_phon(d)))
        peers(lambda d: sent(send_pg(d)))
    peers(lambda d: sent(send_sg(d)))
    for copy in (send_fph, send_cot, send_pgx, *send_frames, send_sx, send_gf):
        sent(copy)
    for j in range(CONVS):
        send_gst(j, sent)
        if j < LAYERS:
            send_bias(j, sent)
        sent(rs_sib(j))
        rs_second(j, sent)
        rs_first(j, sent)
        rs_plane(j, sent)
        rs_inner(j, sent)
    for p in range(n0):
        @pl.when(c0 == p)
        def _():
            z_sends(EARLY, p, sent)
            z_sends(LATE, p, sent)
            if p == RELAY[0]:
                ev_w(sent)
    for zz in range(n0):
        plane_sends(zz, sent)
        sent(sib_send(zz))


def run_train(cfg, phon, sv, fphone, cnt, cot, wmas, smas, rowin):
    ndp, (n0, n1, n2) = cfg["ndp"], cfg["dims"]
    shard, srows = cfg["shard"], cfg["srows"]
    nmax = max(n1, n2)
    vm = pltpu.VMEM
    dma = pltpu.SemaphoreType.DMA
    any_ = pl.BlockSpec(memory_space=pl.ANY)
    vmem = pl.BlockSpec(memory_space=pltpu.VMEM)
    smem = pl.BlockSpec(memory_space=pltpu.SMEM)
    scratch = [
        vm((2, n0, n1, n2, shard, HALF), BF),
        [[vm((PADDED, D), BF)] * ITEMS] * 2,
        [[vm((D, FRAMES), BF)] * ITEMS] * CONVS,
        [[vm((FRAMES, D), BF)] * ITEMS] * CONVS,
        [vm((FRAMES, D), BF)] * ITEMS,
        [vm((FRAMES, D), BF)] * ITEMS,
        vm((ITEMS, FRAMES, D), BF),
        vm((FRAMES, FRAMES), BF),
        vm((ITEMS, TABLE_ROWS, FRAMES), BF),
        vm((TABLE_ROWS, D), BF),
        vm((ITEMS, FRAMES), jnp.int32),
        vm((shard * 4, 128), F32),
        vm((srows * 8, 128), F32),
        vm((S, 1024), F32),
        vm((ndp, 8, S), F32),
        vm((ndp, 16, 128), BF),
        vm((ndp, 16, 128), BF),
        [[vm((16, D), F32)] * ITEMS] * CONVS,
        [vm((2, 8, D), F32)] * ITEMS,
        vm((LAYERS, 8, D), F32),
        vm((LAYERS, 8, D), F32),
        vm((CONVS, 16, 128), BF),
        vm((ndp, 16, 128), BF),
        vm((ndp, 8, 128), F32),
        vm((ndp, 8, S), F32),
        vm((2, srows + 8, 1024), F32),
        [vm((2, n1, n2, shard, HALF), BF)] * CONVS,
        vm((CONVS, n1, n2, shard, HALF), BF),
        vm((CONVS, max((n1 - 1) * n2, (n2 - 1) * n1), shard, HALF), BF),
        vm((CONVS, nmax - 1, shard, HALF), BF),
        vm((4, shard, HALF), BF),
        vm((2, shard, HALF), F32),
        vm((2, TABLE_ROWS, HALF), BF),
        dma((8,)), dma((12,)), dma((12,)),
        dma((ITEMS,)), dma((ITEMS,)),
        dma((n0,)), dma((n0,)),
        dma((n0, n1 * n2)), dma((n0, n1 * n2)),
        dma((n0,)), dma((n0,)),
        dma((CONVS,)), dma((CONVS,)),
        dma((CONVS, nmax)), dma((CONVS, nmax)),
        dma((CONVS, nmax)), dma((CONVS, nmax)),
        dma((CONVS,)), dma((4,)),
    ]
    return pl.pallas_call(
        functools.partial(train_kernel, cfg),
        out_shape=(
            jax.ShapeDtypeStruct((2, ITEMS, FRAMES // 2, D), BF),
            jax.ShapeDtypeStruct((2, TABLE_ROWS, HALF), BF),
            jax.ShapeDtypeStruct((2, ITEMS, S), F32),
            jax.ShapeDtypeStruct((1, cfg["bsize"]), F32),
            jax.ShapeDtypeStruct((max(1, cfg["osize"] // 128), min(128, cfg["osize"])), F32),
            jax.ShapeDtypeStruct((shard * 4, 128), F32),
            jax.ShapeDtypeStruct((srows * 8, 128), F32),
        ),
        in_specs=[any_, vmem, any_, smem, any_, any_, any_, vmem],
        out_specs=(any_, vmem, vmem, vmem, vmem, vmem, vmem),
        scratch_shapes=scratch,
        compiler_params=pltpu.CompilerParams(
            collective_id=0, has_side_effects=True, vmem_limit_bytes=63 * 2**20
        ),
    )(phon, sv, fphone, cnt, cot, wmas, smas, rowin)


def adamw(master, moment, square, gradient):
    new_moment = MOMENT_DECAY * moment + (1.0 - MOMENT_DECAY) * gradient
    new_square = SQUARE_DECAY * square + (1.0 - SQUARE_DECAY) * gradient * gradient
    first_fix = 1.0 - MOMENT_DECAY**STEP
    second_fix = 1.0 - SQUARE_DECAY**STEP
    updated = master - LEARN_RATE * (
        (new_moment / first_fix) / (jnp.sqrt(new_square / second_fix) + ADAM_EPS) + WEIGHT_DECAY * master
    )
    return (updated, new_moment, new_square, updated.astype(BF))


def finish_kernel(cut, *refs):
    ins, outs = refs[:19], refs[19:]
    for n in range(4):
        def update(n=n):
            results = adamw(*(ref[...] for ref in ins[4 * n:4 * n + 4]))
            for ref, value in zip(outs[4 * n:4 * n + 4], results):
                ref[...] = value
        if n < cut:
            update()
        else:
            pl.when(pl.program_id(0) == 0)(update)
    for n in range(16, 19):
        outs[n][...] = ins[n][...].astype(F32)


def finish(groups, casts, steps):
    def rows(a):
        return pl.BlockSpec((a.shape[0] // steps, a.shape[1]), lambda i: (i, 0))

    def whole(a):
        return pl.BlockSpec(a.shape, lambda i: (0,) * a.ndim)

    cut = 2 if groups[1][0].shape[0] % (16 * steps) == 0 else 1
    specs, shapes, args = [], [], []
    for n, group in enumerate(groups):
        for k, a in enumerate(group):
            args.append(a)
            specs.append(rows(a) if n < cut else whole(a))
            shapes.append(jax.ShapeDtypeStruct(a.shape, BF if k == 3 else F32))
    for a in casts:
        args.append(a)
        specs.append(rows(a) if a.ndim == 2 else whole(a))
        shapes.append(jax.ShapeDtypeStruct(a.shape, F32))
    return pl.pallas_call(
        functools.partial(finish_kernel, cut),
        grid=(steps,),
        in_specs=specs,
        out_specs=tuple(specs),
        out_shape=tuple(shapes),
        compiler_params=pltpu.CompilerParams(vmem_limit_bytes=63 * 2**20),
    )(*args)


def on_device(
    phonemes, style_vector, frame_phone, frame_count, cotangent,
    conv_master, conv_moment, conv_square, bias_master, bias_moment, bias_square,
    style_master, style_moment, style_square, offset_master, offset_moment, offset_square,
):
    ndp = lax.axis_size("dp")
    micros, items, slots, _ = phonemes.shape
    shard = conv_master.shape[0] // D
    srows = style_master.shape[0] // (2 * D)
    bsize, osize = bias_master.shape[0], offset_master.shape[0]
    remote_phon = (ITEMS * slots) % 16 == 0
    cfg = dict(
        ndp=ndp, dims=factor(ndp), slots=slots, shard=shard, srows=srows, remote_phon=remote_phon,
        bsize=bsize, osize=osize,
    )
    me = lax.axis_index("dp")
    c = lax.axis_index("seq")
    if remote_phon:
        phon = phonemes.reshape(micros, items * slots, D)
    else:
        mine = lax.dynamic_index_in_dim(phonemes, c, 0, keepdims=False)
        mine = mine.reshape(ndp, ITEMS * slots, D)
        phon = lax.all_to_all(mine, "dp", split_axis=0, concat_axis=0, tiled=True).reshape(TABLE_ROWS, D)
    spread, wide = 128 // bsize, 1024 // osize
    offset_rows = jnp.where(jnp.arange(1024) // osize == me % wide, jnp.tile(offset_master, wide), 0.0)
    bias_rows = jnp.where(jnp.arange(128) // bsize == me % spread, jnp.tile(bias_master, spread), 0.0)
    rowin = jnp.concatenate(
        [offset_rows.reshape(8, 128), jnp.broadcast_to(bias_rows.reshape(1, 128), (8, 128))], axis=0
    )
    frames, phone, style_grads, gbias, goff, gconv, gstyle = run_train(
        cfg, phon, style_vector, frame_phone, frame_count, cotangent,
        conv_master.reshape(shard * 4, 128), style_master.reshape(srows * 8, 128), rowin,
    )
    if not remote_phon:
        phone = lax.all_to_all(
            phone.reshape(micros, ndp, ITEMS * slots, HALF), "dp", split_axis=1, concat_axis=1, tiled=True
        )
    groups = [
        [a.reshape(g.shape) for a in arrays] + [g]
        for arrays, g in (
            ((conv_master, conv_moment, conv_square), gconv),
            ((style_master, style_moment, style_square), gstyle),
            ((bias_master, bias_moment, bias_square), gbias),
            ((offset_master, offset_moment, offset_square), goff),
        )
    ]
    out = finish(
        groups,
        (frames.reshape(micros * ITEMS * FRAMES // 2, D), phone.reshape(micros * TABLE_ROWS, HALF), style_grads), 4,
    )
    flat = [a.reshape(-1) for a in out[:16]]
    return (
        out[16].reshape(frames.shape), out[17].reshape(micros, items, slots, HALF), out[18],
        *flat[0:4], *flat[8:12], *flat[4:8], *flat[12:16],
    )


def solution(mesh):
    return jax.shard_map(
        on_device,
        mesh=mesh,
        in_specs=(
            P(None, None, "dp", None), P(None, "dp", None), P(None, "dp", "seq"), P(None, "dp"),
            P(None, "dp", "seq", None), *[P("dp")] * 12,
        ),
        out_specs=(
            P(None, "dp", "seq", None), P(None, None, "dp", "seq"), P(None, "dp", None), *[P("dp")] * 16,
        ),
        check_vma=False,
    )
```

```python
import functools

import jax
import jax.numpy as jnp
from jax import lax
from jax.experimental import pallas as pl
from jax.experimental.pallas import tpu as pltpu
from jax.sharding import PartitionSpec as P

D = 512
S = 128
KERN = 3
LAYERS = 2
CONVS = 2 * LAYERS
PH = 128
STEP = 10
FRAMES = 1024
SEG = 16
RUN = FRAMES // SEG
HALF = D // 2
ITEMS = 2
PADDED = FRAMES + 2 * SEG
TABLE_ROWS = ITEMS * PH

NORM_EPS = 1e-05
HALF_ROOT = 0.7071067811865476
MOMENT_DECAY = 0.9
SQUARE_DECAY = 0.999
LEARN_RATE = 0.05
WEIGHT_DECAY = 0.01
ADAM_EPS = 1e-08

BF = jnp.bfloat16
F32 = jnp.float32
MESH = pl.DeviceIdType.MESH

C_SCALE, C_SHIFT, C_INV, C_MI, C_ONE, C_2, C_3 = range(7)


PLAN = (
    (
        (7.0, "f", 0), (15.0, "z", 1), (15.0, "f", 1), (16.1, "b", 0), (23.0, "z", 2), (23.0, "f", 2), (25.0, "b", 1),
        (31.5, "z", 3), (31.5, "f", 3), (33.5, "b", 2), (41.5, "b", 3),
    ),
    (
        (7.0, "e", 1), (7.0, "g", 1), (10.5, "z", 0), (10.5, "f", 0), (19.0, "h", 1), (21.0, "b", 0), (23.0, "z", 2),
        (23.0, "f", 2), (25.0, "b", 1), (31.5, "z", 3), (31.5, "f", 3), (33.5, "b", 2), (42.0, "b", 3),
    ),
    (
        (6.0, "w", 0), (6.0, "f", 0), (7.0, "e", 2), (7.0, "v", 2), (14.5, "g", 2), (16.5, "b", 0), (18.5, "z", 1),
        (18.5, "f", 1), (27.0, "h", 2), (28.0, "b", 1), (30.5, "z", 3), (30.5, "f", 3), (32.5, "b", 2), (40.5, "b", 3),
    ),
    (
        (7.0, "e", 3), (7.0, "g", 3), (10.6, "z", 0), (10.6, "f", 0), (20.0, "b", 0), (20.4, "z", 1), (20.4, "f", 1),
        (28.5, "z", 2), (28.5, "f", 2), (30.5, "b", 1), (37.0, "h", 3), (39.0, "b", 2), (43.0, "b", 3),
    ),
)
EARLY = ((2, 1), (0, 2, 3), (1, 0), (2, 1, 0))
LATE = ((), (), (3,), ())
RELAY = (2, 3)


def factor(ndp):
    return {16: (4, 2, 2), 128: (4, 8, 4)}.get(ndp, (4, ndp // 4, 1))


def dot(a, b):
    return jnp.dot(a, b, preferred_element_type=F32)


def dot_nt(a, b):
    return lax.dot_general(a, b, (((1,), (1,)), ((), ())), preferred_element_type=F32)


def dot_tn(a, b):
    return lax.dot_general(a, b, (((0,), (0,)), ((), ())), preferred_element_type=F32)


def fold(tile):
    rows, cols = tile.shape
    return jnp.sum(tile.reshape(rows // 8, 8, cols), axis=0)


def valid_rows(start, rows, count, value):
    i = lax.broadcasted_iota(jnp.int32, (rows, 128), 0)
    frame = (i & (SEG - 1)) * RUN + (i >> 4) + start // SEG
    return jnp.where(frame < count, jnp.float32(value), jnp.float32(0.0))


def train_kernel(cfg, *refs):
    ndp, (n0, n1, n2), slots = cfg["ndp"], cfg["dims"], cfg["slots"]
    shard, srows, remote_phon = cfg["shard"], cfg["srows"], cfg["remote_phon"]
    comm = cfg.get("comm", True)
    skip = cfg.get("skip", ())
    nq = ndp // CONVS
    nb = ndp // 8
    (
        phon, sv, fphone, cnt, cot, wmas, smas, bias_in, offset_in,
        o_frames, o_phone, o_sg, o_gbias, o_goff, o_gconv, o_gstyle,
        W, PAD, AT, ST, G, GY, COT, PM, OHP, TABLE, FPH, WM, SM, AE,
        SVR, PARS, PARR, COEF, STAT, BIAS, BGRAD, GSTS, GSTR, BGR, SGR, SX, ROWS,
        DW, SIBR, RB, RA, ZR, GF, PGX,
        loc, ss, rs, s_o, r_o, s_z, r_z, s_f, r_f, s_b, r_b,
        rss, rsr, rbs, rbr, ras, rar, zs, zr,
    ) = refs
    SGS = SVR
    me = lax.axis_index("dp")
    c = lax.axis_index("seq")
    c0, c1, c2 = me // (n1 * n2), (me // n2) % n1, me % n2
    sib = (me, 1 - c)

    def remote(src, dst, send, recv, target):
        return pltpu.make_async_remote_copy(
            src_ref=src, dst_ref=dst, send_sem=send, recv_sem=recv, device_id=target, device_id_type=MESH
        )

    def wait_bytes(ref, sem):
        pltpu.make_async_copy(ref, ref, sem).wait()

    def sent(copy):
        copy.wait_send()

    def peers(fn):
        def one(d, carry):
            fn(lax.rem(me + d, ndp))
            return carry
        lax.fori_loop(1, ndp, one, 0)

    barrier = pltpu.get_barrier_semaphore()
    peers(lambda d: pl.semaphore_signal(barrier, inc=1, device_id=(d, c), device_id_type=MESH))
    pl.semaphore_signal(barrier, inc=1, device_id=sib, device_id_type=MESH)

    own_in = [
        pltpu.make_async_copy(wmas, WM, loc.at[0]),
        pltpu.make_async_copy(smas, SM, loc.at[1]),
        pltpu.make_async_copy(cot.at[c], COT.at[:, pl.ds(pl.multiple_of(c * HALF * 2, 512), 512)], loc.at[2]),
        pltpu.make_async_copy(fphone.at[c], FPH.at[:, pl.ds(pl.multiple_of(c * HALF * 2, 512), 512)], loc.at[3]),
    ]
    if remote_phon:
        own_in.append(
            pltpu.make_async_copy(
                phon.at[c, pl.ds(pl.multiple_of(me * 16, 16), 16)],
                TABLE.at[pl.ds(pl.multiple_of(me * 16, 16), 16)], loc.at[4],
            )
        )
    else:
        own_in.append(pltpu.make_async_copy(phon, TABLE, loc.at[4]))
    for copy in own_in:
        copy.start()

    own_in[0].wait()
    for cb in range(4):
        W[cb // 2, c0, c1, c2, :, (cb % 2) * 128:(cb % 2) * 128 + 128] = WM[
            pl.ds(cb, shard, stride=4), :
        ].astype(BF)
    own_in[1].wait()
    quarter = lax.rem(me, S // srows)
    for cb in range(8):
        block = SM[pl.ds(cb, srows, stride=8), :].astype(BF).astype(F32)
        for qq in range(S // srows):
            AE[qq * srows:(qq + 1) * srows, cb * 128:cb * 128 + 128] = jnp.where(quarter == qq, block, 0.0)
    ROWS[...] = jnp.zeros(ROWS.shape, F32)
    osize, bsize = cfg["osize"], cfg["bsize"]
    for q in range(nq):
        r, l = q * osize // 128, q * osize % 128
        ROWS[r:r + max(1, osize // 128), l:l + min(128, osize)] = jnp.where(
            lax.rem(me, nq) == q, offset_in[...].astype(BF).astype(F32), 0.0
        )
    for q in range(nb):
        ROWS[8:9, q * bsize:(q + 1) * bsize] = jnp.where(
            lax.rem(me, nb) == q, bias_in[...].astype(BF).astype(F32), 0.0
        )
    bias_row = ROWS[8:9, :]
    vec = sv[c].astype(F32)
    kind8 = lax.broadcasted_iota(jnp.int32, (8, S), 0)
    SVR[me] = jnp.where(kind8 == 0, vec[0:1], jnp.where(kind8 == 1, vec[1:2], bias_row))

    def make_perm(t, carry):
        r0 = pl.multiple_of(t * 128, 128)
        row = lax.broadcasted_iota(jnp.int32, (128, FRAMES), 0)
        col = lax.broadcasted_iota(jnp.int32, (128, FRAMES), 1)
        frame = (row & (SEG - 1)) * RUN + (row >> 4) + r0 // SEG
        PM[pl.ds(r0, 128), :] = jnp.where(col == frame, 1.0, 0.0).astype(BF)
        return carry

    lax.fori_loop(0, FRAMES // 128, make_perm, 0)

    pl.semaphore_wait(barrier, ndp)

    def send_sv(d):
        return remote(SVR.at[me], SVR.at[me], ss.at[0], rs.at[0], (d, c))

    def send_phon(d):
        return remote(
            phon.at[c, pl.ds(pl.multiple_of(d * 16, 16), 16)],
            TABLE.at[pl.ds(pl.multiple_of(me * 16, 16), 16)], ss.at[1], rs.at[1], (d, c),
        )

    send_fph = remote(
        fphone.at[1 - c], FPH.at[:, pl.ds(pl.multiple_of(c * 512, 512), 512)], ss.at[2], rs.at[2], sib
    )
    send_cot = remote(
        cot.at[1 - c], COT.at[:, pl.ds(pl.multiple_of(c * 512, 512), 512)], ss.at[3], rs.at[3], sib
    )
    def z_send(zz, to, k, fn):
        piece = W.at[c, zz, c1, c2]
        fn(remote(piece, piece, s_z.at[k], r_z.at[zz], ((to * n1 + c1) * n2 + c2, c)))

    def z_sends(sends, p, fn):
        for to in sends[p]:
            z_send(p, to, to, fn)

    def z_wait(zz):
        wait_bytes(W.at[c, zz, c1, c2], r_z.at[zz])

    def ev_w(fn=None):
        if fn is None:
            z_wait(0)
        z_send(0, RELAY[1], RELAY[0], fn or start)

    near = [k for k in range(1, n1 * n2) if k // n2 == 0 or k % n2 == 0]
    far = [k for k in range(1, n1 * n2) if k not in near]

    def plane_sends(zz, ks, fn):
        piece = W.at[c, zz, c1, c2]
        for k in ks:
            y, x = lax.rem(c1 + k // n2, n1), lax.rem(c2 + k % n2, n2)
            fn(remote(piece, piece, s_f.at[zz, k], r_f.at[zz, k], ((c0 * n1 + y) * n2 + x, c)))

    def plane_wait(zz):
        for k in range(1, n1 * n2):
            wait_bytes(W.at[c, zz, c1, c2], r_f.at[zz, k])

    def sib_send(zz):
        return remote(W.at[c, zz], W.at[c, zz], s_b.at[zz], r_b.at[zz], sib)

    def start(copy):
        copy.start()

    def ev_b(zz):
        plane_wait(zz)
        sib_send(zz).start()

    def plane_events(p):
        events = []
        for at, kind, zz in PLAN[p]:
            fn = {
                "e": lambda: z_sends(EARLY, p, start),
                "v": lambda: z_sends(LATE, p, start),
                "z": lambda zz=zz: z_wait(zz),
                "w": ev_w,
                "f": lambda zz=zz: plane_sends(zz, near + far, start),
                "g": lambda zz=zz: plane_sends(zz, near, start),
                "h": lambda zz=zz: plane_sends(zz, far, start),
                "b": lambda zz=zz: ev_b(zz),
            }[kind]
            events.append((at, fn))
            if kind == "b":
                ready[p][zz] = at + 0.1
        return events

    ready = {p: {} for p in range(n0)}
    plan = {p: plane_events(p) for p in range(n0)}
    clock = {p: 0.0 for p in range(n0)}

    def take(passed, until=None):
        dues = {}
        for p in range(n0):
            clock[p] += passed
            if until is not None:
                clock[p] = max(clock[p], ready[p][until])
            dues[p] = [e for e in plan[p] if e[0] <= clock[p]]
            plan[p] = plan[p][len(dues[p]):]
            if until is not None:
                clock[p] += 2.4
        return dues

    def run_due(dues, when=True):
        for p, due in dues.items():
            if due:
                @pl.when(jnp.logical_and(c0 == p, when))
                def _(due=due):
                    for _, fn in due:
                        fn()

    def slot(passed, until=None):
        run_due(take(passed, until))
        if until is not None:
            wait_bytes(W.at[c, until], r_b.at[until])

    peers(lambda d: send_sv(d).start())

    @pl.when(c0 == 0)
    def _():
        z_sends(EARLY, 0, start)
    if remote_phon:
        peers(lambda d: send_phon(d).start())
    send_fph.start()
    send_cot.start()

    slot(3.0)
    own_in[3].wait()
    wait_bytes(FPH.at[:, pl.ds(0, 512)], rs.at[2])
    def one_hot(i):
        phone = FPH[i:i + 1, :]
        if slots & (slots - 1) == 0:
            shift = slots.bit_length() - 1
            place = ((phone >> shift) << (shift + 1)) + i * slots + (phone & (slots - 1))
        else:
            place = (phone // slots) * (2 * slots) + i * slots + phone % slots
        spot = lax.broadcasted_iota(jnp.int32, (TABLE_ROWS, FRAMES), 0)
        onehot = jnp.where(spot == place, 1.0, 0.0).astype(BF)
        for t in range(4):
            OHP[i, :, t * 256:t * 256 + 256] = dot_nt(onehot, PM[t * 256:t * 256 + 256, :]).astype(BF)

    one_hot(0)
    slot(1.5)

    one_hot(1)
    slot(1.5)

    row_kind = lax.broadcasted_iota(jnp.int32, (ndp * 16, 1), 0) & 7

    def style_rows():
        got = SVR[...]
        pair = [jnp.broadcast_to(got[:, i:i + 1, :], (ndp, 8, S)) for i in range(ITEMS)]
        return jnp.concatenate(pair, axis=1).reshape(ndp * 16, S)

    wait_bytes(SVR.at[pl.ds(0, ndp - 1)], rs.at[0])
    svall = style_rows()
    acc = jnp.zeros((ndp * 16, 128), F32)
    for b in range(8):
        acc = acc + dot(
            jnp.where(row_kind == b, svall, 0.0).astype(BF), AE[:, b * 128:b * 128 + 128].astype(BF)
        )
    offs = ROWS[0:8, :]
    acc = acc.reshape(ndp, 16, 128) + jnp.concatenate([offs, offs], axis=0).reshape(1, 16, 128)
    PARS[...] = acc.astype(BF)

    def send_par(d):
        return remote(PARS.at[d], PARR.at[me], ss.at[4], rs.at[4], (d, c))

    peers(lambda d: send_par(d).start())
    PARR[me] = PARS[me]
    slot(2.0)

    own_in[2].wait()
    wait_bytes(COT.at[:, pl.ds(0, 512)], rs.at[3])
    for i in range(ITEMS):
        count = cnt[c, i]

        def permute(t, carry):
            r0 = pl.multiple_of(t * 256, 256)
            y = dot(PM[pl.ds(r0, 256), :], COT[i])
            mask = valid_rows(r0, 256, count, 1.0)
            G[i][pl.ds(r0, 256), :] = (y * jnp.concatenate([mask] * 4, axis=1)).astype(BF)
            return carry

        lax.fori_loop(0, 4, permute, 0)
        slot(1.3)

    for i in range(ITEMS):
        STAT[i][...] = jnp.zeros(STAT[i].shape, F32)
    own_in[4].wait()
    if remote_phon:
        wait_bytes(TABLE.at[pl.ds(0, 16 * (ndp - 1))], rs.at[1])
    for i in range(ITEMS):
        count = cnt[c, i]
        for t in range(4):
            x = dot(OHP[i, :, t * 256:t * 256 + 256].T, TABLE[...])
            mask = valid_rows(t * 256, 256, count, 1.0)
            x = x * jnp.concatenate([mask] * 4, axis=1)
            ST[0][i][t * 256:t * 256 + 256, :] = x.astype(BF)
            STAT[i][0] += fold(x)
            STAT[i][1] += fold(x * x)
        slot(3.4 if i == 0 else 1.0)

    wait_bytes(PARR.at[pl.ds(0, ndp - 1)], rs.at[4])
    for j in range(CONVS):
        total = jnp.sum(PARR[j * nq:(j + 1) * nq].astype(F32), axis=0)
        for i in range(ITEMS):
            for b in range(8):
                COEF[j][i][8 + b // 4:9 + b // 4, (b % 4) * 128:(b % 4) * 128 + 128] = total[
                    8 * i + b:8 * i + b + 1, :
                ]
    for l in range(LAYERS):
        for qb in range(4):
            first = l * (ndp // 2) + qb * nb
            BIAS[l, :, qb * 128:qb * 128 + 128] = jnp.broadcast_to(
                jnp.sum(SVR[first:first + nb], axis=0)[2:3, :], (8, 128)
            )
    slot(0.5)

    def stats_to_coef(j, i):
        n = cnt[c, i].astype(F32)
        sums = jnp.sum(STAT[i][0], axis=0, keepdims=True)
        squares = jnp.sum(STAT[i][1], axis=0, keepdims=True)
        STAT[i][...] = jnp.zeros(STAT[i].shape, F32)
        mean = sums / n
        var = jnp.maximum(squares / n - mean * mean, 0.0)
        inv = lax.rsqrt(var + NORM_EPS)
        one = (1.0 + COEF[j][i][8:9]) * inv
        shift = COEF[j][i][9:10] - mean * one

        def put(k, v):
            COEF[j][i][k:k + 1] = v
        put(C_SCALE, 0.5 * one)
        put(C_SHIFT, 0.5 * shift)
        put(C_INV, inv)
        put(C_MI, mean * inv)
        put(C_ONE, one)

    def coef(j, i, k, cols):
        return COEF[j][i][k:k + 1, cols]

    def edges(pad, i):
        row = lax.broadcasted_iota(jnp.int32, (SEG, D), 0)
        last = PAD[pad][i][FRAMES:FRAMES + SEG, :].astype(F32)
        head = jnp.where(row == 0, 0.0, pltpu.roll(last, 1, 0))
        PAD[pad][i][0:SEG, :] = head.astype(BF)
        first = PAD[pad][i][SEG:2 * SEG, :].astype(F32)
        tail = jnp.where(row == SEG - 1, 0.0, pltpu.roll(first, SEG - 1, 0))
        PAD[pad][i][FRAMES + SEG:PADDED, :] = tail.astype(BF)

    TR = 128
    M = 512
    MG = 256

    def adain_tile(j, i):
        count = cnt[c, i]

        def run(r1):
            for rb in range(0, M, TR):
                r0 = pl.multiple_of(r1 + rb, TR)
                mask = valid_rows(r0, TR, count, 1.0)
                for cb in range(4):
                    cols = slice(cb * 128, cb * 128 + 128)
                    x = ST[j][i][pl.ds(r0, TR), cols].astype(F32)
                    v = x * coef(j, i, C_SCALE, cols) + coef(j, i, C_SHIFT, cols)
                    a = ((v + v * jnp.tanh(v)) * mask).astype(BF)
                    PAD[j % 2][i][pl.ds(r0 + SEG, TR), cols] = a
                    AT[j][i][cols, pl.ds(r0, TR)] = a.T
        return run

    def conv_tile(j, i, epilogue):
        def run(r0):
            for h in range(2):
                acc = None
                weights = W[h, j].reshape(KERN * D, HALF)
                for k in range(KERN):
                    part = dot(PAD[j % 2][i][pl.ds(r0 + SEG * k, M), :], weights[k * D:(k + 1) * D])
                    acc = part if acc is None else acc + part
                epilogue(i, r0, h, acc)
        return run

    def together(passed, *parts, then=None):
        steps = FRAMES // M
        dues = [take(passed) for _ in range(steps - 1)]

        def step(t, carry):
            for part in parts:
                part(pl.multiple_of(t * M, M))
            for k, due in enumerate(dues):
                run_due(due, t == k)
            if then is not None:
                pl.when(t == 0)(then)
            return carry

        lax.fori_loop(0, steps, step, 0)
        slot(passed)

    def middle_out(j):
        def epilogue(i, r0, h, acc):
            count = cnt[c, i]
            masks = [valid_rows(r0 + rb, 128, count, 1.0) for rb in range(0, M, 128)]
            for cb in range(2):
                cols = slice(h * HALF + cb * 128, h * HALF + cb * 128 + 128)
                sums = [0.0, 0.0]
                for rb in range(0, M, 128):
                    p = acc[rb:rb + 128, cb * 128:cb * 128 + 128]
                    ST[j + 1][i][pl.ds(r0 + rb, 128), cols] = p.astype(BF)
                    kept = p * masks[rb // 128]
                    sums = [sums[0] + fold(kept), sums[1] + fold(kept * p)]
                for n in range(2):
                    STAT[i][n, :, cols] += sums[n]
        return epilogue

    def block_out(l):
        def epilogue(i, r0, h, acc):
            count = cnt[c, i]
            masks = [valid_rows(r0 + rb, 128, count, HALF_ROOT) for rb in range(0, M, 128)]
            for cb in range(2):
                cols = slice(h * HALF + cb * 128, h * HALF + cb * 128 + 128)
                sums = [0.0, 0.0]
                for rb in range(0, M, 128):
                    q = acc[rb:rb + 128, cb * 128:cb * 128 + 128] + BIAS[l, 0:1, cols]
                    x = (ST[2 * l][i][pl.ds(r0 + rb, 128), cols].astype(F32) + q) * masks[rb // 128]
                    if l < LAYERS - 1:
                        ST[2 * l + 2][i][pl.ds(r0 + rb, 128), cols] = x.astype(BF)
                        sums = [sums[0] + fold(x), sums[1] + fold(x * x)]
                    else:
                        COT[i, pl.ds(r0 + rb, 128), cols] = x.astype(BF)
                if l < LAYERS - 1:
                    for n in range(2):
                        STAT[i][n, :, cols] += sums[n]
        return epilogue

    def enter_tile(i):
        def run(r1):
            for rb in range(0, M, TR):
                r0 = pl.multiple_of(r1 + rb, TR)
                g = (G[i][pl.ds(r0, TR), :].astype(F32) * HALF_ROOT).astype(BF)
                PAD[1][i][pl.ds(r0 + SEG, TR), :] = g
                BGRAD[LAYERS - 1] += fold(g.astype(F32))
        return run

    def grad_weight_tile(j):
        def run(r1):
            h = jnp.where(r1 == 0, 1 - c, c)
            cols = pl.ds(pl.multiple_of(h * HALF, HALF), HALF)
            for r0 in range(0, D, 256):
                for k in range(KERN):
                    acc = None
                    for i in range(ITEMS):
                        part = dot(
                            AT[j][i][r0:r0 + 256, :], PAD[j % 2][i][(2 - k) * SEG:(2 - k) * SEG + FRAMES, cols]
                        )
                        acc = part if acc is None else acc + part
                    DWF[j].at[h][k * D + r0:k * D + r0 + 256, :] = acc.astype(BF)
        return run

    DWF = [DW[j].reshape(2, KERN * D, HALF) for j in range(CONVS)]

    def grad_input_tile(j, i):
        count = cnt[c, i]

        def run(r1):
            for r0, n in ((pl.multiple_of(r1 + r, MG), n) for r in range(0, M, MG) for n in range(2)):
                acc = None
                for k in range(KERN):
                    for h in range(2):
                        weights = W[h, j].reshape(KERN * D, HALF)
                        part = dot_nt(
                            PAD[j % 2][i][pl.ds(r0 + SEG * (2 - k), MG), h * HALF:(h + 1) * HALF],
                            weights[k * D + n * HALF:k * D + (n + 1) * HALF],
                        )
                        acc = part if acc is None else acc + part
                masks = [valid_rows(r0 + rb, 128, count, 0.5) for rb in range(0, MG, 128)]
                for cb in range(2):
                    cols = slice(n * HALF + cb * 128, n * HALF + cb * 128 + 128)
                    sums = [0.0, 0.0]
                    for rb in range(0, MG, 128):
                        mask = masks[rb // 128]
                        x = ST[j][i][pl.ds(r0 + rb, 128), cols].astype(F32)
                        v = x * coef(j, i, C_SCALE, cols) + coef(j, i, C_SHIFT, cols)
                        th = jnp.tanh(v)
                        u = acc[rb:rb + 128, cb * 128:cb * 128 + 128] * mask
                        gy = (u + u * th) * (1.0 + v * (1.0 - th))
                        xhat = x * coef(j, i, C_INV, cols) - coef(j, i, C_MI, cols)
                        sums = [sums[0] + fold(gy), sums[1] + fold(gy * xhat)]
                        GY[i][pl.ds(r0 + rb, 128), cols] = gy.astype(BF)
                    for k in range(2):
                        STAT[i][k, :, cols] += sums[k]
        return run

    def send_gst(j, fn):
        def one(q, carry):
            d = j * nq + q

            @pl.when(d != me)
            def _():
                fn(remote(GSTS.at[j], GSTR.at[me], ss.at[5], rs.at[5], (d, c)))
            return carry
        lax.fori_loop(0, nq, one, 0)

    def send_bias(l, fn):
        def one(q, carry):
            d = l * (ndp // 2) + q
            part = BGRAD.at[l, :, pl.ds(pl.multiple_of(q // nb * 128, 128), 128)]

            @pl.when(d != me)
            def _():
                fn(remote(part, BGR.at[me], ss.at[7], rs.at[7], (d, c)))
            return carry
        lax.fori_loop(0, ndp // 2, one, 0)

    def adain_sums(j, i):
        n = cnt[c, i].astype(F32)
        gt = jnp.sum(STAT[i][0], axis=0, keepdims=True)
        gs = jnp.sum(STAT[i][1], axis=0, keepdims=True)
        STAT[i][...] = jnp.zeros(STAT[i].shape, F32)
        one, inv, mi = (COEF[j][i][k:k + 1] for k in (C_ONE, C_INV, C_MI))
        each = one / n
        COEF[j][i][C_2:C_2 + 1] = each * (gt - mi * gs)
        COEF[j][i][C_3:C_3 + 1] = each * inv * gs
        rows = [x[:, b * 128:b * 128 + 128] for x in (gs, gt) for b in range(4)]
        GSTS[j, 8 * i:8 * i + 8, :] = jnp.concatenate(rows, axis=0).astype(BF)
        if i == ITEMS - 1:
            @pl.when(me // nq == j)
            def _():
                GSTR[me] = GSTS[j]
            send_gst(j, start)

    def adain_back_tile(j, i):
        count = cnt[c, i]

        def run(r1):
            for rb in range(0, M, TR):
                r0 = pl.multiple_of(r1 + rb, TR)
                mask = valid_rows(r0, TR, count, 1.0)
                for cb in range(4):
                    cols = slice(cb * 128, cb * 128 + 128)
                    gy = GY[i][pl.ds(r0, TR), cols].astype(F32)
                    x = ST[j][i][pl.ds(r0, TR), cols].astype(F32)
                    g = gy * coef(j, i, C_ONE, cols) - x * coef(j, i, C_3, cols) - coef(j, i, C_2, cols)
                    g = g * mask
                    if j % 2 == 0:
                        g = G[i][pl.ds(r0, TR), cols].astype(F32) * HALF_ROOT + g
                        if j > 0:
                            G[i][pl.ds(r0, TR), cols] = g.astype(BF)
                            g = g * HALF_ROOT
                            BGRAD[j // 2 - 1, :, cols] += fold(g.astype(BF).astype(F32))
                    PAD[1 - j % 2][i][pl.ds(r0 + SEG, TR), cols] = g.astype(BF)
        return run

    def rs_sib(j):
        return remote(DW[j].at[1 - c], SIBR.at[j], rss.at[j], rsr.at[j], sib)

    def rs_second(j, fn):
        @pl.when(c == 0)
        def _():
            for k in range(1, n1):
                to = lax.rem(c1 + k, n1)
                fn(remote(DW[j].at[0, to], RB.at[j, pl.ds((k - 1) * n2, n2)], rbs.at[j, k], rbr.at[j, k],
                          ((c0 * n1 + to) * n2 + c2, c)))

        @pl.when(c == 1)
        def _():
            for k in range(1, n2):
                to = lax.rem(c2 + k, n2)
                fn(remote(DW[j].at[1, :, to], RB.at[j, pl.ds((k - 1) * n1, n1)], rbs.at[j, k], rbr.at[j, k],
                          ((c0 * n1 + c1) * n2 + to, c)))

    def rs_first(j, fn):
        @pl.when(c == 0)
        def _():
            for k in range(1, n2):
                to = lax.rem(c2 + k, n2)
                fn(remote(DW[j].at[0, c1, to], RA.at[j, k - 1], ras.at[j, k], rar.at[j, k],
                          ((c0 * n1 + c1) * n2 + to, c)))

        @pl.when(c == 1)
        def _():
            for k in range(1, n1):
                to = lax.rem(c1 + k, n1)
                fn(remote(DW[j].at[1, to, c2], RA.at[j, k - 1], ras.at[j, k], rar.at[j, k],
                          ((c0 * n1 + to) * n2 + c2, c)))

    def rs_plane(j, fn):
        outer, inner = ((3, 2) if j < 2 else (0, 1))
        for p, to, k in ((j ^ 1, j, 0), (outer, inner, 2 + j % 2)):
            @pl.when(c0 == p)
            def _(to=to, k=k):
                fn(remote(DW[j].at[c, c1, c2], ZR.at[k], zs.at[j], zr.at[k], ((to * n1 + c1) * n2 + c2, c)))

    def rs_inner(j, fn):
        @pl.when(c0 == (2 if j < 2 else 1))
        def _():
            fn(remote(DW[j].at[c, c1, c2], ZR.at[1], zs.at[j], zr.at[1], ((j * n1 + c1) * n2 + c2, c)))

    def rv4(j):
        @pl.when(c0 == (2 if j < 2 else 1))
        def _():
            k = 2 + j % 2
            wait_bytes(ZR.at[k], zr.at[k])
            DW[j][c, c1, c2] = (DW[j][c, c1, c2].astype(F32) + ZR[k].astype(F32)).astype(BF)
        rs_inner(j, start)

    def rv0(j):
        rs_sib(j).start()

    def rv1(j):
        wait_bytes(SIBR.at[j], rsr.at[j])

        def one(y, carry):
            for x in range(n2):
                DW[j][c, y, x] = (DW[j][c, y, x].astype(F32) + SIBR[j, y, x].astype(F32)).astype(BF)
            return carry
        lax.fori_loop(0, n1, one, 0)
        rs_second(j, lambda copy: copy.start())

    def rv2(j):
        @pl.when(c == 0)
        def _():
            for k in range(1, n1):
                wait_bytes(RB.at[j, pl.ds((k - 1) * n2, n2)], rbr.at[j, k])
            for x in range(n2):
                total = DW[j][0, c1, x].astype(F32)
                for k in range(1, n1):
                    total = total + RB[j, (k - 1) * n2 + x].astype(F32)
                DW[j][0, c1, x] = total.astype(BF)

        @pl.when(c == 1)
        def _():
            for k in range(1, n2):
                wait_bytes(RB.at[j, pl.ds((k - 1) * n1, n1)], rbr.at[j, k])
            for y in range(n1):
                total = DW[j][1, y, c2].astype(F32)
                for k in range(1, n2):
                    total = total + RB[j, (k - 1) * n1 + y].astype(F32)
                DW[j][1, y, c2] = total.astype(BF)
        rs_first(j, lambda copy: copy.start())

    def rv3(j):
        def add(n):
            for k in range(1, n):
                wait_bytes(RA.at[j, k - 1], rar.at[j, k])
            total = DW[j][c, c1, c2].astype(F32)
            for k in range(1, n):
                total = total + RA[j, k - 1].astype(F32)
            DW[j][c, c1, c2] = total.astype(BF)

        @pl.when(c == 0)
        def _():
            add(n2)

        @pl.when(c == 1)
        def _():
            add(n1)
        rs_plane(j, lambda copy: copy.start())

    BGRAD[...] = jnp.zeros(BGRAD.shape, F32)
    stats_to_coef(0, 0)
    together(0.6, adain_tile(0, 0))
    edges(0, 0)
    for j in range(CONVS):
        epilogue = block_out(j // 2) if j % 2 else middle_out(j)
        stats_to_coef(j, 1)
        slot(0.0, j)
        together(1.3, conv_tile(j, 0, epilogue), adain_tile(j, 1))
        edges(j % 2, 1)
        if j < CONVS - 1:
            stats_to_coef(j + 1, 0)
            together(1.3, conv_tile(j, 1, epilogue), adain_tile(j + 1, 0))
            edges((j + 1) % 2, 0)
        else:
            together(1.3, conv_tile(j, 1, epilogue), enter_tile(0))
            edges(1, 0)

    together(1.3, grad_input_tile(3, 0), enter_tile(1))
    edges(1, 1)
    send_bias(1, start)
    for j in reversed(range(1, CONVS)):
        if j < CONVS - 1:
            together(1.3, grad_input_tile(j, 0))
        adain_sums(j, 0)
        together(1.3, grad_input_tile(j, 1), adain_back_tile(j, 0))
        edges(1 - j % 2, 0)
        adain_sums(j, 1)
        if j < CONVS - 1:
            rv2(j + 1)
        together(1.8, grad_weight_tile(j), adain_back_tile(j, 1), then=lambda: rv0(j))
        edges(1 - j % 2, 1)
        rv1(j)
        if j < CONVS - 1:
            rv3(j + 1)
        if j < CONVS - 2:
            rv4(j + 2)
        if j == 2:
            send_bias(0, start)
    together(1.8, grad_weight_tile(0), then=lambda: rv0(0))
    rv1(0)
    together(1.3, grad_input_tile(0, 0))
    rv2(1)
    adain_sums(0, 0)
    together(1.3, grad_input_tile(0, 1), adain_back_tile(0, 0))
    adain_sums(0, 1)
    together(0.3, adain_back_tile(0, 1))
    rv3(1)
    rv2(0)
    rv4(2)

    for n in range(2):
        cols = slice(n * HALF, (n + 1) * HALF)
        pg = dot(OHP[0], PAD[1][0][SEG:SEG + FRAMES, cols]) + dot(OHP[1], PAD[1][1][SEG:SEG + FRAMES, cols])

        @pl.when(c == n)
        def _():
            PGX[c] = pg.astype(BF)

        @pl.when(c != n)
        def _():
            TABLE[:, 0:HALF] = pg.astype(BF)
    send_pgx = remote(TABLE.at[:, pl.ds(0, HALF)], PGX.at[c], ss.at[6], rs.at[6], sib)
    send_pgx.start()

    def unpermute(t, carry):
        f0 = pl.multiple_of(t * 256, 256)
        back = PM[:, pl.ds(f0, 256)].T
        for i in range(ITEMS):
            GY[i][pl.ds(f0, 256), :] = dot(back, COT[i]).astype(BF)
        return carry

    wait_bytes(PGX.at[0], rs.at[6])

    def send_pg(d):
        return remote(
            PGX.at[:, pl.ds(pl.multiple_of(d * 16, 16), 16)],
            o_phone.at[:, pl.ds(pl.multiple_of(me * 16, 16), 16)], ss.at[8], rs.at[8], (d, c),
        )
    if remote_phon:
        peers(lambda d: send_pg(d).start())
        mine = pl.ds(pl.multiple_of(me * 16, 16), 16)
        o_phone[:, mine] = PGX[:, mine]
    else:
        o_phone[...] = PGX[...]

    lax.fori_loop(0, FRAMES // 512, unpermute, 0)
    rv3(0)

    peers(lambda d: sent(send_sv(d)))
    style_columns = style_rows().astype(BF).T
    column_kind = lax.broadcasted_iota(jnp.int32, (S, ndp * 16), 1) & 7
    weights = AE[...].astype(BF)
    wait_bytes(GSTR.at[pl.ds(0, ndp - 1)], rs.at[5])
    gall = GSTR[...].reshape(ndp * 16, 128)
    spread = jnp.concatenate(
        [jnp.where(row_kind == b, gall, jnp.zeros_like(gall)) for b in range(8)], axis=1
    )
    back_rows = dot_nt(spread, weights).reshape(ndp, 2, 8, S)
    item_sums = [jnp.sum(back_rows[:, i], axis=1, keepdims=True) for i in range(ITEMS)]
    half8 = lax.broadcasted_iota(jnp.int32, (1, 8, S), 1) < 4
    SGS[...] = jnp.where(half8, item_sums[0], item_sums[1])

    def send_sg(d):
        return remote(SGS.at[d], SGR.at[me], ss.at[9], rs.at[9], (d, c))

    peers(lambda d: send_sg(d).start())
    SGR[me] = SGS[me]
    rv4(1)
    for b in range(8):
        picked = jnp.where(column_kind == b, style_columns, jnp.zeros_like(style_columns))
        da = dot(picked, gall)
        part = None
        for qq in range(S // srows):
            piece = jnp.where(quarter == qq, da[qq * srows:(qq + 1) * srows], 0.0)
            part = piece if part is None else part + piece
        SX[0, 0:srows, b * 128:b * 128 + 128] = part
    summed = jnp.sum(GSTR[...].astype(F32), axis=0)
    SX[0, srows:srows + 8, 0:128] = summed[0:8] + summed[8:16]
    BGR[me] = BGRAD[
        me // (ndp // 2), :, pl.ds(pl.multiple_of(lax.rem(me, ndp // 2) // nb * 128, 128), 128)
    ]
    wait_bytes(BGR.at[pl.ds(0, ndp - 1)], rs.at[7])
    SX[0, srows:srows + 8, 128:256] = jnp.broadcast_to(
        jnp.sum(jnp.sum(BGR[...], axis=0), axis=0, keepdims=True), (8, 128)
    )
    lax.fori_loop(FRAMES // 512, FRAMES // 256, unpermute, 0)
    there, here = (pl.ds(pl.multiple_of(k * 512, 512), 512) for k in (1 - c, c))
    send_frames = [
        remote(GY[i].at[there], o_frames.at[c, i], s_o.at[i], r_o.at[i], sib) for i in range(ITEMS)
    ]
    keep_frames = [
        pltpu.make_async_copy(GY[i].at[here], o_frames.at[c, i], loc.at[5 + i]) for i in range(ITEMS)
    ]
    for copy in send_frames + keep_frames:
        copy.start()
    rv4(0)
    wait_bytes(SGR.at[pl.ds(0, ndp - 1)], rs.at[9])
    SX[0, srows:srows + 8, 256:384] = jnp.sum(SGR[...], axis=0)
    send_sx = remote(SX.at[0], SX.at[1], ss.at[10], rs.at[10], sib)
    send_sx.start()

    for j in range(CONVS):
        @pl.when(c0 == j)
        def _():
            total = DW[j][c, c1, c2].astype(F32)
            for k in range(2):
                wait_bytes(ZR.at[k], zr.at[k])
                total = total + ZR[k].astype(F32)
            GF[c] = total
    send_gf = remote(GF.at[c], GF.at[c], ss.at[11], rs.at[11], sib)
    send_gf.start()

    wait_bytes(SX.at[1], rs.at[10])
    both = SX[0, srows:srows + 8, 0:256] + SX[1, srows:srows + 8, 0:256]
    own_rows = [SX[n, srows:srows + 8, 256:384] for n in range(2)]
    for i in range(ITEMS):
        o_sg[c, i:i + 1, :] = own_rows[0][4 * i:4 * i + 1]
        o_sg[1 - c, i:i + 1, :] = own_rows[1][4 * i:4 * i + 1]

    def pick(block, size, at):
        tall, wide = max(1, size // 128), min(128, size)
        total = None
        for q in range(block.shape[0] * 128 // size):
            r, l = q * size // 128, q * size % 128
            part = jnp.where(at == q, block[r:r + tall, l:l + wide], 0.0)
            total = part if total is None else total + part
        return total

    o_goff[...] = pick(both[:, 0:128], cfg["osize"], lax.rem(me, nq))
    o_gbias[...] = pick(both[0:1, 128:256], cfg["bsize"], lax.rem(me, nb))
    for cb in range(8):
        cols = slice(cb * 128, cb * 128 + 128)
        o_gstyle[pl.ds(cb, srows, stride=8), :] = SX[0, 0:srows, cols] + SX[1, 0:srows, cols]
    wait_bytes(GF.at[c], rs.at[11])
    for cb in range(4):
        o_gconv[pl.ds(cb, shard, stride=4), :] = GF[cb // 2, :, (cb % 2) * 128:(cb % 2) * 128 + 128]

    if remote_phon:
        wait_bytes(o_phone.at[:, pl.ds(0, 16 * (ndp - 1))], rs.at[8])
    for i in range(ITEMS):
        wait_bytes(GY[i].at[pl.ds(0, 512)], r_o.at[i])
        keep_frames[i].wait()

    peers(lambda d: sent(send_par(d)))
    if remote_phon:
        peers(lambda d: sent(send_phon(d)))
        peers(lambda d: sent(send_pg(d)))
    peers(lambda d: sent(send_sg(d)))
    for copy in (send_fph, send_cot, send_pgx, *send_frames, send_sx, send_gf):
        sent(copy)
    for j in range(CONVS):
        send_gst(j, sent)
        if j < LAYERS:
            send_bias(j, sent)
        sent(rs_sib(j))
        rs_second(j, sent)
        rs_first(j, sent)
        rs_plane(j, sent)
        rs_inner(j, sent)
    for p in range(n0):
        @pl.when(c0 == p)
        def _():
            z_sends(EARLY, p, sent)
            z_sends(LATE, p, sent)
            if p == RELAY[0]:
                ev_w(sent)
    for zz in range(n0):
        plane_sends(zz, near + far, sent)
        sent(sib_send(zz))


def run_train(cfg, phon, sv, fphone, cnt, cot, wmas, smas, bias_in, offset_in):
    ndp, (n0, n1, n2) = cfg["ndp"], cfg["dims"]
    shard, srows = cfg["shard"], cfg["srows"]
    nmax = max(n1, n2)
    vm = pltpu.VMEM
    dma = pltpu.SemaphoreType.DMA
    any_ = pl.BlockSpec(memory_space=pl.ANY)
    vmem = pl.BlockSpec(memory_space=pltpu.VMEM)
    smem = pl.BlockSpec(memory_space=pltpu.SMEM)
    scratch = [
        vm((2, n0, n1, n2, shard, HALF), BF),
        [[vm((PADDED, D), BF)] * ITEMS] * 2,
        [[vm((D, FRAMES), BF)] * ITEMS] * CONVS,
        [[vm((FRAMES, D), BF)] * ITEMS] * CONVS,
        [vm((FRAMES, D), BF)] * ITEMS,
        [vm((FRAMES, D), BF)] * ITEMS,
        vm((ITEMS, FRAMES, D), BF),
        vm((FRAMES, FRAMES), BF),
        vm((ITEMS, TABLE_ROWS, FRAMES), BF),
        vm((TABLE_ROWS, D), BF),
        vm((ITEMS, FRAMES), jnp.int32),
        vm((shard * 4, 128), F32),
        vm((srows * 8, 128), F32),
        vm((S, 1024), F32),
        vm((ndp, 8, S), F32),
        vm((ndp, 16, 128), BF),
        vm((ndp, 16, 128), BF),
        [[vm((16, D), F32)] * ITEMS] * CONVS,
        [vm((2, 8, D), F32)] * ITEMS,
        vm((LAYERS, 8, D), F32),
        vm((LAYERS, 8, D), F32),
        vm((CONVS, 16, 128), BF),
        vm((ndp, 16, 128), BF),
        vm((ndp, 8, 128), F32),
        vm((ndp, 8, S), F32),
        vm((2, srows + 8, 1024), F32),
        vm((16, 128), F32),
        [vm((2, n1, n2, shard, HALF), BF)] * CONVS,
        vm((CONVS, n1, n2, shard, HALF), BF),
        vm((CONVS, max((n1 - 1) * n2, (n2 - 1) * n1), shard, HALF), BF),
        vm((CONVS, nmax - 1, shard, HALF), BF),
        vm((4, shard, HALF), BF),
        vm((2, shard, HALF), F32),
        vm((2, TABLE_ROWS, HALF), BF),
        dma((8,)), dma((12,)), dma((12,)),
        dma((ITEMS,)), dma((ITEMS,)),
        dma((n0,)), dma((n0,)),
        dma((n0, n1 * n2)), dma((n0, n1 * n2)),
        dma((n0,)), dma((n0,)),
        dma((CONVS,)), dma((CONVS,)),
        dma((CONVS, nmax)), dma((CONVS, nmax)),
        dma((CONVS, nmax)), dma((CONVS, nmax)),
        dma((CONVS,)), dma((4,)),
    ]
    return pl.pallas_call(
        functools.partial(train_kernel, cfg),
        out_shape=(
            jax.ShapeDtypeStruct((2, ITEMS, FRAMES // 2, D), BF),
            jax.ShapeDtypeStruct((2, TABLE_ROWS, HALF), BF),
            jax.ShapeDtypeStruct((2, ITEMS, S), F32),
            jax.ShapeDtypeStruct((1, cfg["bsize"]), F32),
            jax.ShapeDtypeStruct((max(1, cfg["osize"] // 128), min(128, cfg["osize"])), F32),
            jax.ShapeDtypeStruct((shard * 4, 128), F32),
            jax.ShapeDtypeStruct((srows * 8, 128), F32),
        ),
        in_specs=[any_, vmem, any_, smem, any_, any_, any_, vmem, vmem],
        out_specs=(any_, vmem, vmem, vmem, vmem, vmem, vmem),
        scratch_shapes=scratch,
        compiler_params=pltpu.CompilerParams(
            collective_id=0, has_side_effects=True, vmem_limit_bytes=63 * 2**20
        ),
    )(phon, sv, fphone, cnt, cot, wmas, smas, bias_in, offset_in)


def adamw(master, moment, square, gradient):
    new_moment = MOMENT_DECAY * moment + (1.0 - MOMENT_DECAY) * gradient
    new_square = SQUARE_DECAY * square + (1.0 - SQUARE_DECAY) * gradient * gradient
    first_fix = 1.0 - MOMENT_DECAY**STEP
    second_fix = 1.0 - SQUARE_DECAY**STEP
    updated = master - LEARN_RATE * (
        (new_moment / first_fix) / (jnp.sqrt(new_square / second_fix) + ADAM_EPS) + WEIGHT_DECAY * master
    )
    return (updated, new_moment, new_square, updated.astype(BF))


def finish_kernel(cut, *refs):
    ins, outs = refs[:19], refs[19:]
    for n in range(4):
        def update(n=n):
            results = adamw(*(ref[...] for ref in ins[4 * n:4 * n + 4]))
            for ref, value in zip(outs[4 * n:4 * n + 4], results):
                ref[...] = value
        if n < cut:
            update()
        else:
            pl.when(pl.program_id(0) == 0)(update)
    for n in range(16, 19):
        outs[n][...] = ins[n][...].astype(F32)


def finish(groups, casts, steps):
    def rows(a):
        return pl.BlockSpec((a.shape[0] // steps, a.shape[1]), lambda i: (i, 0))

    def whole(a):
        return pl.BlockSpec(a.shape, lambda i: (0,) * a.ndim)

    cut = 2 if groups[1][0].shape[0] % (16 * steps) == 0 else 1
    specs, shapes, args = [], [], []
    for n, group in enumerate(groups):
        for k, a in enumerate(group):
            args.append(a)
            specs.append(rows(a) if n < cut else whole(a))
            shapes.append(jax.ShapeDtypeStruct(a.shape, BF if k == 3 else F32))
    for a in casts:
        args.append(a)
        specs.append(rows(a) if a.ndim == 2 else whole(a))
        shapes.append(jax.ShapeDtypeStruct(a.shape, F32))
    return pl.pallas_call(
        functools.partial(finish_kernel, cut),
        grid=(steps,),
        in_specs=specs,
        out_specs=tuple(specs),
        out_shape=tuple(shapes),
        compiler_params=pltpu.CompilerParams(vmem_limit_bytes=63 * 2**20),
    )(*args)


def on_device(
    phonemes, style_vector, frame_phone, frame_count, cotangent,
    conv_master, conv_moment, conv_square, bias_master, bias_moment, bias_square,
    style_master, style_moment, style_square, offset_master, offset_moment, offset_square,
):
    ndp = lax.axis_size("dp")
    micros, items, slots, _ = phonemes.shape
    shard = conv_master.shape[0] // D
    srows = style_master.shape[0] // (2 * D)
    bsize, osize = bias_master.shape[0], offset_master.shape[0]
    remote_phon = (ITEMS * slots) % 16 == 0
    cfg = dict(
        ndp=ndp, dims=factor(ndp), slots=slots, shard=shard, srows=srows, remote_phon=remote_phon,
        bsize=bsize, osize=osize,
    )
    me = lax.axis_index("dp")
    c = lax.axis_index("seq")
    if remote_phon:
        phon = phonemes.reshape(micros, items * slots, D)
    else:
        mine = lax.dynamic_index_in_dim(phonemes, c, 0, keepdims=False)
        mine = mine.reshape(ndp, ITEMS * slots, D)
        phon = lax.all_to_all(mine, "dp", split_axis=0, concat_axis=0, tiled=True).reshape(TABLE_ROWS, D)
    frames, phone, style_grads, gbias, goff, gconv, gstyle = run_train(
        cfg, phon, style_vector, frame_phone, frame_count, cotangent,
        conv_master.reshape(shard * 4, 128), style_master.reshape(srows * 8, 128), bias_master.reshape(1, bsize),
        offset_master.reshape(max(1, osize // 128), min(128, osize)),
    )
    if not remote_phon:
        phone = lax.all_to_all(
            phone.reshape(micros, ndp, ITEMS * slots, HALF), "dp", split_axis=1, concat_axis=1, tiled=True
        )
    groups = [
        [a.reshape(g.shape) for a in arrays] + [g]
        for arrays, g in (
            ((conv_master, conv_moment, conv_square), gconv),
            ((style_master, style_moment, style_square), gstyle),
            ((bias_master, bias_moment, bias_square), gbias),
            ((offset_master, offset_moment, offset_square), goff),
        )
    ]
    out = finish(
        groups,
        (frames.reshape(micros * ITEMS * FRAMES // 2, D), phone.reshape(micros * TABLE_ROWS, HALF), style_grads), 2,
    )
    flat = [a.reshape(-1) for a in out[:16]]
    return (
        out[16].reshape(frames.shape), out[17].reshape(micros, items, slots, HALF), out[18],
        *flat[0:4], *flat[8:12], *flat[4:8], *flat[12:16],
    )


def solution(mesh):
    return jax.shard_map(
        on_device,
        mesh=mesh,
        in_specs=(
            P(None, None, "dp", None), P(None, "dp", None), P(None, "dp", "seq"), P(None, "dp"),
            P(None, "dp", "seq", None), *[P("dp")] * 12,
        ),
        out_specs=(
            P(None, "dp", "seq", None), P(None, None, "dp", "seq"), P(None, "dp", None), *[P("dp")] * 16,
        ),
        check_vma=False,
    )
```

```python
import functools

import jax
import jax.numpy as jnp
from jax import lax
from jax.experimental import pallas as pl
from jax.experimental.pallas import tpu as pltpu
from jax.sharding import PartitionSpec as P

D = 512
S = 128
KERN = 3
LAYERS = 2
CONVS = 2 * LAYERS
PH = 128
STEP = 10
FRAMES = 1024
SEG = 16
RUN = FRAMES // SEG
HALF = D // 2
ITEMS = 2
PADDED = FRAMES + 2 * SEG
TABLE_ROWS = ITEMS * PH

NORM_EPS = 1e-05
HALF_ROOT = 0.7071067811865476
MOMENT_DECAY = 0.9
SQUARE_DECAY = 0.999
LEARN_RATE = 0.05
WEIGHT_DECAY = 0.01
ADAM_EPS = 1e-08

BF = jnp.bfloat16
F32 = jnp.float32
MESH = pl.DeviceIdType.MESH

C_SCALE, C_SHIFT, C_INV, C_MI, C_ONE, C_2, C_3 = range(7)


PLAN = (
    (
        (7.0, "f", 0), (15.0, "z", 1), (15.0, "f", 1), (16.1, "b", 0), (23.0, "z", 2), (23.0, "f", 2), (25.0, "b", 1),
        (31.5, "z", 3), (31.5, "f", 3), (33.5, "b", 2), (41.5, "b", 3),
    ),
    (
        (7.0, "e", 1), (7.0, "g", 1), (10.5, "z", 0), (10.5, "f", 0), (19.0, "h", 1), (21.0, "b", 0), (23.0, "z", 2),
        (23.0, "f", 2), (25.0, "b", 1), (31.5, "z", 3), (31.5, "f", 3), (33.5, "b", 2), (42.0, "b", 3),
    ),
    (
        (6.0, "w", 0), (6.0, "f", 0), (7.0, "e", 2), (7.0, "v", 2), (14.5, "g", 2), (16.5, "b", 0), (18.5, "z", 1),
        (18.5, "f", 1), (27.0, "h", 2), (28.0, "b", 1), (30.5, "z", 3), (30.5, "f", 3), (32.5, "b", 2), (40.5, "b", 3),
    ),
    (
        (7.0, "e", 3), (7.0, "g", 3), (10.6, "z", 0), (10.6, "f", 0), (20.0, "b", 0), (20.4, "z", 1), (20.4, "f", 1),
        (28.5, "z", 2), (28.5, "f", 2), (30.5, "b", 1), (37.0, "h", 3), (39.0, "b", 2), (43.0, "b", 3),
    ),
)
EARLY = ((2, 1), (0, 2, 3), (1, 0), (2, 1, 0))
LATE = ((), (), (3,), ())
RELAY = (2, 3)


def factor(ndp):
    return {16: (4, 2, 2), 128: (4, 8, 4)}.get(ndp, (4, ndp // 4, 1))


def dot(a, b):
    return jnp.dot(a, b, preferred_element_type=F32)


def dot_nt(a, b):
    return lax.dot_general(a, b, (((1,), (1,)), ((), ())), preferred_element_type=F32)


def dot_tn(a, b):
    return lax.dot_general(a, b, (((0,), (0,)), ((), ())), preferred_element_type=F32)


def fold(tile):
    rows, cols = tile.shape
    return jnp.sum(tile.reshape(rows // 8, 8, cols), axis=0)


def valid_rows(start, rows, count, value):
    i = lax.broadcasted_iota(jnp.int32, (rows, 128), 0)
    frame = (i & (SEG - 1)) * RUN + (i >> 4) + start // SEG
    return jnp.where(frame < count, jnp.float32(value), jnp.float32(0.0))


def train_kernel(cfg, *refs):
    ndp, (n0, n1, n2), slots = cfg["ndp"], cfg["dims"], cfg["slots"]
    shard, srows, remote_phon = cfg["shard"], cfg["srows"], cfg["remote_phon"]
    comm = cfg.get("comm", True)
    skip = cfg.get("skip", ())
    nq = ndp // CONVS
    nb = ndp // 8
    (
        phon, sv, fphone, cnt, cot, wmas, smas, bias_in, offset_in,
        o_frames, o_phone, o_sg, o_gbias, o_goff, o_gconv, o_gstyle,
        W, PAD, AT, ST, G, GY, COT, PM, OHP, TABLE, FPH, WM, SM, AE,
        SVR, PARS, PARR, COEF, STAT, BIAS, BGRAD, GSTS, GSTR, BGR, SGR, SX, ROWS,
        DW, SIBR, RB, RA, ZR, GF, PGX,
        loc, ss, rs, s_o, r_o, s_z, r_z, s_f, r_f, s_b, r_b,
        rss, rsr, rbs, rbr, ras, rar, zs, zr,
    ) = refs
    SGS = SVR
    me = lax.axis_index("dp")
    c = lax.axis_index("seq")
    c0, c1, c2 = me // (n1 * n2), (me // n2) % n1, me % n2
    sib = (me, 1 - c)

    def remote(src, dst, send, recv, target):
        return pltpu.make_async_remote_copy(
            src_ref=src, dst_ref=dst, send_sem=send, recv_sem=recv, device_id=target, device_id_type=MESH
        )

    def wait_bytes(ref, sem):
        pltpu.make_async_copy(ref, ref, sem).wait()

    def sent(copy):
        copy.wait_send()

    def peers(fn):
        def one(d, carry):
            fn(lax.rem(me + d, ndp))
            return carry
        lax.fori_loop(1, ndp, one, 0)

    barrier = pltpu.get_barrier_semaphore()
    peers(lambda d: pl.semaphore_signal(barrier, inc=1, device_id=(d, c), device_id_type=MESH))
    pl.semaphore_signal(barrier, inc=1, device_id=sib, device_id_type=MESH)

    own_in = [
        pltpu.make_async_copy(wmas, WM, loc.at[0]),
        pltpu.make_async_copy(smas, SM, loc.at[1]),
        pltpu.make_async_copy(cot.at[c], COT.at[:, pl.ds(pl.multiple_of(c * HALF * 2, 512), 512)], loc.at[2]),
        pltpu.make_async_copy(fphone.at[c], FPH.at[:, pl.ds(pl.multiple_of(c * HALF * 2, 512), 512)], loc.at[3]),
    ]
    if remote_phon:
        own_in.append(
            pltpu.make_async_copy(
                phon.at[c, pl.ds(pl.multiple_of(me * 16, 16), 16)],
                TABLE.at[pl.ds(pl.multiple_of(me * 16, 16), 16)], loc.at[4],
            )
        )
    else:
        own_in.append(pltpu.make_async_copy(phon, TABLE, loc.at[4]))
    for copy in own_in:
        copy.start()

    own_in[0].wait()
    for cb in range(4):
        W[cb // 2, c0, c1, c2, :, (cb % 2) * 128:(cb % 2) * 128 + 128] = WM[
            pl.ds(cb, shard, stride=4), :
        ].astype(BF)
    own_in[1].wait()
    quarter = lax.rem(me, S // srows)
    for cb in range(8):
        block = SM[pl.ds(cb, srows, stride=8), :].astype(BF).astype(F32)
        for qq in range(S // srows):
            AE[qq * srows:(qq + 1) * srows, cb * 128:cb * 128 + 128] = jnp.where(quarter == qq, block, 0.0)
    ROWS[...] = jnp.zeros(ROWS.shape, F32)
    osize, bsize = cfg["osize"], cfg["bsize"]
    for q in range(nq):
        r, l = q * osize // 128, q * osize % 128
        ROWS[r:r + max(1, osize // 128), l:l + min(128, osize)] = jnp.where(
            lax.rem(me, nq) == q, offset_in[...].astype(BF).astype(F32), 0.0
        )
    for q in range(nb):
        ROWS[8:9, q * bsize:(q + 1) * bsize] = jnp.where(
            lax.rem(me, nb) == q, bias_in[...].astype(BF).astype(F32), 0.0
        )
    bias_row = ROWS[8:9, :]
    vec = sv[c].astype(F32)
    kind8 = lax.broadcasted_iota(jnp.int32, (8, S), 0)
    SVR[me] = jnp.where(kind8 == 0, vec[0:1], jnp.where(kind8 == 1, vec[1:2], bias_row))

    def make_perm(t, carry):
        r0 = pl.multiple_of(t * 128, 128)
        row = lax.broadcasted_iota(jnp.int32, (128, FRAMES), 0)
        col = lax.broadcasted_iota(jnp.int32, (128, FRAMES), 1)
        frame = (row & (SEG - 1)) * RUN + (row >> 4) + r0 // SEG
        PM[pl.ds(r0, 128), :] = jnp.where(col == frame, 1.0, 0.0).astype(BF)
        return carry

    lax.fori_loop(0, FRAMES // 128, make_perm, 0)

    pl.semaphore_wait(barrier, ndp)

    def send_sv(d):
        return remote(SVR.at[me], SVR.at[me], ss.at[0], rs.at[0], (d, c))

    def send_phon(d):
        return remote(
            phon.at[c, pl.ds(pl.multiple_of(d * 16, 16), 16)],
            TABLE.at[pl.ds(pl.multiple_of(me * 16, 16), 16)], ss.at[1], rs.at[1], (d, c),
        )

    send_fph = remote(
        fphone.at[1 - c], FPH.at[:, pl.ds(pl.multiple_of(c * 512, 512), 512)], ss.at[2], rs.at[2], sib
    )
    send_cot = remote(
        cot.at[1 - c], COT.at[:, pl.ds(pl.multiple_of(c * 512, 512), 512)], ss.at[3], rs.at[3], sib
    )
    def z_send(zz, to, k, fn):
        piece = W.at[c, zz, c1, c2]
        fn(remote(piece, piece, s_z.at[k], r_z.at[zz], ((to * n1 + c1) * n2 + c2, c)))

    def z_sends(sends, p, fn):
        for to in sends[p]:
            z_send(p, to, to, fn)

    def z_wait(zz):
        wait_bytes(W.at[c, zz, c1, c2], r_z.at[zz])

    def ev_w(fn=None):
        if fn is None:
            z_wait(0)
        z_send(0, RELAY[1], RELAY[0], fn or start)

    near = [k for k in range(1, n1 * n2) if k // n2 == 0 or k % n2 == 0]
    far = [k for k in range(1, n1 * n2) if k not in near]

    def plane_sends(zz, ks, fn):
        piece = W.at[c, zz, c1, c2]
        for k in ks:
            y, x = lax.rem(c1 + k // n2, n1), lax.rem(c2 + k % n2, n2)
            fn(remote(piece, piece, s_f.at[zz, k], r_f.at[zz, k], ((c0 * n1 + y) * n2 + x, c)))

    def plane_wait(zz):
        for k in range(1, n1 * n2):
            wait_bytes(W.at[c, zz, c1, c2], r_f.at[zz, k])

    def sib_send(zz):
        return remote(W.at[c, zz], W.at[c, zz], s_b.at[zz], r_b.at[zz], sib)

    def start(copy):
        copy.start()

    def ev_b(zz):
        plane_wait(zz)
        sib_send(zz).start()

    def plane_events(p):
        events = []
        for at, kind, zz in PLAN[p]:
            fn = {
                "e": lambda: z_sends(EARLY, p, start),
                "v": lambda: z_sends(LATE, p, start),
                "z": lambda zz=zz: z_wait(zz),
                "w": ev_w,
                "f": lambda zz=zz: plane_sends(zz, near + far, start),
                "g": lambda zz=zz: plane_sends(zz, near, start),
                "h": lambda zz=zz: plane_sends(zz, far, start),
                "b": lambda zz=zz: ev_b(zz),
            }[kind]
            events.append((at, fn))
            if kind == "b":
                ready[p][zz] = at + 0.1
        return events

    ready = {p: {} for p in range(n0)}
    plan = {p: plane_events(p) for p in range(n0)}
    clock = {p: 0.0 for p in range(n0)}

    def take(passed, until=None):
        dues = {}
        for p in range(n0):
            clock[p] += passed
            if until is not None:
                clock[p] = max(clock[p], ready[p][until])
            dues[p] = [e for e in plan[p] if e[0] <= clock[p]]
            plan[p] = plan[p][len(dues[p]):]
            if until is not None:
                clock[p] += 2.4
        return dues

    def run_due(dues, when=True):
        for p, due in dues.items():
            if due:
                @pl.when(jnp.logical_and(c0 == p, when))
                def _(due=due):
                    for _, fn in due:
                        fn()

    def slot(passed, until=None):
        run_due(take(passed, until))
        if until is not None:
            wait_bytes(W.at[c, until], r_b.at[until])

    peers(lambda d: send_sv(d).start())

    @pl.when(c0 == 0)
    def _():
        z_sends(EARLY, 0, start)
    if remote_phon:
        peers(lambda d: send_phon(d).start())
    send_fph.start()
    send_cot.start()

    slot(3.0)
    own_in[3].wait()
    wait_bytes(FPH.at[:, pl.ds(0, 512)], rs.at[2])
    def one_hot(i):
        phone = FPH[i:i + 1, :]
        if slots & (slots - 1) == 0:
            shift = slots.bit_length() - 1
            place = ((phone >> shift) << (shift + 1)) + i * slots + (phone & (slots - 1))
        else:
            place = (phone // slots) * (2 * slots) + i * slots + phone % slots
        spot = lax.broadcasted_iota(jnp.int32, (TABLE_ROWS, FRAMES), 0)
        onehot = jnp.where(spot == place, 1.0, 0.0).astype(BF)
        for t in range(4):
            OHP[i, :, t * 256:t * 256 + 256] = dot_nt(onehot, PM[t * 256:t * 256 + 256, :]).astype(BF)

    one_hot(0)
    slot(1.5)

    one_hot(1)
    slot(1.5)

    row_kind = lax.broadcasted_iota(jnp.int32, (ndp * 16, 1), 0) & 7

    def style_rows():
        got = SVR[...]
        pair = [jnp.broadcast_to(got[:, i:i + 1, :], (ndp, 8, S)) for i in range(ITEMS)]
        return jnp.concatenate(pair, axis=1).reshape(ndp * 16, S)

    wait_bytes(SVR.at[pl.ds(0, ndp - 1)], rs.at[0])
    svall = style_rows()
    acc = jnp.zeros((ndp * 16, 128), F32)
    for b in range(8):
        acc = acc + dot(
            jnp.where(row_kind == b, svall, 0.0).astype(BF), AE[:, b * 128:b * 128 + 128].astype(BF)
        )
    offs = ROWS[0:8, :]
    acc = acc.reshape(ndp, 16, 128) + jnp.concatenate([offs, offs], axis=0).reshape(1, 16, 128)
    PARS[...] = acc.astype(BF)

    def send_par(d):
        return remote(PARS.at[d], PARR.at[me], ss.at[4], rs.at[4], (d, c))

    peers(lambda d: send_par(d).start())
    PARR[me] = PARS[me]
    slot(2.0)

    own_in[2].wait()
    wait_bytes(COT.at[:, pl.ds(0, 512)], rs.at[3])
    for i in range(ITEMS):
        count = cnt[c, i]

        def permute(t, carry):
            r0 = pl.multiple_of(t * 256, 256)
            y = dot(PM[pl.ds(r0, 256), :], COT[i])
            mask = valid_rows(r0, 256, count, 1.0)
            G[i][pl.ds(r0, 256), :] = (y * jnp.concatenate([mask] * 4, axis=1)).astype(BF)
            return carry

        lax.fori_loop(0, 4, permute, 0)
        slot(1.3)

    for i in range(ITEMS):
        STAT[i][...] = jnp.zeros(STAT[i].shape, F32)
    own_in[4].wait()
    if remote_phon:
        wait_bytes(TABLE.at[pl.ds(0, 16 * (ndp - 1))], rs.at[1])
    for i in range(ITEMS):
        count = cnt[c, i]
        for t in range(4):
            x = dot(OHP[i, :, t * 256:t * 256 + 256].T, TABLE[...])
            mask = valid_rows(t * 256, 256, count, 1.0)
            x = x * jnp.concatenate([mask] * 4, axis=1)
            ST[0][i][t * 256:t * 256 + 256, :] = x.astype(BF)
            STAT[i][0] += fold(x)
            STAT[i][1] += fold(x * x)
        slot(3.4 if i == 0 else 1.0)

    wait_bytes(PARR.at[pl.ds(0, ndp - 1)], rs.at[4])
    for j in range(CONVS):
        total = jnp.sum(PARR[j * nq:(j + 1) * nq].astype(F32), axis=0)
        for i in range(ITEMS):
            for b in range(8):
                COEF[j][i][8 + b // 4:9 + b // 4, (b % 4) * 128:(b % 4) * 128 + 128] = total[
                    8 * i + b:8 * i + b + 1, :
                ]
    for l in range(LAYERS):
        for qb in range(4):
            first = l * (ndp // 2) + qb * nb
            BIAS[l, :, qb * 128:qb * 128 + 128] = jnp.broadcast_to(
                jnp.sum(SVR[first:first + nb], axis=0)[2:3, :], (8, 128)
            )
    slot(0.5)

    def stats_to_coef(j, i):
        n = cnt[c, i].astype(F32)
        sums = jnp.sum(STAT[i][0], axis=0, keepdims=True)
        squares = jnp.sum(STAT[i][1], axis=0, keepdims=True)
        STAT[i][...] = jnp.zeros(STAT[i].shape, F32)
        mean = sums / n
        var = jnp.maximum(squares / n - mean * mean, 0.0)
        inv = lax.rsqrt(var + NORM_EPS)
        one = (1.0 + COEF[j][i][8:9]) * inv
        shift = COEF[j][i][9:10] - mean * one

        def put(k, v):
            COEF[j][i][k:k + 1] = v
        put(C_SCALE, 0.5 * one)
        put(C_SHIFT, 0.5 * shift)
        put(C_INV, inv)
        put(C_MI, mean * inv)
        put(C_ONE, one)

    def coef(j, i, k, cols):
        return COEF[j][i][k:k + 1, cols]

    def edges(pad, i):
        row = lax.broadcasted_iota(jnp.int32, (SEG, D), 0)
        last = PAD[pad][i][FRAMES:FRAMES + SEG, :].astype(F32)
        head = jnp.where(row == 0, 0.0, pltpu.roll(last, 1, 0))
        PAD[pad][i][0:SEG, :] = head.astype(BF)
        first = PAD[pad][i][SEG:2 * SEG, :].astype(F32)
        tail = jnp.where(row == SEG - 1, 0.0, pltpu.roll(first, SEG - 1, 0))
        PAD[pad][i][FRAMES + SEG:PADDED, :] = tail.astype(BF)

    TR = 128
    M = 512
    MG = 256

    def adain_tile(j, i):
        count = cnt[c, i]

        def run(r1):
            for rb in range(0, M, TR):
                r0 = pl.multiple_of(r1 + rb, TR)
                mask = valid_rows(r0, TR, count, 1.0)
                for cb in range(4):
                    cols = slice(cb * 128, cb * 128 + 128)
                    x = ST[j][i][pl.ds(r0, TR), cols].astype(F32)
                    v = x * coef(j, i, C_SCALE, cols) + coef(j, i, C_SHIFT, cols)
                    a = ((v + v * jnp.tanh(v)) * mask).astype(BF)
                    PAD[j % 2][i][pl.ds(r0 + SEG, TR), cols] = a
                    AT[j][i][cols, pl.ds(r0, TR)] = a.T
        return run

    def conv_tile(j, i, epilogue):
        def run(r0):
            for h in range(2):
                acc = None
                weights = W[h, j].reshape(KERN * D, HALF)
                for k in range(KERN):
                    part = dot(PAD[j % 2][i][pl.ds(r0 + SEG * k, M), :], weights[k * D:(k + 1) * D])
                    acc = part if acc is None else acc + part
                epilogue(i, r0, h, acc)
        return run

    def together(passed, *parts, then=None):
        for t in range(FRAMES // M):
            for part in parts:
                part(t * M)
            if then is not None and t == 0:
                then()
            slot(passed)

    def middle_out(j):
        def epilogue(i, r0, h, acc):
            count = cnt[c, i]
            masks = [valid_rows(r0 + rb, 128, count, 1.0) for rb in range(0, M, 128)]
            for cb in range(2):
                cols = slice(h * HALF + cb * 128, h * HALF + cb * 128 + 128)
                sums = [0.0, 0.0]
                for rb in range(0, M, 128):
                    p = acc[rb:rb + 128, cb * 128:cb * 128 + 128]
                    ST[j + 1][i][pl.ds(r0 + rb, 128), cols] = p.astype(BF)
                    kept = p * masks[rb // 128]
                    sums = [sums[0] + fold(kept), sums[1] + fold(kept * p)]
                for n in range(2):
                    STAT[i][n, :, cols] += sums[n]
        return epilogue

    def block_out(l):
        def epilogue(i, r0, h, acc):
            count = cnt[c, i]
            masks = [valid_rows(r0 + rb, 128, count, HALF_ROOT) for rb in range(0, M, 128)]
            for cb in range(2):
                cols = slice(h * HALF + cb * 128, h * HALF + cb * 128 + 128)
                sums = [0.0, 0.0]
                for rb in range(0, M, 128):
                    q = acc[rb:rb + 128, cb * 128:cb * 128 + 128] + BIAS[l, 0:1, cols]
                    x = (ST[2 * l][i][pl.ds(r0 + rb, 128), cols].astype(F32) + q) * masks[rb // 128]
                    if l < LAYERS - 1:
                        ST[2 * l + 2][i][pl.ds(r0 + rb, 128), cols] = x.astype(BF)
                        sums = [sums[0] + fold(x), sums[1] + fold(x * x)]
                    else:
                        COT[i, pl.ds(r0 + rb, 128), cols] = x.astype(BF)
                if l < LAYERS - 1:
                    for n in range(2):
                        STAT[i][n, :, cols] += sums[n]
        return epilogue

    def enter_tile(i):
        def run(r1):
            for rb in range(0, M, TR):
                r0 = pl.multiple_of(r1 + rb, TR)
                g = (G[i][pl.ds(r0, TR), :].astype(F32) * HALF_ROOT).astype(BF)
                PAD[1][i][pl.ds(r0 + SEG, TR), :] = g
                BGRAD[LAYERS - 1] += fold(g.astype(F32))
        return run

    def grad_weight_tile(j):
        def run(r1):
            h = jnp.where(r1 == 0, 1 - c, c)
            cols = pl.ds(pl.multiple_of(h * HALF, HALF), HALF)
            for r0 in range(0, D, 256):
                for k in range(KERN):
                    acc = None
                    for i in range(ITEMS):
                        part = dot(
                            AT[j][i][r0:r0 + 256, :], PAD[j % 2][i][(2 - k) * SEG:(2 - k) * SEG + FRAMES, cols]
                        )
                        acc = part if acc is None else acc + part
                    DWF[j].at[h][k * D + r0:k * D + r0 + 256, :] = acc.astype(BF)
        return run

    DWF = [DW[j].reshape(2, KERN * D, HALF) for j in range(CONVS)]

    def grad_input_tile(j, i):
        count = cnt[c, i]

        def run(r1):
            for r0, n in ((pl.multiple_of(r1 + r, MG), n) for r in range(0, M, MG) for n in range(2)):
                acc = None
                for k in range(KERN):
                    for h in range(2):
                        weights = W[h, j].reshape(KERN * D, HALF)
                        part = dot_nt(
                            PAD[j % 2][i][pl.ds(r0 + SEG * (2 - k), MG), h * HALF:(h + 1) * HALF],
                            weights[k * D + n * HALF:k * D + (n + 1) * HALF],
                        )
                        acc = part if acc is None else acc + part
                masks = [valid_rows(r0 + rb, 128, count, 0.5) for rb in range(0, MG, 128)]
                for cb in range(2):
                    cols = slice(n * HALF + cb * 128, n * HALF + cb * 128 + 128)
                    sums = [0.0, 0.0]
                    for rb in range(0, MG, 128):
                        mask = masks[rb // 128]
                        x = ST[j][i][pl.ds(r0 + rb, 128), cols].astype(F32)
                        v = x * coef(j, i, C_SCALE, cols) + coef(j, i, C_SHIFT, cols)
                        th = jnp.tanh(v)
                        u = acc[rb:rb + 128, cb * 128:cb * 128 + 128] * mask
                        gy = (u + u * th) * (1.0 + v * (1.0 - th))
                        xhat = x * coef(j, i, C_INV, cols) - coef(j, i, C_MI, cols)
                        sums = [sums[0] + fold(gy), sums[1] + fold(gy * xhat)]
                        GY[i][pl.ds(r0 + rb, 128), cols] = gy.astype(BF)
                    for k in range(2):
                        STAT[i][k, :, cols] += sums[k]
        return run

    def send_gst(j, fn):
        def one(q, carry):
            d = j * nq + q

            @pl.when(d != me)
            def _():
                fn(remote(GSTS.at[j], GSTR.at[me], ss.at[5], rs.at[5], (d, c)))
            return carry
        lax.fori_loop(0, nq, one, 0)

    def send_bias(l, fn):
        def one(q, carry):
            d = l * (ndp // 2) + q
            part = BGRAD.at[l, :, pl.ds(pl.multiple_of(q // nb * 128, 128), 128)]

            @pl.when(d != me)
            def _():
                fn(remote(part, BGR.at[me], ss.at[7], rs.at[7], (d, c)))
            return carry
        lax.fori_loop(0, ndp // 2, one, 0)

    def adain_sums(j, i):
        n = cnt[c, i].astype(F32)
        gt = jnp.sum(STAT[i][0], axis=0, keepdims=True)
        gs = jnp.sum(STAT[i][1], axis=0, keepdims=True)
        STAT[i][...] = jnp.zeros(STAT[i].shape, F32)
        one, inv, mi = (COEF[j][i][k:k + 1] for k in (C_ONE, C_INV, C_MI))
        each = one / n
        COEF[j][i][C_2:C_2 + 1] = each * (gt - mi * gs)
        COEF[j][i][C_3:C_3 + 1] = each * inv * gs
        rows = [x[:, b * 128:b * 128 + 128] for x in (gs, gt) for b in range(4)]
        GSTS[j, 8 * i:8 * i + 8, :] = jnp.concatenate(rows, axis=0).astype(BF)
        if i == ITEMS - 1:
            @pl.when(me // nq == j)
            def _():
                GSTR[me] = GSTS[j]
            send_gst(j, start)

    def adain_back_tile(j, i):
        count = cnt[c, i]

        def run(r1):
            for rb in range(0, M, TR):
                r0 = pl.multiple_of(r1 + rb, TR)
                mask = valid_rows(r0, TR, count, 1.0)
                for cb in range(4):
                    cols = slice(cb * 128, cb * 128 + 128)
                    gy = GY[i][pl.ds(r0, TR), cols].astype(F32)
                    x = ST[j][i][pl.ds(r0, TR), cols].astype(F32)
                    g = gy * coef(j, i, C_ONE, cols) - x * coef(j, i, C_3, cols) - coef(j, i, C_2, cols)
                    g = g * mask
                    if j % 2 == 0:
                        g = G[i][pl.ds(r0, TR), cols].astype(F32) * HALF_ROOT + g
                        if j > 0:
                            G[i][pl.ds(r0, TR), cols] = g.astype(BF)
                            g = g * HALF_ROOT
                            BGRAD[j // 2 - 1, :, cols] += fold(g.astype(BF).astype(F32))
                    PAD[1 - j % 2][i][pl.ds(r0 + SEG, TR), cols] = g.astype(BF)
        return run

    def rs_sib(j):
        return remote(DW[j].at[1 - c], SIBR.at[j], rss.at[j], rsr.at[j], sib)

    def rs_second(j, fn):
        @pl.when(c == 0)
        def _():
            for k in range(1, n1):
                to = lax.rem(c1 + k, n1)
                fn(remote(DW[j].at[0, to], RB.at[j, pl.ds((k - 1) * n2, n2)], rbs.at[j, k], rbr.at[j, k],
                          ((c0 * n1 + to) * n2 + c2, c)))

        @pl.when(c == 1)
        def _():
            for k in range(1, n2):
                to = lax.rem(c2 + k, n2)
                fn(remote(DW[j].at[1, :, to], RB.at[j, pl.ds((k - 1) * n1, n1)], rbs.at[j, k], rbr.at[j, k],
                          ((c0 * n1 + c1) * n2 + to, c)))

    def rs_first(j, fn):
        @pl.when(c == 0)
        def _():
            for k in range(1, n2):
                to = lax.rem(c2 + k, n2)
                fn(remote(DW[j].at[0, c1, to], RA.at[j, k - 1], ras.at[j, k], rar.at[j, k],
                          ((c0 * n1 + c1) * n2 + to, c)))

        @pl.when(c == 1)
        def _():
            for k in range(1, n1):
                to = lax.rem(c1 + k, n1)
                fn(remote(DW[j].at[1, to, c2], RA.at[j, k - 1], ras.at[j, k], rar.at[j, k],
                          ((c0 * n1 + to) * n2 + c2, c)))

    def rs_plane(j, fn):
        outer, inner = ((3, 2) if j < 2 else (0, 1))
        for p, to, k in ((j ^ 1, j, 0), (outer, inner, 2 + j % 2)):
            @pl.when(c0 == p)
            def _(to=to, k=k):
                fn(remote(DW[j].at[c, c1, c2], ZR.at[k], zs.at[j], zr.at[k], ((to * n1 + c1) * n2 + c2, c)))

    def rs_inner(j, fn):
        @pl.when(c0 == (2 if j < 2 else 1))
        def _():
            fn(remote(DW[j].at[c, c1, c2], ZR.at[1], zs.at[j], zr.at[1], ((j * n1 + c1) * n2 + c2, c)))

    def rv4(j):
        @pl.when(c0 == (2 if j < 2 else 1))
        def _():
            k = 2 + j % 2
            wait_bytes(ZR.at[k], zr.at[k])
            DW[j][c, c1, c2] = (DW[j][c, c1, c2].astype(F32) + ZR[k].astype(F32)).astype(BF)
        rs_inner(j, start)

    def rv0(j):
        rs_sib(j).start()

    def rv1(j):
        wait_bytes(SIBR.at[j], rsr.at[j])

        def one(y, carry):
            for x in range(n2):
                DW[j][c, y, x] = (DW[j][c, y, x].astype(F32) + SIBR[j, y, x].astype(F32)).astype(BF)
            return carry
        lax.fori_loop(0, n1, one, 0)
        rs_second(j, lambda copy: copy.start())

    def rv2(j):
        @pl.when(c == 0)
        def _():
            for k in range(1, n1):
                wait_bytes(RB.at[j, pl.ds((k - 1) * n2, n2)], rbr.at[j, k])
            for x in range(n2):
                total = DW[j][0, c1, x].astype(F32)
                for k in range(1, n1):
                    total = total + RB[j, (k - 1) * n2 + x].astype(F32)
                DW[j][0, c1, x] = total.astype(BF)

        @pl.when(c == 1)
        def _():
            for k in range(1, n2):
                wait_bytes(RB.at[j, pl.ds((k - 1) * n1, n1)], rbr.at[j, k])
            for y in range(n1):
                total = DW[j][1, y, c2].astype(F32)
                for k in range(1, n2):
                    total = total + RB[j, (k - 1) * n1 + y].astype(F32)
                DW[j][1, y, c2] = total.astype(BF)
        rs_first(j, lambda copy: copy.start())

    def rv3(j):
        def add(n):
            for k in range(1, n):
                wait_bytes(RA.at[j, k - 1], rar.at[j, k])
            total = DW[j][c, c1, c2].astype(F32)
            for k in range(1, n):
                total = total + RA[j, k - 1].astype(F32)
            DW[j][c, c1, c2] = total.astype(BF)

        @pl.when(c == 0)
        def _():
            add(n2)

        @pl.when(c == 1)
        def _():
            add(n1)
        rs_plane(j, lambda copy: copy.start())

    BGRAD[...] = jnp.zeros(BGRAD.shape, F32)
    stats_to_coef(0, 0)
    together(0.6, adain_tile(0, 0))
    edges(0, 0)
    for j in range(CONVS):
        epilogue = block_out(j // 2) if j % 2 else middle_out(j)
        stats_to_coef(j, 1)
        slot(0.0, j)
        together(1.3, conv_tile(j, 0, epilogue), adain_tile(j, 1))
        edges(j % 2, 1)
        if j < CONVS - 1:
            stats_to_coef(j + 1, 0)
            together(1.3, conv_tile(j, 1, epilogue), adain_tile(j + 1, 0))
            edges((j + 1) % 2, 0)
        else:
            together(1.3, conv_tile(j, 1, epilogue), enter_tile(0))
            edges(1, 0)

    together(1.3, grad_input_tile(3, 0), enter_tile(1))
    edges(1, 1)
    send_bias(1, start)
    for j in reversed(range(1, CONVS)):
        if j < CONVS - 1:
            together(1.3, grad_input_tile(j, 0))
        adain_sums(j, 0)
        together(1.3, grad_input_tile(j, 1), adain_back_tile(j, 0))
        edges(1 - j % 2, 0)
        adain_sums(j, 1)
        if j < CONVS - 1:
            rv2(j + 1)
        together(1.8, grad_weight_tile(j), adain_back_tile(j, 1), then=lambda: rv0(j))
        edges(1 - j % 2, 1)
        rv1(j)
        if j < CONVS - 1:
            rv3(j + 1)
        if j < CONVS - 2:
            rv4(j + 2)
        if j == 2:
            send_bias(0, start)
    together(1.8, grad_weight_tile(0), then=lambda: rv0(0))
    rv1(0)
    together(1.3, grad_input_tile(0, 0))
    rv2(1)
    adain_sums(0, 0)
    together(1.3, grad_input_tile(0, 1), adain_back_tile(0, 0))
    adain_sums(0, 1)
    together(0.3, adain_back_tile(0, 1))
    rv3(1)
    rv2(0)
    rv4(2)

    for n in range(2):
        cols = slice(n * HALF, (n + 1) * HALF)
        pg = dot(OHP[0], PAD[1][0][SEG:SEG + FRAMES, cols]) + dot(OHP[1], PAD[1][1][SEG:SEG + FRAMES, cols])

        @pl.when(c == n)
        def _():
            PGX[c] = pg.astype(BF)

        @pl.when(c != n)
        def _():
            TABLE[:, 0:HALF] = pg.astype(BF)
    send_pgx = remote(TABLE.at[:, pl.ds(0, HALF)], PGX.at[c], ss.at[6], rs.at[6], sib)
    send_pgx.start()

    def unpermute(t, carry):
        f0 = pl.multiple_of(t * 256, 256)
        back = PM[:, pl.ds(f0, 256)].T
        for i in range(ITEMS):
            GY[i][pl.ds(f0, 256), :] = dot(back, COT[i]).astype(BF)
        return carry

    wait_bytes(PGX.at[0], rs.at[6])

    def send_pg(d):
        return remote(
            PGX.at[:, pl.ds(pl.multiple_of(d * 16, 16), 16)],
            o_phone.at[:, pl.ds(pl.multiple_of(me * 16, 16), 16)], ss.at[8], rs.at[8], (d, c),
        )
    if remote_phon:
        peers(lambda d: send_pg(d).start())
        mine = pl.ds(pl.multiple_of(me * 16, 16), 16)
        o_phone[:, mine] = PGX[:, mine]
    else:
        o_phone[...] = PGX[...]

    lax.fori_loop(0, FRAMES // 512, unpermute, 0)
    rv3(0)

    peers(lambda d: sent(send_sv(d)))
    style_columns = style_rows().astype(BF).T
    column_kind = lax.broadcasted_iota(jnp.int32, (S, ndp * 16), 1) & 7
    weights = AE[...].astype(BF)
    wait_bytes(GSTR.at[pl.ds(0, ndp - 1)], rs.at[5])
    gall = GSTR[...].reshape(ndp * 16, 128)
    spread = jnp.concatenate(
        [jnp.where(row_kind == b, gall, jnp.zeros_like(gall)) for b in range(8)], axis=1
    )
    back_rows = dot_nt(spread, weights).reshape(ndp, 2, 8, S)
    item_sums = [jnp.sum(back_rows[:, i], axis=1, keepdims=True) for i in range(ITEMS)]
    half8 = lax.broadcasted_iota(jnp.int32, (1, 8, S), 1) < 4
    SGS[...] = jnp.where(half8, item_sums[0], item_sums[1])

    def send_sg(d):
        return remote(SGS.at[d], SGR.at[me], ss.at[9], rs.at[9], (d, c))

    peers(lambda d: send_sg(d).start())
    SGR[me] = SGS[me]
    rv4(1)
    for b in range(8):
        picked = jnp.where(column_kind == b, style_columns, jnp.zeros_like(style_columns))
        da = dot(picked, gall)
        part = None
        for qq in range(S // srows):
            piece = jnp.where(quarter == qq, da[qq * srows:(qq + 1) * srows], 0.0)
            part = piece if part is None else part + piece
        SX[0, 0:srows, b * 128:b * 128 + 128] = part
    summed = jnp.sum(GSTR[...].astype(F32), axis=0)
    SX[0, srows:srows + 8, 0:128] = summed[0:8] + summed[8:16]
    BGR[me] = BGRAD[
        me // (ndp // 2), :, pl.ds(pl.multiple_of(lax.rem(me, ndp // 2) // nb * 128, 128), 128)
    ]
    wait_bytes(BGR.at[pl.ds(0, ndp - 1)], rs.at[7])
    SX[0, srows:srows + 8, 128:256] = jnp.broadcast_to(
        jnp.sum(jnp.sum(BGR[...], axis=0), axis=0, keepdims=True), (8, 128)
    )
    lax.fori_loop(FRAMES // 512, FRAMES // 256, unpermute, 0)
    there, here = (pl.ds(pl.multiple_of(k * 512, 512), 512) for k in (1 - c, c))
    send_frames = [
        remote(GY[i].at[there], o_frames.at[c, i], s_o.at[i], r_o.at[i], sib) for i in range(ITEMS)
    ]
    keep_frames = [
        pltpu.make_async_copy(GY[i].at[here], o_frames.at[c, i], loc.at[5 + i]) for i in range(ITEMS)
    ]
    for copy in send_frames + keep_frames:
        copy.start()
    rv4(0)
    wait_bytes(SGR.at[pl.ds(0, ndp - 1)], rs.at[9])
    SX[0, srows:srows + 8, 256:384] = jnp.sum(SGR[...], axis=0)
    send_sx = remote(SX.at[0], SX.at[1], ss.at[10], rs.at[10], sib)
    send_sx.start()

    for j in range(CONVS):
        @pl.when(c0 == j)
        def _():
            total = DW[j][c, c1, c2].astype(F32)
            for k in range(2):
                wait_bytes(ZR.at[k], zr.at[k])
                total = total + ZR[k].astype(F32)
            GF[c] = total
    send_gf = remote(GF.at[c], GF.at[c], ss.at[11], rs.at[11], sib)
    send_gf.start()

    wait_bytes(SX.at[1], rs.at[10])
    both = SX[0, srows:srows + 8, 0:256] + SX[1, srows:srows + 8, 0:256]
    own_rows = [SX[n, srows:srows + 8, 256:384] for n in range(2)]
    for i in range(ITEMS):
        o_sg[c, i:i + 1, :] = own_rows[0][4 * i:4 * i + 1]
        o_sg[1 - c, i:i + 1, :] = own_rows[1][4 * i:4 * i + 1]

    def pick(block, size, at):
        tall, wide = max(1, size // 128), min(128, size)
        total = None
        for q in range(block.shape[0] * 128 // size):
            r, l = q * size // 128, q * size % 128
            part = jnp.where(at == q, block[r:r + tall, l:l + wide], 0.0)
            total = part if total is None else total + part
        return total

    o_goff[...] = pick(both[:, 0:128], cfg["osize"], lax.rem(me, nq))
    o_gbias[...] = pick(both[0:1, 128:256], cfg["bsize"], lax.rem(me, nb))
    for cb in range(8):
        cols = slice(cb * 128, cb * 128 + 128)
        o_gstyle[pl.ds(cb, srows, stride=8), :] = SX[0, 0:srows, cols] + SX[1, 0:srows, cols]
    wait_bytes(GF.at[c], rs.at[11])
    for cb in range(4):
        o_gconv[pl.ds(cb, shard, stride=4), :] = GF[cb // 2, :, (cb % 2) * 128:(cb % 2) * 128 + 128]

    if remote_phon:
        wait_bytes(o_phone.at[:, pl.ds(0, 16 * (ndp - 1))], rs.at[8])
    for i in range(ITEMS):
        wait_bytes(GY[i].at[pl.ds(0, 512)], r_o.at[i])
        keep_frames[i].wait()

    peers(lambda d: sent(send_par(d)))
    if remote_phon:
        peers(lambda d: sent(send_phon(d)))
        peers(lambda d: sent(send_pg(d)))
    peers(lambda d: sent(send_sg(d)))
    for copy in (send_fph, send_cot, send_pgx, *send_frames, send_sx, send_gf):
        sent(copy)
    for j in range(CONVS):
        send_gst(j, sent)
        if j < LAYERS:
            send_bias(j, sent)
        sent(rs_sib(j))
        rs_second(j, sent)
        rs_first(j, sent)
        rs_plane(j, sent)
        rs_inner(j, sent)
    for p in range(n0):
        @pl.when(c0 == p)
        def _():
            z_sends(EARLY, p, sent)
            z_sends(LATE, p, sent)
            if p == RELAY[0]:
                ev_w(sent)
    for zz in range(n0):
        plane_sends(zz, near + far, sent)
        sent(sib_send(zz))


def run_train(cfg, phon, sv, fphone, cnt, cot, wmas, smas, bias_in, offset_in):
    ndp, (n0, n1, n2) = cfg["ndp"], cfg["dims"]
    shard, srows = cfg["shard"], cfg["srows"]
    nmax = max(n1, n2)
    vm = pltpu.VMEM
    dma = pltpu.SemaphoreType.DMA
    any_ = pl.BlockSpec(memory_space=pl.ANY)
    vmem = pl.BlockSpec(memory_space=pltpu.VMEM)
    smem = pl.BlockSpec(memory_space=pltpu.SMEM)
    scratch = [
        vm((2, n0, n1, n2, shard, HALF), BF),
        [[vm((PADDED, D), BF)] * ITEMS] * 2,
        [[vm((D, FRAMES), BF)] * ITEMS] * CONVS,
        [[vm((FRAMES, D), BF)] * ITEMS] * CONVS,
        [vm((FRAMES, D), BF)] * ITEMS,
        [vm((FRAMES, D), BF)] * ITEMS,
        vm((ITEMS, FRAMES, D), BF),
        vm((FRAMES, FRAMES), BF),
        vm((ITEMS, TABLE_ROWS, FRAMES), BF),
        vm((TABLE_ROWS, D), BF),
        vm((ITEMS, FRAMES), jnp.int32),
        vm((shard * 4, 128), F32),
        vm((srows * 8, 128), F32),
        vm((S, 1024), F32),
        vm((ndp, 8, S), F32),
        vm((ndp, 16, 128), BF),
        vm((ndp, 16, 128), BF),
        [[vm((16, D), F32)] * ITEMS] * CONVS,
        [vm((2, 8, D), F32)] * ITEMS,
        vm((LAYERS, 8, D), F32),
        vm((LAYERS, 8, D), F32),
        vm((CONVS, 16, 128), BF),
        vm((ndp, 16, 128), BF),
        vm((ndp, 8, 128), F32),
        vm((ndp, 8, S), F32),
        vm((2, srows + 8, 1024), F32),
        vm((16, 128), F32),
        [vm((2, n1, n2, shard, HALF), BF)] * CONVS,
        vm((CONVS, n1, n2, shard, HALF), BF),
        vm((CONVS, max((n1 - 1) * n2, (n2 - 1) * n1), shard, HALF), BF),
        vm((CONVS, nmax - 1, shard, HALF), BF),
        vm((4, shard, HALF), BF),
        vm((2, shard, HALF), F32),
        vm((2, TABLE_ROWS, HALF), BF),
        dma((8,)), dma((12,)), dma((12,)),
        dma((ITEMS,)), dma((ITEMS,)),
        dma((n0,)), dma((n0,)),
        dma((n0, n1 * n2)), dma((n0, n1 * n2)),
        dma((n0,)), dma((n0,)),
        dma((CONVS,)), dma((CONVS,)),
        dma((CONVS, nmax)), dma((CONVS, nmax)),
        dma((CONVS, nmax)), dma((CONVS, nmax)),
        dma((CONVS,)), dma((4,)),
    ]
    return pl.pallas_call(
        functools.partial(train_kernel, cfg),
        out_shape=(
            jax.ShapeDtypeStruct((2, ITEMS, FRAMES // 2, D), BF),
            jax.ShapeDtypeStruct((2, TABLE_ROWS, HALF), BF),
            jax.ShapeDtypeStruct((2, ITEMS, S), F32),
            jax.ShapeDtypeStruct((1, cfg["bsize"]), F32),
            jax.ShapeDtypeStruct((max(1, cfg["osize"] // 128), min(128, cfg["osize"])), F32),
            jax.ShapeDtypeStruct((shard * 4, 128), F32),
            jax.ShapeDtypeStruct((srows * 8, 128), F32),
        ),
        in_specs=[any_, vmem, any_, smem, any_, any_, any_, vmem, vmem],
        out_specs=(any_, vmem, vmem, vmem, vmem, vmem, vmem),
        scratch_shapes=scratch,
        compiler_params=pltpu.CompilerParams(
            collective_id=0, has_side_effects=True, vmem_limit_bytes=63 * 2**20
        ),
    )(phon, sv, fphone, cnt, cot, wmas, smas, bias_in, offset_in)


def adamw(master, moment, square, gradient):
    new_moment = MOMENT_DECAY * moment + (1.0 - MOMENT_DECAY) * gradient
    new_square = SQUARE_DECAY * square + (1.0 - SQUARE_DECAY) * gradient * gradient
    first_fix = 1.0 - MOMENT_DECAY**STEP
    second_fix = 1.0 - SQUARE_DECAY**STEP
    updated = master - LEARN_RATE * (
        (new_moment / first_fix) / (jnp.sqrt(new_square / second_fix) + ADAM_EPS) + WEIGHT_DECAY * master
    )
    return (updated, new_moment, new_square, updated.astype(BF))


def finish_kernel(cut, *refs):
    ins, outs = refs[:19], refs[19:]
    for n in range(4):
        def update(n=n):
            results = adamw(*(ref[...] for ref in ins[4 * n:4 * n + 4]))
            for ref, value in zip(outs[4 * n:4 * n + 4], results):
                ref[...] = value
        if n < cut:
            update()
        else:
            pl.when(pl.program_id(0) == 0)(update)
    for n in range(16, 19):
        outs[n][...] = ins[n][...].astype(F32)


def finish(groups, casts, steps):
    def rows(a):
        return pl.BlockSpec((a.shape[0] // steps, a.shape[1]), lambda i: (i, 0))

    def whole(a):
        return pl.BlockSpec(a.shape, lambda i: (0,) * a.ndim)

    cut = 2 if groups[1][0].shape[0] % (16 * steps) == 0 else 1
    specs, shapes, args = [], [], []
    for n, group in enumerate(groups):
        for k, a in enumerate(group):
            args.append(a)
            specs.append(rows(a) if n < cut else whole(a))
            shapes.append(jax.ShapeDtypeStruct(a.shape, BF if k == 3 else F32))
    for a in casts:
        args.append(a)
        specs.append(rows(a) if a.ndim == 2 else whole(a))
        shapes.append(jax.ShapeDtypeStruct(a.shape, F32))
    return pl.pallas_call(
        functools.partial(finish_kernel, cut),
        grid=(steps,),
        in_specs=specs,
        out_specs=tuple(specs),
        out_shape=tuple(shapes),
        compiler_params=pltpu.CompilerParams(vmem_limit_bytes=63 * 2**20),
    )(*args)


def on_device(
    phonemes, style_vector, frame_phone, frame_count, cotangent,
    conv_master, conv_moment, conv_square, bias_master, bias_moment, bias_square,
    style_master, style_moment, style_square, offset_master, offset_moment, offset_square,
):
    ndp = lax.axis_size("dp")
    micros, items, slots, _ = phonemes.shape
    shard = conv_master.shape[0] // D
    srows = style_master.shape[0] // (2 * D)
    bsize, osize = bias_master.shape[0], offset_master.shape[0]
    remote_phon = (ITEMS * slots) % 16 == 0
    cfg = dict(
        ndp=ndp, dims=factor(ndp), slots=slots, shard=shard, srows=srows, remote_phon=remote_phon,
        bsize=bsize, osize=osize,
    )
    me = lax.axis_index("dp")
    c = lax.axis_index("seq")
    if remote_phon:
        phon = phonemes.reshape(micros, items * slots, D)
    else:
        mine = lax.dynamic_index_in_dim(phonemes, c, 0, keepdims=False)
        mine = mine.reshape(ndp, ITEMS * slots, D)
        phon = lax.all_to_all(mine, "dp", split_axis=0, concat_axis=0, tiled=True).reshape(TABLE_ROWS, D)
    frames, phone, style_grads, gbias, goff, gconv, gstyle = run_train(
        cfg, phon, style_vector, frame_phone, frame_count, cotangent,
        conv_master.reshape(shard * 4, 128), style_master.reshape(srows * 8, 128), bias_master.reshape(1, bsize),
        offset_master.reshape(max(1, osize // 128), min(128, osize)),
    )
    if not remote_phon:
        phone = lax.all_to_all(
            phone.reshape(micros, ndp, ITEMS * slots, HALF), "dp", split_axis=1, concat_axis=1, tiled=True
        )
    groups = [
        [a.reshape(g.shape) for a in arrays] + [g]
        for arrays, g in (
            ((conv_master, conv_moment, conv_square), gconv),
            ((style_master, style_moment, style_square), gstyle),
            ((bias_master, bias_moment, bias_square), gbias),
            ((offset_master, offset_moment, offset_square), goff),
        )
    ]
    out = finish(
        groups,
        (frames.reshape(micros * ITEMS * FRAMES // 2, D), phone.reshape(micros * TABLE_ROWS, HALF), style_grads), 2,
    )
    flat = [a.reshape(-1) for a in out[:16]]
    return (
        out[16].reshape(frames.shape), out[17].reshape(micros, items, slots, HALF), out[18],
        *flat[0:4], *flat[8:12], *flat[4:8], *flat[12:16],
    )


def solution(mesh):
    return jax.shard_map(
        on_device,
        mesh=mesh,
        in_specs=(
            P(None, None, "dp", None), P(None, "dp", None), P(None, "dp", "seq"), P(None, "dp"),
            P(None, "dp", "seq", None), *[P("dp")] * 12,
        ),
        out_specs=(
            P(None, "dp", "seq", None), P(None, None, "dp", "seq"), P(None, "dp", None), *[P("dp")] * 16,
        ),
        check_vma=False,
    )
```
